32 devices in a mesh: probe: 4 (over y, x), seq: 8 (over z, core).
Axes of the slice: x: 2, y: 2, z: 4, core: 2. Of those that a mesh axis runs over, the one named last changes fastest.
Arguments:
- probe_bits: int32 [4, 8, 16384], P('probe', 'seq'), may hold values from 0 to 1
- noise_var: float32 [8, 16384], P('seq'), may hold values from 0.2 to 12
- kernel_spectrum: float32 [16384, 8], P('seq'), may hold values from 0.05 to 4, as said below
- symbol: float32 [16384, 8], P('seq'), may hold values from 0.3 to 3, as said below
- grad_prev: float32 [16384, 8], P('seq', 'probe'), may hold values from -6 to 6
Outputs:
- residual: float32 [4, 8, 16384], P('probe', 'seq')
- grad_total: float32 [16384, 8], P('seq', 'probe')
The draws below stay inside these ranges and needn't reach their ends.
Inputs may be any that keep to these rules, and one draw needn't show every extreme that they name: kernel_spectrum at frequency k equals kernel_spectrum at frequency (131072 - k) mod 131072. symbol at frequency k equals symbol at frequency (131072 - k) mod 131072.
All inputs are finite; a program needn't handle non-finite values.
Results may differ from the reference program's by a relative error of at most 0.00017.
Values sent between devices are 32-bit elements; how exact they have to be, the bound alone decides.
No kernel may reach another device: no remote copies, remote signals or barrier semaphores. Data moves between devices by JAX's collectives and lax.ppermute only.
A program may use at most 64 MiB of HBM per device.

```python
import math
import jax
import jax.numpy as jnp
from jax import lax

COLS = 16384
ROWS = 8
SAMPLES = 131072
PROBES = 4


def mirror(base):
    column_index = jnp.arange(COLS, dtype=jnp.int32)[:, None]
    row_index = jnp.arange(ROWS, dtype=jnp.int32)[None, :]
    frequency = column_index + COLS * row_index
    mirrored = (SAMPLES - frequency) % SAMPLES
    flipped = base[mirrored % COLS, mirrored // COLS]
    return jnp.sqrt(base * flipped)


def draw_kernel_spectrum(key, part):
    key = jax.random.fold_in(key, 11)
    base = jnp.exp(jax.random.uniform(key, (COLS, ROWS), jnp.float32, math.log(0.05), math.log(4.0)))
    return mirror(base)


def draw_symbol(key, part):
    key = jax.random.fold_in(key, 23)
    base = jnp.exp(jax.random.uniform(key, (COLS, ROWS), jnp.float32, math.log(0.3), math.log(3.0)))
    return mirror(base)


def draw_noise_var(key, part):
    key = jax.random.fold_in(key, 37)
    position = jnp.arange(ROWS, dtype=jnp.float32)[:, None] / max(ROWS - 1, 1)
    rising = 0.5 * jnp.power(12.0, position)
    rough = jnp.exp(jax.random.uniform(key, (ROWS, COLS), jnp.float32, math.log(0.7), math.log(1.4)))
    return rising * rough


def touch_ends(values, key, smallest, high):
    extent = values.shape
    place = [jax.random.randint(jax.random.fold_in(key, axis), (), 0, extent[axis]) for axis in range(len(extent))]
    values = values.at[tuple(place)].set(smallest)
    longest = extent.index(max(extent))
    place[longest] = (place[longest] + 1) % extent[longest]
    return values.at[tuple(place)].set(high)


def level_of(own_key, shape, pieces, smallest, largest):
    loudness = 1.0
    for dim, parts in pieces:
        draws = jax.random.uniform(jax.random.fold_in(jax.random.fold_in(own_key, 6), dim), (parts,), jnp.float32, smallest / len(pieces), largest / len(pieces))
        loudness = loudness * jnp.repeat(jnp.exp(draws), shape[dim] // parts).reshape((-1,) + (1,) * (len(shape) - 1 - dim))
    return loudness


def bell_draw(rng, extent, width, bound, cuts=(), held_as=jnp.bfloat16):
    result = width * jax.random.normal(rng, extent, jnp.float32)
    if cuts:
        result = result * level_of(rng, extent, cuts, -0.22, 0.18)
    return jnp.clip(result, -bound, bound).astype(held_as)


def setup_inputs(seed: int = 0) -> dict:
    key_of = jax.random.split(jax.random.key(seed), 6)
    return {
        "probe_bits": touch_ends(jax.random.randint(key_of[0], (PROBES, ROWS, COLS), 0, 2), jax.random.fold_in(key_of[0], 1), 0, 1).astype(jnp.int32),
        "noise_var": draw_noise_var(jax.random.fold_in(key_of[5], 71), 0),
        "kernel_spectrum": draw_kernel_spectrum(jax.random.fold_in(key_of[5], 71), 0),
        "symbol": draw_symbol(jax.random.fold_in(key_of[5], 71), 0),
        "grad_prev": bell_draw(key_of[4], (COLS, ROWS), 1.0, 6.0, ((0, 8), (1, 4)), jnp.float32),
    }


def to_spectrum(series):
    ordered = series.T.reshape(-1)
    spectrum = jnp.fft.fft(ordered).reshape(ROWS, COLS).T
    return jnp.real(spectrum), jnp.imag(spectrum)


def from_spectrum(real_part, imaginary):
    ordered = lax.complex(real_part, imaginary).T.reshape(-1)
    return jnp.real(jnp.fft.ifft(ordered)).reshape(COLS, ROWS).T


def reference(probe_bits, noise_var, kernel_spectrum, symbol, grad_prev):
    accumulated = jnp.zeros(grad_prev.shape, jnp.float32)
    residuals = []
    for probe_number in range(PROBES):
        sign_field = (2 * probe_bits[probe_number] - 1).astype(jnp.float32)
        base_real, base_imag = to_spectrum(sign_field)
        precond = from_spectrum(base_real / symbol, base_imag / symbol)
        again_real, again_imag = to_spectrum(precond)
        kernel_image = from_spectrum(kernel_spectrum * again_real, kernel_spectrum * again_imag) + noise_var * precond
        numerator = jnp.sum(sign_field * precond)
        curvature = jnp.sum(precond * kernel_image)
        step_size = numerator / curvature
        residual = sign_field - step_size * kernel_image
        cross_term = jnp.sum(residual * kernel_image)
        weight = -2.0 * cross_term
        resid_real, resid_imag = to_spectrum(residual)
        applied = from_spectrum(kernel_spectrum * resid_real, kernel_spectrum * resid_imag) + noise_var * residual
        adjoint = (weight / curvature) * sign_field - (2.0 * weight * step_size / curvature) * kernel_image - (2.0 * step_size) * applied
        adjoint_real, adjoint_imag = to_spectrum(adjoint)
        accumulated = accumulated - (adjoint_real * base_real + adjoint_imag * base_imag) / (SAMPLES * symbol * symbol)
        residuals.append(residual)
    return jnp.stack(residuals), grad_prev + accumulated / PROBES
```

```python
import functools
import math

import jax
import jax.numpy as jnp
import numpy as np
from jax import lax
from jax.experimental import pallas as pl
from jax.experimental.pallas import tpu as pltpu
from jax.sharding import PartitionSpec as P

lanes = 128
lead = 8
near = jnp.bfloat16
exact = jnp.float32


def split_table(table):
    high = table.astype(near)
    low = (table - high.astype(np.float64)).astype(near)
    return high, low


def angle_parts(phase):
    return np.cos(phase), np.sin(phase)


@functools.cache
def tables(rows):
    index = np.arange(lanes, dtype=np.float64)
    row_len = lanes * lanes
    turn = -2.0 * np.pi
    c, s = angle_parts(turn * (np.outer(index, index) % lanes) / lanes)
    forward = np.block([[c, s], [-s, c]])
    high, low = split_table(forward)
    right = np.concatenate([high, high, low], 0)
    left = np.ascontiguousarray(right.T)
    real_high, real_low = high[:lanes], low[:lanes]
    sign_right = np.concatenate([real_high, real_low], 0)
    real_right = np.concatenate([real_high, real_high, real_low], 0)
    back_high, back_low = split_table(np.concatenate([c, s], 0))
    back_right = np.concatenate([back_high, back_high, back_low], 0)
    wc, ws = angle_parts(turn * np.outer(index, index) / row_len)
    small_turn = np.concatenate([wc, ws], 1).astype(np.float32)
    flat = (index[:, None] * lanes + index[None, :])[None]
    row = np.arange(rows, dtype=np.float64)[:, None, None]
    gc, gs = angle_parts(turn * flat * row / (rows * row_len))
    big_turn = np.concatenate([gc, gs], 2).astype(np.float32)
    return {
        "right": right,
        "left": left,
        "sign_right": sign_right,
        "real_right": real_right,
        "back_right": back_right,
        "small_turn": small_turn,
        "big_turn": big_turn,
    }


@functools.cache
def block_left(rows):
    left = tables(rows)["left"]
    depth = lanes // rows
    parts = [
        np.concatenate([left[k * depth : (k + 1) * depth], left[lanes + k * depth : lanes + (k + 1) * depth]], 0)
        for k in range(rows)
    ]
    return np.stack(parts)


def split(x):
    high = x.astype(near)
    return high, (x - high.astype(exact)).astype(near)


def stacked(first, second, axis):
    fh, fl = split(first)
    sh, sl = split(second)
    return jnp.concatenate([fh, sh, fl, sl, fh, sh], axis)


def times(left, right):
    return jnp.dot(left, right, preferred_element_type=exact)


def turned(re, im, cos, sin):
    return re * cos - im * sin, re * sin + im * cos


def turned_back(re, im, cos, sin):
    return re * cos + im * sin, im * cos - re * sin


def add(x, y):
    return x[0] + y[0], x[1] + y[1]


def sub(x, y):
    return x[0] - y[0], x[1] - y[1]


def unit_turn(x, k, n, orient):
    k = (k * orient) % n
    if k == 0:
        return x
    if 4 * k == n:
        return -x[1], x[0]
    if 2 * k == n:
        return -x[0], -x[1]
    if 4 * k == 3 * n:
        return x[1], -x[0]
    cos, sin = math.cos(2 * math.pi * k / n), math.sin(2 * math.pi * k / n)
    return x[0] * cos - x[1] * sin, x[0] * sin + x[1] * cos


def small_dft(xs, orient):
    n = len(xs)
    if n == 1:
        return xs
    even, odd = small_dft(xs[0::2], orient), small_dft(xs[1::2], orient)
    odd = [unit_turn(x, k, n, orient) for k, x in enumerate(odd)]
    return [add(e, o) for e, o in zip(even, odd)] + [sub(e, o) for e, o in zip(even, odd)]


def half_dft(xs, orient):
    n = 2 * len(xs)
    even = small_dft(xs, orient)
    odd = small_dft([unit_turn(x, k, n, orient) for k, x in enumerate(xs)], orient)
    return [(odd if r % 2 else even)[r // 2] for r in range(n)]


def pack_kernel(half, bits, noise, kernel, symbol, signs_out, spectra_out, noise_out):
    signs_out[...] = (2 * bits[...] - 1).astype(exact).T
    noise_out[...] = noise[...].T
    depth = kernel.shape[0]
    for a in range(half):
        spectra_out[a * depth : (a + 1) * depth] = kernel[:, a]
        spectra_out[(half + a) * depth : (half + a + 1) * depth] = symbol[:, a]
    middle = jnp.concatenate([kernel[0, half : half + 1], symbol[0, half : half + 1]], 0)
    spectra_out[2 * half * depth :] = jnp.concatenate([middle] * (lead // 2), 0)


def spectrum_kernel(rows, *refs):
    signs = refs[:rows]
    sign_right, left, small_turn, big_turn, spectrum, work = refs[rows:]
    me = lax.axis_index("seq")
    wc, ws = small_turn[:, :lanes], small_turn[:, lanes:]
    for pair in range(rows // 2):
        columns = []
        for j in (2 * pair, 2 * pair + 1):
            x = signs[j][...].astype(near)
            section = times(jnp.concatenate([x, x], 1), sign_right[...])
            columns.append(stacked(*turned(section[:, :lanes], section[:, lanes:], wc, ws), 0))
        done = times(left[...], jnp.concatenate(columns, 1))
        for k, j in enumerate((2 * pair, 2 * pair + 1)):
            r = me ^ j
            re, im = done[:lanes, k * lanes : (k + 1) * lanes], done[lanes:, k * lanes : (k + 1) * lanes]
            re, im = turned(re, im, big_turn[r, :, :lanes], big_turn[r, :, lanes:])
            work[r, 0] = re
            work[r, 1] = im
    for t in range(0, lanes, lead):
        at = slice(t, t + lead)
        out = small_dft([(work[r, 0, at], work[r, 1, at]) for r in range(rows)], -1)
        for a in range(rows):
            spectrum[a, 0, at] = out[a][0]
            spectrum[a, 1, at] = out[a][1]


def inverse_kernel(rows, *refs):
    blocks = refs[:rows]
    spectrum, left, back_right, small_turn, big_turn, precond, circulant, kernel, symbol, ends, work = refs[rows:]
    half = rows // 2
    depth = lanes // rows
    samples = rows * lanes * lanes
    me = lax.axis_index("seq")
    for j in range(rows):
        place = pl.multiple_of((me ^ j) * depth, depth)
        for a in range(half):
            kernel[a, pl.ds(place, depth)] = blocks[j][a * depth : (a + 1) * depth]
            symbol[a, pl.ds(place, depth)] = blocks[j][(half + a) * depth : (half + a + 1) * depth]
        ends[me ^ j] = blocks[j][2 * half * depth :]
    middle = spectrum[half, 0, 0:1, 0:1] / ends[0, 1:2, 0:1] / samples
    middle_image = middle * ends[0, 0:1, 0:1]
    for t in range(0, lanes, lead):
        at = slice(t, t + lead)
        first, second = [], []
        for a in range(half):
            scale = 2.0 / samples / symbol[a, at]
            if a == 0 and t == 0:
                zero = (lax.broadcasted_iota(jnp.int32, (lead, lanes), 0) == 0) & (
                    lax.broadcasted_iota(jnp.int32, (lead, lanes), 1) == 0
                )
                scale = jnp.where(zero, 0.5 * scale, scale)
            re, im = spectrum[a, 0, at] * scale, spectrum[a, 1, at] * scale
            first.append((re, im))
            second.append((re * kernel[a, at], im * kernel[a, at]))
        for field, entries in enumerate((first, second)):
            out = half_dft(entries, 1)
            for r in range(rows):
                re, im = turned_back(*out[r], big_turn[r, at, :lanes], big_turn[r, at, lanes:])
                work[r, field, 0, at] = re
                work[r, field, 1, at] = im
    wc, ws = small_turn[:, :lanes], small_turn[:, lanes:]
    for r in range(rows):
        columns = [stacked(work[r, field, 1], work[r, field, 0], 0) for field in range(2)]
        done = times(left[...], jnp.concatenate(columns, 1))
        lined = []
        for field in range(2):
            at = slice(field * lanes, (field + 1) * lanes)
            lined.append(stacked(*turned_back(done[lanes:, at], done[:lanes, at], wc, ws), 1))
        done = times(jnp.concatenate(lined, 0), back_right[...])
        sign = 1.0 if r % 2 == 0 else -1.0
        precond[r] = done[:lanes] + sign * middle
        circulant[r] = done[lanes:] + sign * middle_image


def whole_sum(x):
    return jnp.sum(jnp.sum(x, axis=0, keepdims=True), axis=1, keepdims=True)


def adjoint_kernel(rows, probes, *refs):
    signs, noises = refs[:rows], refs[rows : 2 * rows]
    refs = refs[2 * rows :]
    precond, circulant, spectrum, kernel, symbol, block, real_right, small_turn, big_turn, residual_out = refs[:10]
    outs = refs[10 : 10 + probes]
    image, field, work, shares = refs[10 + probes :]
    depth = lanes // rows
    samples = rows * lanes * lanes
    me = lax.axis_index("seq")
    numerator = jnp.zeros((lanes, lanes), exact)
    curvature = jnp.zeros((lanes, lanes), exact)
    for j in range(rows):
        p = precond[me ^ j]
        ki = circulant[me ^ j] + noises[j][...] * p
        image[j] = ki
        numerator += signs[j][...] * p
        curvature += p * ki
    numerator, curvature = whole_sum(numerator), whole_sum(curvature)
    step_size = numerator / curvature
    cross = jnp.zeros((lanes, lanes), exact)
    for j in range(rows):
        residual = signs[j][...] - step_size * image[j]
        cross += residual * image[j]
        field[j] = residual
    weight = -2.0 * whole_sum(cross)
    residual_out[...] = field[0].T
    wc, ws = small_turn[:, :lanes], small_turn[:, lanes:]
    own = pl.multiple_of(me * depth, depth)
    for j in range(rows):
        r = me ^ j
        lined = []
        for x in (precond[r], field[j]):
            high, low = split(noises[j][...] * x)
            lined.append(jnp.concatenate([high, low, high], 1))
        section = times(jnp.concatenate(lined, 0), real_right[...])
        columns = []
        for k in range(2):
            at = slice(k * lanes, (k + 1) * lanes)
            columns.append(stacked(*turned(section[at, :lanes], section[at, lanes:], wc, ws), 0))
        done = times(block[me], jnp.concatenate(columns, 1))
        gc, gs = big_turn[r, pl.ds(own, depth), :lanes], big_turn[r, pl.ds(own, depth), lanes:]
        for k in range(2):
            at = slice(k * lanes, (k + 1) * lanes)
            re, im = turned(done[:depth, at], done[depth:, at], gc, gs)
            work[r, k, 0] = re
            work[r, k, 1] = im
    noisy = small_dft([(work[r, 0, 0], work[r, 0, 1]) for r in range(rows)], -1)
    noisy_residual = small_dft([(work[r, 1, 0], work[r, 1, 1]) for r in range(rows)], -1)
    for a in range(rows):
        k, s = kernel[:, a], symbol[:, a]
        total = 0.0
        for part in range(2):
            base = spectrum[a, part, pl.ds(own, depth)]
            ki = k * (base / s) + noisy[a][part]
            applied = k * (base - step_size * ki) + noisy_residual[a][part]
            adjoint = (
                (weight / curvature) * base
                - (2.0 * weight * step_size / curvature) * ki
                - (2.0 * step_size) * applied
            )
            total += adjoint * base
        shares[a] = -total / (samples * s * s)
    width = rows // probes
    column = lax.axis_index("probe")
    for d in range(probes):
        for k in range(width):
            outs[d][:, k] = shares[(column ^ d) * width + k]


def finish_kernel(probes, *refs):
    parts, before, out = refs[:probes], refs[probes], refs[probes + 1]
    out[...] = before[...] + sum(part[...] for part in parts) / probes


def call(kernel, outs, scratch, *operands):
    whole = pl.BlockSpec(memory_space=pltpu.VMEM)
    shapes = tuple(jax.ShapeDtypeStruct(shape, exact) for shape in outs)
    return pl.pallas_call(
        kernel,
        out_shape=shapes,
        in_specs=[whole] * len(operands),
        out_specs=(whole,) * len(shapes),
        scratch_shapes=[pltpu.VMEM(shape, exact) for shape in scratch],
        compiler_params=pltpu.CompilerParams(vmem_limit_bytes=24 << 20),
    )(*operands)


def swapped(x, axis, d):
    return lax.ppermute(x, axis, [(i, i ^ d) for i in range(lax.axis_size(axis))])


def spread(x):
    near_block = swapped(x, "seq", 1)
    got = [x, near_block]
    for d in range(2, lax.axis_size("seq"), 2):
        there = swapped(x, "seq", d)
        got += [there, swapped(there, "seq", 1)]
    return got


def gathered_shards(probe_bits, noise_var, kernel_spectrum, symbol, grad_prev):
    rows = kernel_spectrum.shape[1]
    probes = lax.axis_size("probe")
    half, depth, width = rows // 2, lanes // rows, rows // probes
    t = tables(rows)
    kernel = kernel_spectrum.T.reshape(rows, depth, lanes).transpose(1, 0, 2)
    symbols = symbol.T.reshape(rows, depth, lanes).transpose(1, 0, 2)
    before = grad_prev.T.reshape(width, depth, lanes).transpose(1, 0, 2)
    square = (lanes, lanes)
    signs, spectra, noise = call(
        functools.partial(pack_kernel, half),
        [square, (2 * half * depth + lead, lanes), square],
        [],
        probe_bits.reshape(square),
        noise_var.reshape(square),
        kernel,
        symbols,
    )
    signs, spectra, noise = spread(signs), spread(spectra), spread(noise)
    whole = (rows, 2, *square)
    (spectrum,) = call(
        functools.partial(spectrum_kernel, rows),
        [whole],
        [whole],
        *signs,
        t["sign_right"],
        t["left"],
        t["small_turn"],
        t["big_turn"],
    )
    field = (rows, *square)
    precond, circulant = call(
        functools.partial(inverse_kernel, rows),
        [field, field],
        [(half, *square), (half, *square), (rows, lead, lanes), (rows, 2, 2, *square)],
        *spectra,
        spectrum,
        t["left"],
        t["back_right"],
        t["small_turn"],
        t["big_turn"],
    )
    share = (depth, width, lanes)
    residual, *parts = call(
        functools.partial(adjoint_kernel, rows, probes),
        [square] + [share] * probes,
        [field, field, (rows, 2, 2, depth, lanes), (rows, depth, lanes)],
        *signs,
        *noise,
        precond,
        circulant,
        spectrum,
        kernel,
        symbols,
        block_left(rows),
        t["real_right"],
        t["small_turn"],
        t["big_turn"],
    )
    parts = [parts[0]] + [swapped(parts[d], "probe", d) for d in range(1, probes)]
    (total,) = call(functools.partial(finish_kernel, probes), [share], [], *parts, before)
    total = total.transpose(1, 0, 2).reshape(width, depth * lanes).T
    return residual.reshape(probe_bits.shape), total


highest = lax.Precision.HIGHEST
minor_width = 128


def dft_table(height, breadth, modulus, orient):
    left_index = jnp.arange(height, dtype=jnp.int32)[:, None]
    right_index = jnp.arange(breadth, dtype=jnp.int32)[None, :]
    phases = (
        orient * 2.0 * math.pi / modulus * (left_index * right_index % modulus).astype(jnp.float32)
    )
    return (jnp.cos(phases), jnp.sin(phases))


def complex_product(pattern, real_part, imaginary, cosine_table, sine_table):
    real_cos = jnp.einsum(pattern, real_part, cosine_table, precision=highest)
    real_sin = jnp.einsum(pattern, real_part, sine_table, precision=highest)
    if imaginary is None:
        return (real_cos, real_sin)
    imag_cos = jnp.einsum(pattern, imaginary, cosine_table, precision=highest)
    imag_sin = jnp.einsum(pattern, imaginary, sine_table, precision=highest)
    return (real_cos - imag_sin, real_sin + imag_cos)


def rotate(real_part, imaginary, cosine_table, sine_table):
    return (
        real_part * cosine_table - imaginary * sine_table,
        real_part * sine_table + imaginary * cosine_table,
    )


def forward_rows(series):
    major_len = series.shape[-2]
    length = major_len * minor_width
    cosine_table, sine_table = dft_table(major_len, major_len, major_len, -1.0)
    section_real, section_imag = complex_product(
        "...mi,mk->...ik", series, None, cosine_table, sine_table
    )
    turn_cos, turn_sin = dft_table(minor_width, major_len, length, -1.0)
    twisted_real, twisted_imag = rotate(section_real, section_imag, turn_cos, turn_sin)
    cosine_table, sine_table = dft_table(minor_width, minor_width, minor_width, -1.0)
    return complex_product("...ik,ij->...jk", twisted_real, twisted_imag, cosine_table, sine_table)


def inverse_rows(real_part, imaginary):
    major_len = real_part.shape[-1]
    length = major_len * minor_width
    cosine_table, sine_table = dft_table(minor_width, minor_width, minor_width, 1.0)
    section_real, section_imag = complex_product(
        "...jk,ji->...ik", real_part, imaginary, cosine_table, sine_table
    )
    turn_cos, turn_sin = dft_table(minor_width, major_len, length, 1.0)
    twisted_real, twisted_imag = rotate(section_real, section_imag, turn_cos, turn_sin)
    cosine_table, sine_table = dft_table(major_len, major_len, major_len, 1.0)
    final_real, unused = complex_product(
        "...ik,km->...mi", twisted_real, twisted_imag, cosine_table, sine_table
    )
    return final_real


def global_twiddle(local_rows, major_len, samples, orient):
    row_index = lax.axis_index("seq") * local_rows + jnp.arange(local_rows, dtype=jnp.int32)
    column_index = (
        jnp.arange(minor_width, dtype=jnp.int32)[:, None] * major_len
        + jnp.arange(major_len, dtype=jnp.int32)[None, :]
    )
    phases = (
        orient
        * 2.0
        * math.pi
        / samples
        * (row_index[:, None, None] * column_index[None, :, :] % samples).astype(jnp.float32)
    )
    return (jnp.cos(phases), jnp.sin(phases))


def forward_spectrum(series):
    local_rows = series.shape[1]
    major_len = series.shape[2]
    devices = lax.axis_size("seq")
    all_rows = local_rows * devices
    samples = all_rows * major_len * minor_width
    real_part, imaginary = forward_rows(series)
    turn_cos, turn_sin = global_twiddle(local_rows, major_len, samples, -1.0)
    turned_real, turned_imag = rotate(real_part, imaginary, turn_cos, turn_sin)
    arrived = lax.all_to_all(
        jnp.stack([turned_real, turned_imag]), "seq", split_axis=3, concat_axis=2, tiled=True
    )
    block = minor_width // devices * major_len
    arrived = arrived.reshape(arrived.shape[0], arrived.shape[1], all_rows, block)
    cosine_table, sine_table = dft_table(all_rows, all_rows, all_rows, -1.0)
    return complex_product("zrb,ra->zba", arrived[0], arrived[1], cosine_table, sine_table)


def inverse_field(spectrum_real, spectrum_imag):
    all_rows = spectrum_real.shape[2]
    block = spectrum_real.shape[1]
    devices = lax.axis_size("seq")
    major_len = block * devices // minor_width
    cosine_table, sine_table = dft_table(all_rows, all_rows, all_rows, 1.0)
    back_real, back_imag = complex_product(
        "zba,ar->zrb", spectrum_real, spectrum_imag, cosine_table, sine_table
    )
    stacked = jnp.stack([back_real, back_imag])
    stacked = stacked.reshape(
        stacked.shape[0], stacked.shape[1], all_rows, minor_width // devices, major_len
    )
    arrived = lax.all_to_all(stacked, "seq", split_axis=2, concat_axis=3, tiled=True)
    local_rows = arrived.shape[2]
    samples = all_rows * major_len * minor_width
    turn_cos, turn_sin = global_twiddle(local_rows, major_len, samples, 1.0)
    turned_real, turned_imag = rotate(arrived[0], arrived[1], turn_cos, turn_sin)
    return inverse_rows(turned_real, turned_imag) / samples


def shards(probe_bits, noise_var, kernel_spectrum, symbol, grad_prev):
    field_shape = (
        probe_bits.shape[0],
        probe_bits.shape[1],
        probe_bits.shape[2] // minor_width,
        minor_width,
    )
    sign_field = (2 * probe_bits - 1).astype(jnp.float32).reshape(field_shape)
    noise_field = noise_var.reshape(field_shape[1:])
    samples = kernel_spectrum.shape[1] * noise_var.shape[1]
    base_real, base_imag = forward_spectrum(sign_field)
    scaled_real = base_real / symbol
    scaled_imag = base_imag / symbol
    precond = inverse_field(scaled_real, scaled_imag)
    again_real, again_imag = forward_spectrum(precond)
    circulant = inverse_field(kernel_spectrum * again_real, kernel_spectrum * again_imag)
    kernel_image = circulant + noise_field * precond
    numerator, curvature = lax.psum(
        (jnp.sum(sign_field * precond), jnp.sum(precond * kernel_image)), "seq"
    )
    step_size = numerator / curvature
    residual = sign_field - step_size * kernel_image
    cross_term = lax.psum(jnp.sum(residual * kernel_image), "seq")
    weight = -2.0 * cross_term
    resid_real, resid_imag = forward_spectrum(residual)
    applied = (
        inverse_field(kernel_spectrum * resid_real, kernel_spectrum * resid_imag)
        + noise_field * residual
    )
    adjoint = (
        weight / curvature * sign_field
        - 2.0 * weight * step_size / curvature * kernel_image
        - 2.0 * step_size * applied
    )
    adjoint_real, adjoint_imag = forward_spectrum(adjoint)
    local_grad = -(adjoint_real[0] * base_real[0] + adjoint_imag[0] * base_imag[0]) / (
        samples * symbol * symbol
    )
    probes = lax.axis_size("probe")
    summed = lax.psum(local_grad, "probe")
    share_width = summed.shape[1] // probes
    own_share = lax.dynamic_slice_in_dim(
        summed, lax.axis_index("probe") * share_width, share_width, 1
    )
    grad_total = grad_prev + own_share / probes
    return (residual.reshape(probe_bits.shape), grad_total)


def fits(mesh, cols, rows):
    seq, probe = mesh.shape["seq"], mesh.shape["probe"]
    powers = all(n & (n - 1) == 0 for n in (rows, seq, probe))
    return powers and rows == seq == lead and rows % probe == 0 and probe > 1 and cols == lanes * lanes


def solution(mesh):
    placed = (
        P("probe", "seq", None),
        P("seq", None),
        P("seq", None),
        P("seq", None),
        P("seq", "probe"),
    )

    def whole(probe_bits, noise_var, kernel_spectrum, symbol, grad_prev):
        small = fits(mesh, *symbol.shape)
        return jax.shard_map(
            gathered_shards if small else shards,
            mesh=mesh,
            in_specs=placed,
            out_specs=(P("probe", "seq", None), P("seq", "probe")),
            check_vma=False,
        )(probe_bits, noise_var, kernel_spectrum, symbol, grad_prev)

    return whole
```

```python
import functools
import math

import jax
import jax.numpy as jnp
import numpy as np
from jax import lax
from jax.experimental import pallas as pl
from jax.experimental.pallas import tpu as pltpu
from jax.sharding import PartitionSpec as P

lanes = 128
lead = 8
near = jnp.bfloat16
exact = jnp.float32


def split_table(table):
    high = table.astype(near)
    low = (table - high.astype(np.float64)).astype(near)
    return high, low


def angle_parts(phase):
    return np.cos(phase), np.sin(phase)


@functools.cache
def tables(rows):
    index = np.arange(lanes, dtype=np.float64)
    turn = -2.0 * np.pi
    c, s = angle_parts(turn * (np.outer(index, index) % lanes) / lanes)
    c_high, c_low = split_table(c)
    s_high, s_low = split_table(s)
    row_len = lanes * lanes
    wc, ws = angle_parts(turn * np.outer(index, index) / row_len)
    flat = index[:, None] * lanes + index[None, :]
    gc, gs = angle_parts(turn * flat / (rows * row_len))
    turns = np.stack([np.concatenate([wc, ws], 1), np.concatenate([gc, gs], 1)])
    return np.stack([c_high, s_high, c_low, s_low]), turns.astype(np.float32)


def split(x):
    high = x.astype(near)
    return high, (x - high.astype(exact)).astype(near)


def stacked(first, second, axis):
    fh, fl = split(first)
    sh, sl = split(second)
    return jnp.concatenate([fh, sh, fl, sl, fh, sh], axis)


def times(left, right):
    return jnp.dot(left, right, preferred_element_type=exact)


def turned(re, im, cos, sin):
    return re * cos - im * sin, re * sin + im * cos


def turned_back(re, im, cos, sin):
    return re * cos + im * sin, im * cos - re * sin


def add(x, y):
    return x[0] + y[0], x[1] + y[1]


def sub(x, y):
    return x[0] - y[0], x[1] - y[1]


def unit_turn(x, k, n, orient):
    k = (k * orient) % n
    if k == 0:
        return x
    if 4 * k == n:
        return -x[1], x[0]
    if 2 * k == n:
        return -x[0], -x[1]
    if 4 * k == 3 * n:
        return x[1], -x[0]
    cos, sin = math.cos(2 * math.pi * k / n), math.sin(2 * math.pi * k / n)
    return x[0] * cos - x[1] * sin, x[0] * sin + x[1] * cos


def small_dft(xs, orient):
    n = len(xs)
    if n == 1:
        return xs
    even, odd = small_dft(xs[0::2], orient), small_dft(xs[1::2], orient)
    odd = [unit_turn(x, k, n, orient) for k, x in enumerate(odd)]
    return [add(e, o) for e, o in zip(even, odd)] + [sub(e, o) for e, o in zip(even, odd)]


def half_dft(xs, orient):
    n = 2 * len(xs)
    even = small_dft(xs, orient)
    odd = small_dft([unit_turn(x, k, n, orient) for k, x in enumerate(xs)], orient)
    return [(odd if r % 2 else even)[r // 2] for r in range(n)]


def pack_kernel(half, *refs):
    sources, out, landed, done = refs[:4], refs[4], refs[5:9], refs[9]
    copies = [pltpu.make_async_copy(sources[i], landed[i], done.at[i]) for i in range(4)]
    for copy in copies:
        copy.start()
    bits, noise, kernel, symbol = landed
    copies[0].wait()
    out[:lanes] = (2 * bits[...] - 1).astype(exact).T
    copies[1].wait()
    out[lanes : 2 * lanes] = noise[...].T
    copies[2].wait()
    copies[3].wait()
    depth = kernel.shape[0]
    for a in range(half):
        at = 2 * lanes + a * depth
        out[at : at + depth] = kernel[:, a]
        at += half * depth
        out[at : at + depth] = symbol[:, a]
    middle = jnp.concatenate([kernel[0, half : half + 1], symbol[0, half : half + 1]], 0)
    out[2 * (lanes + half * depth) :] = jnp.concatenate([middle] * (lead // 2), 0)


def spectrum_kernel(rows, *refs):
    blocks = refs[:rows]
    dft, turns, spectrum, left, big_turn, work = refs[rows:]
    me = lax.axis_index("seq")
    c_high, s_high, c_low, s_low = (dft[k] for k in range(4))
    left[:lanes] = jnp.concatenate([c_high, -s_high, c_high, -s_high, c_low, -s_low], 1)
    left[lanes:] = jnp.concatenate([s_high, c_high, s_high, c_high, s_low, c_low], 1)
    sign_right = jnp.concatenate(
        [jnp.concatenate([c_high, s_high], 1), jnp.concatenate([c_low, s_low], 1)], 0
    )
    for t in range(0, lanes, lead):
        at = slice(t, t + lead)
        one = turns[1, at, :lanes], turns[1, at, lanes:]
        powers = [(jnp.ones((lead, lanes), exact), jnp.zeros((lead, lanes), exact)), one]
        for r in range(2, rows):
            powers.append(turned(*powers[r // 2], *powers[r - r // 2]))
        for r in range(rows):
            big_turn[r, at, :lanes] = powers[r][0]
            big_turn[r, at, lanes:] = powers[r][1]
    wc, ws = turns[0, :, :lanes], turns[0, :, lanes:]
    for pair in range(rows // 2):
        columns = []
        for j in (2 * pair, 2 * pair + 1):
            x = blocks[j][:lanes].astype(near)
            section = times(jnp.concatenate([x, x], 1), sign_right)
            columns.append(stacked(*turned(section[:, :lanes], section[:, lanes:], wc, ws), 0))
        done = times(left[...], jnp.concatenate(columns, 1))
        for k, j in enumerate((2 * pair, 2 * pair + 1)):
            r = me ^ j
            re, im = done[:lanes, k * lanes : (k + 1) * lanes], done[lanes:, k * lanes : (k + 1) * lanes]
            re, im = turned(re, im, big_turn[r, :, :lanes], big_turn[r, :, lanes:])
            work[r, 0] = re
            work[r, 1] = im
    for t in range(0, lanes, lead):
        at = slice(t, t + lead)
        out = small_dft([(work[r, 0, at], work[r, 1, at]) for r in range(rows)], -1)
        for a in range(rows):
            spectrum[a, 0, at] = out[a][0]
            spectrum[a, 1, at] = out[a][1]


def inverse_kernel(rows, *refs):
    blocks = refs[:rows]
    spectrum, left, dft, turns, big_turn, precond, circulant, kernel, symbol, ends, work = refs[rows:]
    half = rows // 2
    depth = lanes // rows
    samples = rows * lanes * lanes
    me = lax.axis_index("seq")
    for j in range(rows):
        place = pl.multiple_of((me ^ j) * depth, depth)
        for a in range(half):
            at = 2 * lanes + a * depth
            kernel[a, pl.ds(place, depth)] = blocks[j][at : at + depth]
            at += half * depth
            symbol[a, pl.ds(place, depth)] = blocks[j][at : at + depth]
        ends[me ^ j] = blocks[j][2 * lanes + 2 * half * depth :]
    middle = spectrum[half, 0, 0:1, 0:1] / ends[0, 1:2, 0:1] / samples
    middle_image = middle * ends[0, 0:1, 0:1]
    for t in range(0, lanes, lead):
        at = slice(t, t + lead)
        first, second = [], []
        for a in range(half):
            scale = 2.0 / samples / symbol[a, at]
            if a == 0 and t == 0:
                zero = (lax.broadcasted_iota(jnp.int32, (lead, lanes), 0) == 0) & (
                    lax.broadcasted_iota(jnp.int32, (lead, lanes), 1) == 0
                )
                scale = jnp.where(zero, 0.5 * scale, scale)
            re, im = spectrum[a, 0, at] * scale, spectrum[a, 1, at] * scale
            first.append((re, im))
            second.append((re * kernel[a, at], im * kernel[a, at]))
        for field, entries in enumerate((first, second)):
            out = half_dft(entries, 1)
            for r in range(rows):
                re, im = turned_back(*out[r], big_turn[r, at, :lanes], big_turn[r, at, lanes:])
                work[r, field, 0, at] = re
                work[r, field, 1, at] = im
    wc, ws = turns[0, :, :lanes], turns[0, :, lanes:]
    back_right = jnp.concatenate([dft[k] for k in (0, 1, 0, 1, 2, 3)], 0)
    for r in range(rows):
        columns = [stacked(work[r, field, 1], work[r, field, 0], 0) for field in range(2)]
        done = times(left[...], jnp.concatenate(columns, 1))
        lined = []
        for field in range(2):
            at = slice(field * lanes, (field + 1) * lanes)
            lined.append(stacked(*turned_back(done[lanes:, at], done[:lanes, at], wc, ws), 1))
        done = times(jnp.concatenate(lined, 0), back_right)
        sign = 1.0 if r % 2 == 0 else -1.0
        precond[r] = done[:lanes] + sign * middle
        circulant[r] = done[lanes:] + sign * middle_image


def whole_sum(x):
    return jnp.sum(jnp.sum(x, axis=0, keepdims=True), axis=1, keepdims=True)


def adjoint_kernel(rows, probes, *refs):
    signs = [refs[j].at[:lanes] for j in range(rows)]
    noises = [refs[j].at[lanes : 2 * lanes] for j in range(rows)]
    refs = refs[rows:]
    precond, circulant, spectrum, kernel, symbol, left, dft, turns, big_turn, residual_out = refs[:10]
    outs = refs[10 : 10 + probes]
    image, field, work, shares = refs[10 + probes :]
    depth = lanes // rows
    samples = rows * lanes * lanes
    me = lax.axis_index("seq")
    numerator = jnp.zeros((lanes, lanes), exact)
    curvature = jnp.zeros((lanes, lanes), exact)
    for j in range(rows):
        p = precond[me ^ j]
        ki = circulant[me ^ j] + noises[j][...] * p
        image[j] = ki
        numerator += signs[j][...] * p
        curvature += p * ki
    numerator, curvature = whole_sum(numerator), whole_sum(curvature)
    step_size = numerator / curvature
    cross = jnp.zeros((lanes, lanes), exact)
    for j in range(rows):
        residual = signs[j][...] - step_size * image[j]
        cross += residual * image[j]
        field[j] = residual
    weight = -2.0 * whole_sum(cross)
    residual_out[...] = field[0].T
    wc, ws = turns[0, :, :lanes], turns[0, :, lanes:]
    own = pl.multiple_of(me * depth, depth)
    real_right = jnp.concatenate([jnp.concatenate([dft[k], dft[k + 1]], 1) for k in (0, 0, 2)], 0)
    block = jnp.concatenate([left[pl.ds(own, depth)], left[pl.ds(pl.multiple_of(lanes + own, depth), depth)]], 0)
    for j in range(rows):
        r = me ^ j
        lined = []
        for x in (precond[r], field[j]):
            high, low = split(noises[j][...] * x)
            lined.append(jnp.concatenate([high, low, high], 1))
        section = times(jnp.concatenate(lined, 0), real_right)
        columns = []
        for k in range(2):
            at = slice(k * lanes, (k + 1) * lanes)
            columns.append(stacked(*turned(section[at, :lanes], section[at, lanes:], wc, ws), 0))
        done = times(block, jnp.concatenate(columns, 1))
        gc, gs = big_turn[r, pl.ds(own, depth), :lanes], big_turn[r, pl.ds(own, depth), lanes:]
        for k in range(2):
            at = slice(k * lanes, (k + 1) * lanes)
            re, im = turned(done[:depth, at], done[depth:, at], gc, gs)
            work[r, k, 0] = re
            work[r, k, 1] = im
    noisy = small_dft([(work[r, 0, 0], work[r, 0, 1]) for r in range(rows)], -1)
    noisy_residual = small_dft([(work[r, 1, 0], work[r, 1, 1]) for r in range(rows)], -1)
    for a in range(rows):
        k, s = kernel[:, a], symbol[:, a]
        total = 0.0
        for part in range(2):
            base = spectrum[a, part, pl.ds(own, depth)]
            ki = k * (base / s) + noisy[a][part]
            applied = k * (base - step_size * ki) + noisy_residual[a][part]
            adjoint = (
                (weight / curvature) * base
                - (2.0 * weight * step_size / curvature) * ki
                - (2.0 * step_size) * applied
            )
            total += adjoint * base
        shares[a] = -total / (samples * s * s)
    width = rows // probes
    column = lax.axis_index("probe")
    for d in range(probes):
        for k in range(width):
            outs[d][:, k] = shares[(column ^ d) * width + k]


def call(kernel, outs, scratch, *operands):
    whole = pl.BlockSpec(memory_space=pltpu.VMEM)
    typed = [out if isinstance(out[0], tuple) else (out, exact) for out in outs]
    shapes = tuple(jax.ShapeDtypeStruct(shape, dtype) for shape, dtype in typed)
    return pl.pallas_call(
        kernel,
        out_shape=shapes,
        in_specs=[whole] * len(operands),
        out_specs=(whole,) * len(shapes),
        scratch_shapes=[pltpu.VMEM(shape, exact) for shape in scratch],
        compiler_params=pltpu.CompilerParams(vmem_limit_bytes=24 << 20),
    )(*operands)


def swapped(x, axis, d):
    return lax.ppermute(x, axis, [(i, i ^ d) for i in range(lax.axis_size(axis))])


def after(x, *earlier):
    return lax.optimization_barrier((x, *earlier))[0]


def spread(x):
    got = {1: swapped(x, "seq", 1)}
    for d in reversed(range(2, lax.axis_size("seq"), 2)):
        got[d] = swapped(x, "seq", d)
        got[d + 1] = swapped(got[d], "seq", 1)
    return [x] + [got[d] for d in sorted(got)]


def gathered_shards(probe_bits, noise_var, kernel_spectrum, symbol, grad_prev):
    rows = kernel_spectrum.shape[1]
    probes = lax.axis_size("probe")
    half, depth, width = rows // 2, lanes // rows, rows // probes
    kernel = kernel_spectrum.T.reshape(rows, depth, lanes).transpose(1, 0, 2)
    symbols = symbol.T.reshape(rows, depth, lanes).transpose(1, 0, 2)
    before = grad_prev.T.reshape(width, depth, lanes).transpose(1, 0, 2)
    square = (lanes, lanes)
    dft, turns = tables(rows)
    packed = (2 * (lanes + half * depth) + lead, lanes)
    block = pl.pallas_call(
        functools.partial(pack_kernel, half),
        out_shape=jax.ShapeDtypeStruct(packed, exact),
        in_specs=[pl.BlockSpec(memory_space=pl.ANY)] * 4,
        out_specs=pl.BlockSpec(memory_space=pltpu.VMEM),
        scratch_shapes=[
            pltpu.VMEM(square, jnp.int32),
            pltpu.VMEM(square, exact),
            pltpu.VMEM(kernel.shape, exact),
            pltpu.VMEM(kernel.shape, exact),
            pltpu.SemaphoreType.DMA((4,)),
        ],
    )(probe_bits.reshape(square), noise_var.reshape(square), kernel, symbols)
    blocks = spread(block)
    whole = (rows, 2, *square)
    spectrum, left, big_turn = call(
        functools.partial(spectrum_kernel, rows),
        [whole, ((2 * lanes, 6 * lanes), near), (rows, lanes, 2 * lanes)],
        [whole],
        *blocks,
        dft,
        turns,
    )
    field = (rows, *square)
    precond, circulant = call(
        functools.partial(inverse_kernel, rows),
        [field, field],
        [(half, *square), (half, *square), (rows, lead, lanes), (rows, 2, 2, *square)],
        *blocks,
        spectrum,
        left,
        dft,
        turns,
        big_turn,
    )
    share = (depth, width, lanes)
    residual, *parts = call(
        functools.partial(adjoint_kernel, rows, probes),
        [square] + [share] * probes,
        [field, field, (rows, 2, 2, depth, lanes), (rows, depth, lanes)],
        *blocks,
        precond,
        circulant,
        spectrum,
        kernel,
        symbols,
        left,
        dft,
        turns,
        big_turn,
    )
    arrived = [swapped(parts[d], "probe", d) for d in reversed(range(1, probes))]
    total = before + sum(arrived, parts[0]) / probes
    total = total.transpose(1, 0, 2).reshape(width, depth * lanes).T
    return residual.reshape(probe_bits.shape), total


highest = lax.Precision.HIGHEST
minor_width = 128


def dft_table(height, breadth, modulus, orient):
    left_index = jnp.arange(height, dtype=jnp.int32)[:, None]
    right_index = jnp.arange(breadth, dtype=jnp.int32)[None, :]
    phases = (
        orient * 2.0 * math.pi / modulus * (left_index * right_index % modulus).astype(jnp.float32)
    )
    return (jnp.cos(phases), jnp.sin(phases))


def complex_product(pattern, real_part, imaginary, cosine_table, sine_table):
    real_cos = jnp.einsum(pattern, real_part, cosine_table, precision=highest)
    real_sin = jnp.einsum(pattern, real_part, sine_table, precision=highest)
    if imaginary is None:
        return (real_cos, real_sin)
    imag_cos = jnp.einsum(pattern, imaginary, cosine_table, precision=highest)
    imag_sin = jnp.einsum(pattern, imaginary, sine_table, precision=highest)
    return (real_cos - imag_sin, real_sin + imag_cos)


def rotate(real_part, imaginary, cosine_table, sine_table):
    return (
        real_part * cosine_table - imaginary * sine_table,
        real_part * sine_table + imaginary * cosine_table,
    )


def forward_rows(series):
    major_len = series.shape[-2]
    length = major_len * minor_width
    cosine_table, sine_table = dft_table(major_len, major_len, major_len, -1.0)
    section_real, section_imag = complex_product(
        "...mi,mk->...ik", series, None, cosine_table, sine_table
    )
    turn_cos, turn_sin = dft_table(minor_width, major_len, length, -1.0)
    twisted_real, twisted_imag = rotate(section_real, section_imag, turn_cos, turn_sin)
    cosine_table, sine_table = dft_table(minor_width, minor_width, minor_width, -1.0)
    return complex_product("...ik,ij->...jk", twisted_real, twisted_imag, cosine_table, sine_table)


def inverse_rows(real_part, imaginary):
    major_len = real_part.shape[-1]
    length = major_len * minor_width
    cosine_table, sine_table = dft_table(minor_width, minor_width, minor_width, 1.0)
    section_real, section_imag = complex_product(
        "...jk,ji->...ik", real_part, imaginary, cosine_table, sine_table
    )
    turn_cos, turn_sin = dft_table(minor_width, major_len, length, 1.0)
    twisted_real, twisted_imag = rotate(section_real, section_imag, turn_cos, turn_sin)
    cosine_table, sine_table = dft_table(major_len, major_len, major_len, 1.0)
    final_real, unused = complex_product(
        "...ik,km->...mi", twisted_real, twisted_imag, cosine_table, sine_table
    )
    return final_real


def global_twiddle(local_rows, major_len, samples, orient):
    row_index = lax.axis_index("seq") * local_rows + jnp.arange(local_rows, dtype=jnp.int32)
    column_index = (
        jnp.arange(minor_width, dtype=jnp.int32)[:, None] * major_len
        + jnp.arange(major_len, dtype=jnp.int32)[None, :]
    )
    phases = (
        orient
        * 2.0
        * math.pi
        / samples
        * (row_index[:, None, None] * column_index[None, :, :] % samples).astype(jnp.float32)
    )
    return (jnp.cos(phases), jnp.sin(phases))


def forward_spectrum(series):
    local_rows = series.shape[1]
    major_len = series.shape[2]
    devices = lax.axis_size("seq")
    all_rows = local_rows * devices
    samples = all_rows * major_len * minor_width
    real_part, imaginary = forward_rows(series)
    turn_cos, turn_sin = global_twiddle(local_rows, major_len, samples, -1.0)
    turned_real, turned_imag = rotate(real_part, imaginary, turn_cos, turn_sin)
    arrived = lax.all_to_all(
        jnp.stack([turned_real, turned_imag]), "seq", split_axis=3, concat_axis=2, tiled=True
    )
    block = minor_width // devices * major_len
    arrived = arrived.reshape(arrived.shape[0], arrived.shape[1], all_rows, block)
    cosine_table, sine_table = dft_table(all_rows, all_rows, all_rows, -1.0)
    return complex_product("zrb,ra->zba", arrived[0], arrived[1], cosine_table, sine_table)


def inverse_field(spectrum_real, spectrum_imag):
    all_rows = spectrum_real.shape[2]
    block = spectrum_real.shape[1]
    devices = lax.axis_size("seq")
    major_len = block * devices // minor_width
    cosine_table, sine_table = dft_table(all_rows, all_rows, all_rows, 1.0)
    back_real, back_imag = complex_product(
        "zba,ar->zrb", spectrum_real, spectrum_imag, cosine_table, sine_table
    )
    stacked = jnp.stack([back_real, back_imag])
    stacked = stacked.reshape(
        stacked.shape[0], stacked.shape[1], all_rows, minor_width // devices, major_len
    )
    arrived = lax.all_to_all(stacked, "seq", split_axis=2, concat_axis=3, tiled=True)
    local_rows = arrived.shape[2]
    samples = all_rows * major_len * minor_width
    turn_cos, turn_sin = global_twiddle(local_rows, major_len, samples, 1.0)
    turned_real, turned_imag = rotate(arrived[0], arrived[1], turn_cos, turn_sin)
    return inverse_rows(turned_real, turned_imag) / samples


def shards(probe_bits, noise_var, kernel_spectrum, symbol, grad_prev):
    field_shape = (
        probe_bits.shape[0],
        probe_bits.shape[1],
        probe_bits.shape[2] // minor_width,
        minor_width,
    )
    sign_field = (2 * probe_bits - 1).astype(jnp.float32).reshape(field_shape)
    noise_field = noise_var.reshape(field_shape[1:])
    samples = kernel_spectrum.shape[1] * noise_var.shape[1]
    base_real, base_imag = forward_spectrum(sign_field)
    scaled_real = base_real / symbol
    scaled_imag = base_imag / symbol
    precond = inverse_field(scaled_real, scaled_imag)
    again_real, again_imag = forward_spectrum(precond)
    circulant = inverse_field(kernel_spectrum * again_real, kernel_spectrum * again_imag)
    kernel_image = circulant + noise_field * precond
    numerator, curvature = lax.psum(
        (jnp.sum(sign_field * precond), jnp.sum(precond * kernel_image)), "seq"
    )
    step_size = numerator / curvature
    residual = sign_field - step_size * kernel_image
    cross_term = lax.psum(jnp.sum(residual * kernel_image), "seq")
    weight = -2.0 * cross_term
    resid_real, resid_imag = forward_spectrum(residual)
    applied = (
        inverse_field(kernel_spectrum * resid_real, kernel_spectrum * resid_imag)
        + noise_field * residual
    )
    adjoint = (
        weight / curvature * sign_field
        - 2.0 * weight * step_size / curvature * kernel_image
        - 2.0 * step_size * applied
    )
    adjoint_real, adjoint_imag = forward_spectrum(adjoint)
    local_grad = -(adjoint_real[0] * base_real[0] + adjoint_imag[0] * base_imag[0]) / (
        samples * symbol * symbol
    )
    probes = lax.axis_size("probe")
    summed = lax.psum(local_grad, "probe")
    share_width = summed.shape[1] // probes
    own_share = lax.dynamic_slice_in_dim(
        summed, lax.axis_index("probe") * share_width, share_width, 1
    )
    grad_total = grad_prev + own_share / probes
    return (residual.reshape(probe_bits.shape), grad_total)


def fits(mesh, cols, rows):
    seq, probe = mesh.shape["seq"], mesh.shape["probe"]
    powers = all(n & (n - 1) == 0 for n in (rows, seq, probe))
    return powers and rows == seq == lead and rows % probe == 0 and probe > 1 and cols == lanes * lanes


def solution(mesh):
    placed = (
        P("probe", "seq", None),
        P("seq", None),
        P("seq", None),
        P("seq", None),
        P("seq", "probe"),
    )

    def whole(probe_bits, noise_var, kernel_spectrum, symbol, grad_prev):
        small = fits(mesh, *symbol.shape)
        return jax.shard_map(
            gathered_shards if small else shards,
            mesh=mesh,
            in_specs=placed,
            out_specs=(P("probe", "seq", None), P("seq", "probe")),
            check_vma=False,
        )(probe_bits, noise_var, kernel_spectrum, symbol, grad_prev)

    return whole
```

```python
import functools
import math

import jax
import jax.numpy as jnp
import numpy as np
from jax import lax
from jax.experimental import pallas as pl
from jax.experimental.pallas import tpu as pltpu
from jax.sharding import PartitionSpec as P

lanes = 128
lead = 8
near = jnp.bfloat16
exact = jnp.float32


def split_table(table):
    high = table.astype(near)
    low = (table - high.astype(np.float64)).astype(near)
    return high, low


def angle_parts(phase):
    return np.cos(phase), np.sin(phase)


@functools.cache
def tables(rows):
    index = np.arange(lanes, dtype=np.float64)
    turn = -2.0 * np.pi
    c, s = angle_parts(turn * (np.outer(index, index) % lanes) / lanes)
    c_high, c_low = split_table(c)
    s_high, s_low = split_table(s)
    row_len = lanes * lanes
    wc, ws = angle_parts(turn * np.outer(index, index) / row_len)
    flat = index[:, None] * lanes + index[None, :]
    gc, gs = angle_parts(turn * flat / (rows * row_len))
    turns = np.stack([np.concatenate([wc, ws], 1), np.concatenate([gc, gs], 1)])
    return np.stack([c_high, s_high, c_low, s_low]), turns.astype(np.float32)


def split(x):
    high = x.astype(near)
    return high, (x - high.astype(exact)).astype(near)


def stacked(first, second, axis):
    fh, fl = split(first)
    sh, sl = split(second)
    return jnp.concatenate([fh, sh, fl, sl, fh, sh], axis)


def times(left, right):
    return jnp.dot(left, right, preferred_element_type=exact)


def turned(re, im, cos, sin):
    return re * cos - im * sin, re * sin + im * cos


def turned_back(re, im, cos, sin):
    return re * cos + im * sin, im * cos - re * sin


def add(x, y):
    return x[0] + y[0], x[1] + y[1]


def sub(x, y):
    return x[0] - y[0], x[1] - y[1]


def unit_turn(x, k, n, orient):
    k = (k * orient) % n
    if k == 0:
        return x
    if 4 * k == n:
        return -x[1], x[0]
    if 2 * k == n:
        return -x[0], -x[1]
    if 4 * k == 3 * n:
        return x[1], -x[0]
    cos, sin = math.cos(2 * math.pi * k / n), math.sin(2 * math.pi * k / n)
    return x[0] * cos - x[1] * sin, x[0] * sin + x[1] * cos


def small_dft(xs, orient):
    n = len(xs)
    if n == 1:
        return xs
    even, odd = small_dft(xs[0::2], orient), small_dft(xs[1::2], orient)
    odd = [unit_turn(x, k, n, orient) for k, x in enumerate(odd)]
    return [add(e, o) for e, o in zip(even, odd)] + [sub(e, o) for e, o in zip(even, odd)]


def half_dft(xs, orient):
    n = 2 * len(xs)
    even = small_dft(xs, orient)
    odd = small_dft([unit_turn(x, k, n, orient) for k, x in enumerate(xs)], orient)
    return [(odd if r % 2 else even)[r // 2] for r in range(n)]


def pack_kernel(half, *refs):
    sources, (out, first_out, noise_out), held, landed, done = refs[:6], refs[6:9], refs[9:11], refs[11:15], refs[15]
    targets = (*landed, *held)
    copies = [pltpu.make_async_copy(sources[i], targets[i], done.at[i]) for i in range(6)]
    for copy in copies:
        copy.start()
    bits, noise, kernel, symbol = landed
    first = first_out.shape[0]
    copies[0].wait()
    signs = (2 * bits[...] - 1).astype(exact).T
    out[:lanes] = signs
    first_out[:lanes] = signs
    copies[1].wait()
    noise = noise[...].T
    out[first:] = noise
    noise_out[...] = noise
    copies[2].wait()
    copies[3].wait()
    depth = kernel.shape[0]
    middle = jnp.concatenate([kernel[0, half : half + 1], symbol[0, half : half + 1]], 0)
    for target in (out, first_out):
        for a in range(half):
            at = lanes + a * depth
            target[at : at + depth] = kernel[:, a]
            at += half * depth
            target[at : at + depth] = symbol[:, a]
        target[first - lead : first] = jnp.concatenate([middle] * (lead // 2), 0)
    copies[4].wait()
    copies[5].wait()


def row_spectrum(signs, r, sign_right, left, w):
    columns = []
    for x in signs:
        x = x[:lanes].astype(near)
        section = times(jnp.concatenate([x, x], 1), sign_right)
        columns.append(stacked(*turned(section[:, :lanes], section[:, lanes:], *w), 0))
    done = times(left, jnp.concatenate(columns, 1))
    out = []
    for k, turn in enumerate(r):
        at = slice(k * lanes, (k + 1) * lanes)
        out.append(turned(done[:lanes, at], done[lanes:, at], turn[:, :lanes], turn[:, lanes:]))
    return out


def sign_table(dft):
    c_high, s_high, c_low, s_low = (dft[k] for k in range(4))
    return jnp.concatenate([jnp.concatenate([c_high, s_high], 1), jnp.concatenate([c_low, s_low], 1)], 0)


def early_kernel(rows, *refs):
    early = rows - 2
    blocks = refs[:early]
    dft, turns, found, left, big_turn = refs[early:]
    me = lax.axis_index("seq")
    c_high, s_high, c_low, s_low = (dft[k] for k in range(4))
    left[:lanes] = jnp.concatenate([c_high, -s_high, c_high, -s_high, c_low, -s_low], 1)
    left[lanes:] = jnp.concatenate([s_high, c_high, s_high, c_high, s_low, c_low], 1)
    for t in range(0, lanes, lead):
        at = slice(t, t + lead)
        one = turns[1, at, :lanes], turns[1, at, lanes:]
        powers = [(jnp.ones((lead, lanes), exact), jnp.zeros((lead, lanes), exact)), one]
        for r in range(2, rows):
            powers.append(turned(*powers[r // 2], *powers[r - r // 2]))
        for r in range(rows):
            big_turn[r, at, :lanes] = powers[r][0]
            big_turn[r, at, lanes:] = powers[r][1]
    w = turns[0, :, :lanes], turns[0, :, lanes:]
    for j in range(0, early, 2):
        turn = [big_turn[me ^ j], big_turn[me ^ (j + 1)]]
        for k, x in enumerate(row_spectrum(blocks[j : j + 2], turn, sign_table(dft), left[...], w)):
            found[j + k, 0], found[j + k, 1] = x


def inverse_kernel(rows, *refs):
    blocks = refs[:rows]
    found, left, dft, turns, big_turn, spectrum, precond, circulant, kernel, symbol, ends, work = refs[rows:]
    half, early = rows // 2, rows - 2
    depth = lanes // rows
    samples = rows * lanes * lanes
    me = lax.axis_index("seq")
    w = turns[0, :, :lanes], turns[0, :, lanes:]
    for j in range(early):
        work[me ^ j, 0, 0], work[me ^ j, 0, 1] = found[j, 0], found[j, 1]
    for j in range(early, rows, 2):
        turn = [big_turn[me ^ j], big_turn[me ^ (j + 1)]]
        for k, x in enumerate(row_spectrum(blocks[j : j + 2], turn, sign_table(dft), left[...], w)):
            work[me ^ (j + k), 0, 0], work[me ^ (j + k), 0, 1] = x
    for t in range(0, lanes, lead):
        at = slice(t, t + lead)
        out = small_dft([(work[r, 0, 0, at], work[r, 0, 1, at]) for r in range(rows)], -1)
        for a in range(rows):
            spectrum[a, 0, at], spectrum[a, 1, at] = out[a]
    for j in range(rows):
        place = pl.multiple_of((me ^ j) * depth, depth)
        for a in range(half):
            at = lanes + a * depth
            kernel[a, pl.ds(place, depth)] = blocks[j][at : at + depth]
            at += half * depth
            symbol[a, pl.ds(place, depth)] = blocks[j][at : at + depth]
        ends[me ^ j] = blocks[j][lanes + 2 * half * depth : lanes + 2 * half * depth + lead]
    middle = spectrum[half, 0, 0:1, 0:1] / ends[0, 1:2, 0:1] / samples
    middle_image = middle * ends[0, 0:1, 0:1]
    for t in range(0, lanes, lead):
        at = slice(t, t + lead)
        first, second = [], []
        for a in range(half):
            scale = 2.0 / samples / symbol[a, at]
            if a == 0 and t == 0:
                zero = (lax.broadcasted_iota(jnp.int32, (lead, lanes), 0) == 0) & (
                    lax.broadcasted_iota(jnp.int32, (lead, lanes), 1) == 0
                )
                scale = jnp.where(zero, 0.5 * scale, scale)
            re, im = spectrum[a, 0, at] * scale, spectrum[a, 1, at] * scale
            first.append((re, im))
            second.append((re * kernel[a, at], im * kernel[a, at]))
        for field, entries in enumerate((first, second)):
            out = half_dft(entries, 1)
            for r in range(rows):
                re, im = turned_back(*out[r], big_turn[r, at, :lanes], big_turn[r, at, lanes:])
                work[r, field, 0, at] = re
                work[r, field, 1, at] = im
    back_right = jnp.concatenate([dft[k] for k in (0, 1, 0, 1, 2, 3)], 0)
    for r in range(rows):
        columns = [stacked(work[r, field, 1], work[r, field, 0], 0) for field in range(2)]
        done = times(left[...], jnp.concatenate(columns, 1))
        lined = []
        for field in range(2):
            at = slice(field * lanes, (field + 1) * lanes)
            lined.append(stacked(*turned_back(done[lanes:, at], done[:lanes, at], *w), 1))
        done = times(jnp.concatenate(lined, 0), back_right)
        sign = 1.0 if r % 2 == 0 else -1.0
        precond[r] = done[:lanes] + sign * middle
        circulant[r] = done[lanes:] + sign * middle_image


def whole_sum(x):
    return jnp.sum(jnp.sum(x, axis=0, keepdims=True), axis=1, keepdims=True)


def adjoint_kernel(rows, probes, *refs):
    signs = [refs[j].at[:lanes] for j in range(rows)]
    near_noises = [refs[j].at[refs[j].shape[0] - lanes :] for j in range(rows // 2)]
    noises = (*near_noises, *refs[rows : rows + rows // 2])
    refs = refs[rows + rows // 2 :]
    precond, circulant, spectrum, kernel, symbol, left, dft, turns, big_turn, residual_out = refs[:10]
    outs = refs[10 : 10 + probes]
    image, field, work, shares = refs[10 + probes :]
    depth = lanes // rows
    samples = rows * lanes * lanes
    me = lax.axis_index("seq")
    numerator = jnp.zeros((lanes, lanes), exact)
    curvature = jnp.zeros((lanes, lanes), exact)
    for j in range(rows):
        p = precond[me ^ j]
        ki = circulant[me ^ j] + noises[j][...] * p
        image[j] = ki
        numerator += signs[j][...] * p
        curvature += p * ki
    numerator, curvature = whole_sum(numerator), whole_sum(curvature)
    step_size = numerator / curvature
    cross = jnp.zeros((lanes, lanes), exact)
    for j in range(rows):
        residual = signs[j][...] - step_size * image[j]
        cross += residual * image[j]
        field[j] = residual
    weight = -2.0 * whole_sum(cross)
    residual_out[...] = field[0].T
    wc, ws = turns[0, :, :lanes], turns[0, :, lanes:]
    own = pl.multiple_of(me * depth, depth)
    real_right = jnp.concatenate([jnp.concatenate([dft[k], dft[k + 1]], 1) for k in (0, 0, 2)], 0)
    block = jnp.concatenate([left[pl.ds(own, depth)], left[pl.ds(pl.multiple_of(lanes + own, depth), depth)]], 0)
    for j in range(rows):
        r = me ^ j
        lined = []
        for x in (precond[r], field[j]):
            high, low = split(noises[j][...] * x)
            lined.append(jnp.concatenate([high, low, high], 1))
        section = times(jnp.concatenate(lined, 0), real_right)
        columns = []
        for k in range(2):
            at = slice(k * lanes, (k + 1) * lanes)
            columns.append(stacked(*turned(section[at, :lanes], section[at, lanes:], wc, ws), 0))
        done = times(block, jnp.concatenate(columns, 1))
        gc, gs = big_turn[r, pl.ds(own, depth), :lanes], big_turn[r, pl.ds(own, depth), lanes:]
        for k in range(2):
            at = slice(k * lanes, (k + 1) * lanes)
            re, im = turned(done[:depth, at], done[depth:, at], gc, gs)
            work[r, k, 0] = re
            work[r, k, 1] = im
    noisy = small_dft([(work[r, 0, 0], work[r, 0, 1]) for r in range(rows)], -1)
    noisy_residual = small_dft([(work[r, 1, 0], work[r, 1, 1]) for r in range(rows)], -1)
    for a in range(rows):
        k, s = kernel[:, a], symbol[:, a]
        total = 0.0
        for part in range(2):
            base = spectrum[a, part, pl.ds(own, depth)]
            ki = k * (base / s) + noisy[a][part]
            applied = k * (base - step_size * ki) + noisy_residual[a][part]
            adjoint = (
                (weight / curvature) * base
                - (2.0 * weight * step_size / curvature) * ki
                - (2.0 * step_size) * applied
            )
            total += adjoint * base
        shares[a] = -total / (samples * s * s)
    width = rows // probes
    column = lax.axis_index("probe")
    for d in range(probes):
        for k in range(width):
            outs[d][:, k] = shares[(column ^ d) * width + k]


def call(kernel, outs, scratch, *operands):
    whole = pl.BlockSpec(memory_space=pltpu.VMEM)
    typed = [out if isinstance(out[0], tuple) else (out, exact) for out in outs]
    shapes = tuple(jax.ShapeDtypeStruct(shape, dtype) for shape, dtype in typed)
    return pl.pallas_call(
        kernel,
        out_shape=shapes,
        in_specs=[whole] * len(operands),
        out_specs=(whole,) * len(shapes),
        scratch_shapes=[pltpu.VMEM(shape, exact) for shape in scratch],
        compiler_params=pltpu.CompilerParams(vmem_limit_bytes=24 << 20),
        cost_estimate=pl.CostEstimate(flops=0, bytes_accessed=0, transcendentals=0),
    )(*operands)


def swapped(x, axis, d):
    return lax.ppermute(x, axis, [(i, i ^ d) for i in range(lax.axis_size(axis))])


def after(x, *earlier):
    return lax.optimization_barrier((x, *earlier))[0]


def after(x, *earlier):
    return lax.optimization_barrier((x, *earlier))[0]


def other_core(x):
    return swapped(x, "seq", 1)


def next_chip(x):
    return swapped(x, "seq", 2)


def beyond_middle(x):
    return swapped(x, "seq", 4)


def gathered_shards(probe_bits, noise_var, kernel_spectrum, symbol, grad_prev):
    rows = kernel_spectrum.shape[1]
    probes = lax.axis_size("probe")
    half, depth, width = rows // 2, lanes // rows, rows // probes
    kernel = kernel_spectrum.T.reshape(rows, depth, lanes).transpose(1, 0, 2)
    symbols = symbol.T.reshape(rows, depth, lanes).transpose(1, 0, 2)
    before = grad_prev.T.reshape(width, depth, lanes).transpose(1, 0, 2)
    square = (lanes, lanes)
    dft, turns = tables(rows)
    first = lanes + 2 * half * depth + lead
    block, mine, noise, dft, turns = pl.pallas_call(
        functools.partial(pack_kernel, half),
        out_shape=(
            *(pltpu.VMEM((n, lanes), exact) for n in (first + lanes, first, lanes)),
            pltpu.VMEM(dft.shape, near),
            pltpu.VMEM(turns.shape, exact),
        ),
        in_specs=[pl.BlockSpec(memory_space=pl.ANY)] * 6,
        out_specs=(pl.BlockSpec(memory_space=pltpu.VMEM),) * 5,
        scratch_shapes=[
            pltpu.VMEM(square, jnp.int32),
            pltpu.VMEM(square, exact),
            pltpu.VMEM(kernel.shape, exact),
            pltpu.VMEM(kernel.shape, exact),
            pltpu.SemaphoreType.DMA((6,)),
        ],
    )(probe_bits.reshape(square), noise_var.reshape(square), kernel, symbols, dft, turns)
    far = beyond_middle(mine)
    neighbour = next_chip(block)
    blocks = [block, other_core(block), neighbour, other_core(neighbour), far, other_core(far)]
    passed_on = next_chip(far)
    far_noise = beyond_middle(after(noise, far))
    passed_noise = next_chip(far_noise)
    found, left, big_turn = call(
        functools.partial(early_kernel, rows),
        [(rows - 2, 2, *square), ((2 * lanes, 6 * lanes), near), (rows, lanes, 2 * lanes)],
        [],
        *blocks,
        dft,
        turns,
    )
    last = after(passed_on, found, far_noise)
    blocks += [last, other_core(last)]
    field = (rows, *square)
    spectrum, precond, circulant = call(
        functools.partial(inverse_kernel, rows),
        [(rows, 2, *square), field, field],
        [(half, *square), (half, *square), (rows, lead, lanes), (rows, 2, 2, *square)],
        *blocks,
        found,
        left,
        dft,
        turns,
        big_turn,
    )
    passed_noise = after(passed_noise, precond)
    noises = [far_noise, other_core(far_noise), passed_noise, other_core(passed_noise)]
    share = (depth, width, lanes)
    residual, *parts = call(
        functools.partial(adjoint_kernel, rows, probes),
        [square] + [share] * probes,
        [field, field, (rows, 2, 2, depth, lanes), (rows, depth, lanes)],
        *blocks,
        *noises,
        precond,
        circulant,
        spectrum,
        kernel,
        symbols,
        left,
        dft,
        turns,
        big_turn,
    )
    arrived = [swapped(parts[d], "probe", d) for d in reversed(range(1, probes))]
    total = before + sum(arrived, parts[0]) / probes
    total = total.transpose(1, 0, 2).reshape(width, depth * lanes).T
    return residual.reshape(probe_bits.shape), total


highest = lax.Precision.HIGHEST
minor_width = 128


def dft_table(height, breadth, modulus, orient):
    left_index = jnp.arange(height, dtype=jnp.int32)[:, None]
    right_index = jnp.arange(breadth, dtype=jnp.int32)[None, :]
    phases = (
        orient * 2.0 * math.pi / modulus * (left_index * right_index % modulus).astype(jnp.float32)
    )
    return (jnp.cos(phases), jnp.sin(phases))


def complex_product(pattern, real_part, imaginary, cosine_table, sine_table):
    real_cos = jnp.einsum(pattern, real_part, cosine_table, precision=highest)
    real_sin = jnp.einsum(pattern, real_part, sine_table, precision=highest)
    if imaginary is None:
        return (real_cos, real_sin)
    imag_cos = jnp.einsum(pattern, imaginary, cosine_table, precision=highest)
    imag_sin = jnp.einsum(pattern, imaginary, sine_table, precision=highest)
    return (real_cos - imag_sin, real_sin + imag_cos)


def rotate(real_part, imaginary, cosine_table, sine_table):
    return (
        real_part * cosine_table - imaginary * sine_table,
        real_part * sine_table + imaginary * cosine_table,
    )


def forward_rows(series):
    major_len = series.shape[-2]
    length = major_len * minor_width
    cosine_table, sine_table = dft_table(major_len, major_len, major_len, -1.0)
    section_real, section_imag = complex_product(
        "...mi,mk->...ik", series, None, cosine_table, sine_table
    )
    turn_cos, turn_sin = dft_table(minor_width, major_len, length, -1.0)
    twisted_real, twisted_imag = rotate(section_real, section_imag, turn_cos, turn_sin)
    cosine_table, sine_table = dft_table(minor_width, minor_width, minor_width, -1.0)
    return complex_product("...ik,ij->...jk", twisted_real, twisted_imag, cosine_table, sine_table)


def inverse_rows(real_part, imaginary):
    major_len = real_part.shape[-1]
    length = major_len * minor_width
    cosine_table, sine_table = dft_table(minor_width, minor_width, minor_width, 1.0)
    section_real, section_imag = complex_product(
        "...jk,ji->...ik", real_part, imaginary, cosine_table, sine_table
    )
    turn_cos, turn_sin = dft_table(minor_width, major_len, length, 1.0)
    twisted_real, twisted_imag = rotate(section_real, section_imag, turn_cos, turn_sin)
    cosine_table, sine_table = dft_table(major_len, major_len, major_len, 1.0)
    final_real, unused = complex_product(
        "...ik,km->...mi", twisted_real, twisted_imag, cosine_table, sine_table
    )
    return final_real


def global_twiddle(local_rows, major_len, samples, orient):
    row_index = lax.axis_index("seq") * local_rows + jnp.arange(local_rows, dtype=jnp.int32)
    column_index = (
        jnp.arange(minor_width, dtype=jnp.int32)[:, None] * major_len
        + jnp.arange(major_len, dtype=jnp.int32)[None, :]
    )
    phases = (
        orient
        * 2.0
        * math.pi
        / samples
        * (row_index[:, None, None] * column_index[None, :, :] % samples).astype(jnp.float32)
    )
    return (jnp.cos(phases), jnp.sin(phases))


def forward_spectrum(series):
    local_rows = series.shape[1]
    major_len = series.shape[2]
    devices = lax.axis_size("seq")
    all_rows = local_rows * devices
    samples = all_rows * major_len * minor_width
    real_part, imaginary = forward_rows(series)
    turn_cos, turn_sin = global_twiddle(local_rows, major_len, samples, -1.0)
    turned_real, turned_imag = rotate(real_part, imaginary, turn_cos, turn_sin)
    arrived = lax.all_to_all(
        jnp.stack([turned_real, turned_imag]), "seq", split_axis=3, concat_axis=2, tiled=True
    )
    block = minor_width // devices * major_len
    arrived = arrived.reshape(arrived.shape[0], arrived.shape[1], all_rows, block)
    cosine_table, sine_table = dft_table(all_rows, all_rows, all_rows, -1.0)
    return complex_product("zrb,ra->zba", arrived[0], arrived[1], cosine_table, sine_table)


def inverse_field(spectrum_real, spectrum_imag):
    all_rows = spectrum_real.shape[2]
    block = spectrum_real.shape[1]
    devices = lax.axis_size("seq")
    major_len = block * devices // minor_width
    cosine_table, sine_table = dft_table(all_rows, all_rows, all_rows, 1.0)
    back_real, back_imag = complex_product(
        "zba,ar->zrb", spectrum_real, spectrum_imag, cosine_table, sine_table
    )
    stacked = jnp.stack([back_real, back_imag])
    stacked = stacked.reshape(
        stacked.shape[0], stacked.shape[1], all_rows, minor_width // devices, major_len
    )
    arrived = lax.all_to_all(stacked, "seq", split_axis=2, concat_axis=3, tiled=True)
    local_rows = arrived.shape[2]
    samples = all_rows * major_len * minor_width
    turn_cos, turn_sin = global_twiddle(local_rows, major_len, samples, 1.0)
    turned_real, turned_imag = rotate(arrived[0], arrived[1], turn_cos, turn_sin)
    return inverse_rows(turned_real, turned_imag) / samples


def shards(probe_bits, noise_var, kernel_spectrum, symbol, grad_prev):
    field_shape = (
        probe_bits.shape[0],
        probe_bits.shape[1],
        probe_bits.shape[2] // minor_width,
        minor_width,
    )
    sign_field = (2 * probe_bits - 1).astype(jnp.float32).reshape(field_shape)
    noise_field = noise_var.reshape(field_shape[1:])
    samples = kernel_spectrum.shape[1] * noise_var.shape[1]
    base_real, base_imag = forward_spectrum(sign_field)
    scaled_real = base_real / symbol
    scaled_imag = base_imag / symbol
    precond = inverse_field(scaled_real, scaled_imag)
    again_real, again_imag = forward_spectrum(precond)
    circulant = inverse_field(kernel_spectrum * again_real, kernel_spectrum * again_imag)
    kernel_image = circulant + noise_field * precond
    numerator, curvature = lax.psum(
        (jnp.sum(sign_field * precond), jnp.sum(precond * kernel_image)), "seq"
    )
    step_size = numerator / curvature
    residual = sign_field - step_size * kernel_image
    cross_term = lax.psum(jnp.sum(residual * kernel_image), "seq")
    weight = -2.0 * cross_term
    resid_real, resid_imag = forward_spectrum(residual)
    applied = (
        inverse_field(kernel_spectrum * resid_real, kernel_spectrum * resid_imag)
        + noise_field * residual
    )
    adjoint = (
        weight / curvature * sign_field
        - 2.0 * weight * step_size / curvature * kernel_image
        - 2.0 * step_size * applied
    )
    adjoint_real, adjoint_imag = forward_spectrum(adjoint)
    local_grad = -(adjoint_real[0] * base_real[0] + adjoint_imag[0] * base_imag[0]) / (
        samples * symbol * symbol
    )
    probes = lax.axis_size("probe")
    summed = lax.psum(local_grad, "probe")
    share_width = summed.shape[1] // probes
    own_share = lax.dynamic_slice_in_dim(
        summed, lax.axis_index("probe") * share_width, share_width, 1
    )
    grad_total = grad_prev + own_share / probes
    return (residual.reshape(probe_bits.shape), grad_total)


def fits(mesh, cols, rows):
    seq, probe = mesh.shape["seq"], mesh.shape["probe"]
    powers = all(n & (n - 1) == 0 for n in (rows, seq, probe))
    return powers and rows == seq == lead and rows % probe == 0 and probe > 1 and cols == lanes * lanes


def solution(mesh):
    placed = (
        P("probe", "seq", None),
        P("seq", None),
        P("seq", None),
        P("seq", None),
        P("seq", "probe"),
    )

    def whole(probe_bits, noise_var, kernel_spectrum, symbol, grad_prev):
        small = fits(mesh, *symbol.shape)
        return jax.shard_map(
            gathered_shards if small else shards,
            mesh=mesh,
            in_specs=placed,
            out_specs=(P("probe", "seq", None), P("seq", "probe")),
            check_vma=False,
        )(probe_bits, noise_var, kernel_spectrum, symbol, grad_prev)

    return whole
```

```python
import functools
import math

import jax
import jax.numpy as jnp
import numpy as np
from jax import lax
from jax.experimental import pallas as pl
from jax.experimental.pallas import tpu as pltpu
from jax.sharding import PartitionSpec as P

lanes = 128
lead = 8
near = jnp.bfloat16
exact = jnp.float32


def split_table(table):
    high = table.astype(near)
    low = (table - high.astype(np.float64)).astype(near)
    return high, low


def angle_parts(phase):
    return np.cos(phase), np.sin(phase)


@functools.cache
def tables(rows):
    index = np.arange(lanes, dtype=np.float64)
    turn = -2.0 * np.pi
    c, s = angle_parts(turn * (np.outer(index, index) % lanes) / lanes)
    c_high, c_low = split_table(c)
    s_high, s_low = split_table(s)
    row_len = lanes * lanes
    wc, ws = angle_parts(turn * np.outer(index, index) / row_len)
    flat = index[:, None] * lanes + index[None, :]
    gc, gs = angle_parts(turn * flat / (rows * row_len))
    turns = np.stack([np.concatenate([wc, ws], 1), np.concatenate([gc, gs], 1)])
    return np.stack([c_high, s_high, c_low, s_low]), turns.astype(np.float32)


def split(x):
    high = x.astype(near)
    return high, (x - high.astype(exact)).astype(near)


def stacked(first, second, axis):
    fh, fl = split(first)
    sh, sl = split(second)
    return jnp.concatenate([fh, sh], axis), jnp.concatenate([fl, sl], axis)


def times(left, right):
    return jnp.dot(left, right, preferred_element_type=exact)


def left_product(table, columns):
    n = table.shape[0] // 2
    high = jnp.concatenate([column[0] for column in columns], 1)
    low = jnp.concatenate([column[1] for column in columns], 1)
    both = times(table[...], high)
    return both[:n] + both[n:] + times(table[:n], low)


def turned(re, im, cos, sin):
    return re * cos - im * sin, re * sin + im * cos


def turned_back(re, im, cos, sin):
    return re * cos + im * sin, im * cos - re * sin


def add(x, y):
    return x[0] + y[0], x[1] + y[1]


def sub(x, y):
    return x[0] - y[0], x[1] - y[1]


def unit_turn(x, k, n, orient):
    k = (k * orient) % n
    if k == 0:
        return x
    if 4 * k == n:
        return -x[1], x[0]
    if 2 * k == n:
        return -x[0], -x[1]
    if 4 * k == 3 * n:
        return x[1], -x[0]
    cos, sin = math.cos(2 * math.pi * k / n), math.sin(2 * math.pi * k / n)
    return x[0] * cos - x[1] * sin, x[0] * sin + x[1] * cos


def small_dft(xs, orient):
    n = len(xs)
    if n == 1:
        return xs
    even, odd = small_dft(xs[0::2], orient), small_dft(xs[1::2], orient)
    odd = [unit_turn(x, k, n, orient) for k, x in enumerate(odd)]
    return [add(e, o) for e, o in zip(even, odd)] + [sub(e, o) for e, o in zip(even, odd)]


def half_dft(xs, orient):
    n = 2 * len(xs)
    even = small_dft(xs, orient)
    odd = small_dft([unit_turn(x, k, n, orient) for k, x in enumerate(xs)], orient)
    return [(odd if r % 2 else even)[r // 2] for r in range(n)]


def pack_kernel(half, first, *refs):
    sources, out, sent, held, landed, done = refs[:6], refs[6], refs[7], refs[8:10], refs[10:14], refs[14]
    targets = (*landed, *held)
    copies = [pltpu.make_async_copy(sources[i], targets[i], done.at[i]) for i in range(6)]
    for copy in copies:
        copy.start()
    bits, noise, kernel, symbol = landed
    copies[0].wait()
    out[:lanes] = (2 * bits[...] - 1).astype(exact).T
    copies[1].wait()
    out[first:] = noise[...].T
    copies[2].wait()
    copies[3].wait()
    depth = kernel.shape[0]
    for a in range(half):
        at = lanes + a * depth
        out[at : at + depth] = kernel[:, a]
        at += half * depth
        out[at : at + depth] = symbol[:, a]
    middle = jnp.concatenate([kernel[0, half : half + 1], symbol[0, half : half + 1]], 0)
    out[first - lead : first] = jnp.concatenate([middle] * (lead // 2), 0)
    sent[:first] = out[:first]
    share = lanes // 2
    side = lax.rem(lax.axis_index("probe"), 2)
    sent[first:] = out[pl.ds(pl.multiple_of(first + side * share, lead), share)]
    copies[4].wait()
    copies[5].wait()


def row_spectra(signs, rows, sign_right, left, w, big_turn):
    lined = [jnp.concatenate([x[:lanes].astype(near)] * 2, 1) for x in signs]
    section = times(jnp.concatenate(lined, 0), sign_right)
    out = []
    for j in range(0, len(signs), 2):
        columns = []
        for k in (j, j + 1):
            at = slice(k * lanes, (k + 1) * lanes)
            columns.append(stacked(*turned(section[at, :lanes], section[at, lanes:], *w), 0))
        done = left_product(left, columns)
        for k in range(2):
            at, r = slice(k * lanes, (k + 1) * lanes), rows[j + k]
            out.append(turned(done[:lanes, at], done[lanes:, at], big_turn[r, :, :lanes], big_turn[r, :, lanes:]))
    return out


def sign_table(dft):
    c_high, s_high, c_low, s_low = (dft[k] for k in range(4))
    return jnp.concatenate([jnp.concatenate([c_high, s_high], 1), jnp.concatenate([c_low, s_low], 1)], 0)


def early_slots(rows):
    return [0, 1, *range(2, rows - 2, 2)]


def early_kernel(rows, *refs):
    early = early_slots(rows)
    blocks = refs[: len(early)]
    dft, turns, found, left, big_turn = refs[len(early) :]
    me = lax.axis_index("seq")
    c_high, s_high, c_low, s_low = (dft[k] for k in range(4))
    left[:lanes] = jnp.concatenate([c_high, -s_high], 1)
    left[lanes : 2 * lanes] = jnp.concatenate([s_high, c_high], 1)
    left[2 * lanes : 3 * lanes] = jnp.concatenate([c_low, -s_low], 1)
    left[3 * lanes :] = jnp.concatenate([s_low, c_low], 1)
    for t in range(0, lanes, lead):
        at = slice(t, t + lead)
        one = turns[1, at, :lanes], turns[1, at, lanes:]
        powers = [(jnp.ones((lead, lanes), exact), jnp.zeros((lead, lanes), exact)), one]
        for r in range(2, rows):
            powers.append(turned(*powers[r // 2], *powers[r - r // 2]))
        for r in range(rows):
            big_turn[r, at, :lanes] = powers[r][0]
            big_turn[r, at, lanes:] = powers[r][1]
    w = turns[0, :, :lanes], turns[0, :, lanes:]
    at = [me ^ j for j in early]
    for k, x in enumerate(row_spectra(blocks, at, sign_table(dft), left, w, big_turn)):
        found[k, 0], found[k, 1] = x


def inverse_kernel(rows, *refs):
    blocks = refs[:rows]
    found, left, dft, turns, big_turn, spectrum, precond, circulant, kernel, symbol, ends, work = refs[rows:]
    half, early = rows // 2, early_slots(rows)
    depth = lanes // rows
    samples = rows * lanes * lanes
    me = lax.axis_index("seq")
    w = turns[0, :, :lanes], turns[0, :, lanes:]
    for k, j in enumerate(early):
        work[me ^ j, 0, 0], work[me ^ j, 0, 1] = found[k, 0], found[k, 1]
    late = [j for j in range(rows) if j not in early]
    at = [me ^ j for j in late]
    for r, x in zip(at, row_spectra([blocks[j] for j in late], at, sign_table(dft), left, w, big_turn)):
        work[r, 0, 0], work[r, 0, 1] = x
    for t in range(0, lanes, lead):
        at = slice(t, t + lead)
        out = small_dft([(work[r, 0, 0, at], work[r, 0, 1, at]) for r in range(rows)], -1)
        for a in range(rows):
            spectrum[a, 0, at], spectrum[a, 1, at] = out[a]
    for j in range(rows):
        place = pl.multiple_of((me ^ j) * depth, depth)
        for a in range(half):
            at = lanes + a * depth
            kernel[a, pl.ds(place, depth)] = blocks[j][at : at + depth]
            at += half * depth
            symbol[a, pl.ds(place, depth)] = blocks[j][at : at + depth]
        ends[me ^ j] = blocks[j][lanes + 2 * half * depth : lanes + 2 * half * depth + lead]
    middle = spectrum[half, 0, 0:1, 0:1] / ends[0, 1:2, 0:1] / samples
    middle_image = middle * ends[0, 0:1, 0:1]
    for t in range(0, lanes, lead):
        at = slice(t, t + lead)
        first, second = [], []
        for a in range(half):
            scale = 2.0 / samples / symbol[a, at]
            if a == 0 and t == 0:
                zero = (lax.broadcasted_iota(jnp.int32, (lead, lanes), 0) == 0) & (
                    lax.broadcasted_iota(jnp.int32, (lead, lanes), 1) == 0
                )
                scale = jnp.where(zero, 0.5 * scale, scale)
            re, im = spectrum[a, 0, at] * scale, spectrum[a, 1, at] * scale
            first.append((re, im))
            second.append((re * kernel[a, at], im * kernel[a, at]))
        for field, entries in enumerate((first, second)):
            out = half_dft(entries, 1)
            for r in range(rows):
                re, im = turned_back(*out[r], big_turn[r, at, :lanes], big_turn[r, at, lanes:])
                work[r, field, 0, at] = re
                work[r, field, 1, at] = im
    c_high, s_high, c_low, s_low = (dft[k] for k in range(4))
    back_right = jnp.concatenate([jnp.concatenate([c_high, s_high], 0), jnp.concatenate([c_low, s_low], 0)], 1)
    highs, lows = [], []
    for r in range(rows):
        columns = [stacked(work[r, field, 1], work[r, field, 0], 0) for field in range(2)]
        done = left_product(left, columns)
        for field in range(2):
            at = slice(field * lanes, (field + 1) * lanes)
            high, low = stacked(*turned_back(done[lanes:, at], done[:lanes, at], *w), 1)
            highs.append(high)
            lows.append(low)
    both = times(jnp.concatenate(highs, 0), back_right)
    done = both[:, :lanes] + both[:, lanes:] + times(jnp.concatenate(lows, 0), back_right[:, :lanes])
    for r in range(rows):
        sign = 1.0 if r % 2 == 0 else -1.0
        precond[r] = done[2 * r * lanes : (2 * r + 1) * lanes] + sign * middle
        circulant[r] = done[(2 * r + 1) * lanes : (2 * r + 2) * lanes] + sign * middle_image


def whole_sum(x):
    return jnp.sum(jnp.sum(x, axis=0, keepdims=True), axis=1, keepdims=True)


def adjoint_kernel(rows, probes, *refs):
    signs = [refs[j].at[:lanes] for j in range(rows)]
    share = lanes // 2
    own_noises = [refs[j].at[refs[j].shape[0] - lanes :] for j in range(2)]
    held = [refs[j].at[refs[j].shape[0] - share :] for j in range(2, rows)]
    others = [refs[rows + k].at[at : at + share] for at in (0, share) for k in (0, 1)] + list(refs[rows + 2 : rows + 4])
    refs = refs[rows + 4 :]
    noise = refs[-1]
    refs = refs[:-1]
    side = lax.rem(lax.axis_index("probe"), 2) * share
    for j in range(rows - 2):
        noise[j, pl.ds(pl.multiple_of(side, share), share)] = held[j][...]
        noise[j, pl.ds(pl.multiple_of(share - side, share), share)] = others[j][...]
    noises = (*own_noises, *(noise.at[j] for j in range(rows - 2)))
    precond, circulant, spectrum, kernel, symbol, left, dft, turns, big_turn, residual_out = refs[:10]
    outs = refs[10 : 10 + probes]
    image, work, shares = refs[10 + probes :]
    depth = lanes // rows
    samples = rows * lanes * lanes
    me = lax.axis_index("seq")
    c_high, s_high, c_low, s_low = (dft[k] for k in range(4))
    wide_high, wide_low = jnp.concatenate([c_high, s_high], 1), jnp.concatenate([c_low, s_low], 1)
    twice_high = jnp.concatenate([wide_high, wide_high], 0)
    w = turns[0, :, :lanes], turns[0, :, lanes:]
    own = pl.multiple_of(me * depth, depth)
    parts = [left[pl.ds(pl.multiple_of(k * lanes + own, depth), depth)] for k in range(4)]
    block = jnp.concatenate(parts, 0)

    def own_spectra(fields, k):
        highs, lows = zip(*(split(x) for x in fields))
        highs, lows = jnp.concatenate(highs, 0), jnp.concatenate(lows, 0)
        section = times(jnp.concatenate([highs, lows], 1), twice_high) + times(highs, wide_low)
        for j in range(0, rows, 2):
            columns = []
            for i in (j, j + 1):
                at = slice(i * lanes, (i + 1) * lanes)
                columns.append(stacked(*turned(section[at, :lanes], section[at, lanes:], *w), 0))
            done = left_product(block, columns)
            for i in range(2):
                at, r = slice(i * lanes, (i + 1) * lanes), me ^ (j + i)
                gc, gs = big_turn[r, pl.ds(own, depth), :lanes], big_turn[r, pl.ds(own, depth), lanes:]
                work[r, k, 0], work[r, k, 1] = turned(done[:depth, at], done[depth:, at], gc, gs)

    numerator = jnp.zeros((lanes, lanes), exact)
    curvature = jnp.zeros((lanes, lanes), exact)
    fields = []
    for j in range(rows):
        p = precond[me ^ j]
        noisy = noises[j][...] * p
        ki = circulant[me ^ j] + noisy
        image[j] = ki
        fields.append(noisy)
        numerator += signs[j][...] * p
        curvature += p * ki
    numerator, curvature = whole_sum(numerator), whole_sum(curvature)
    own_spectra(fields, 0)
    step_size = numerator / curvature
    cross = jnp.zeros((lanes, lanes), exact)
    fields = []
    for j in range(rows):
        residual = signs[j][...] - step_size * image[j]
        cross += residual * image[j]
        fields.append(noises[j][...] * residual)
        if j == 0:
            residual_out[...] = residual.T
    weight = -2.0 * whole_sum(cross)
    own_spectra(fields, 1)
    noisy = small_dft([(work[r, 0, 0], work[r, 0, 1]) for r in range(rows)], -1)
    noisy_residual = small_dft([(work[r, 1, 0], work[r, 1, 1]) for r in range(rows)], -1)
    for a in range(rows):
        k, s = kernel[:, a], symbol[:, a]
        total = 0.0
        for part in range(2):
            base = spectrum[a, part, pl.ds(own, depth)]
            ki = k * (base / s) + noisy[a][part]
            applied = k * (base - step_size * ki) + noisy_residual[a][part]
            adjoint = (
                (weight / curvature) * base
                - (2.0 * weight * step_size / curvature) * ki
                - (2.0 * step_size) * applied
            )
            total += adjoint * base
        shares[a] = -total / (samples * s * s)
    width = rows // probes
    column = lax.axis_index("probe")
    for d in range(probes):
        for k in range(width):
            outs[d][:, k] = shares[(column ^ d) * width + k]


def call(kernel, outs, scratch, *operands):
    whole = pl.BlockSpec(memory_space=pltpu.VMEM)
    typed = [out if isinstance(out[0], tuple) else (out, exact) for out in outs]
    shapes = tuple(pltpu.VMEM(shape, dtype) for shape, dtype in typed)
    return pl.pallas_call(
        kernel,
        out_shape=shapes,
        in_specs=[whole] * len(operands),
        out_specs=(whole,) * len(shapes),
        scratch_shapes=[pltpu.VMEM(shape, exact) for shape in scratch],
        compiler_params=pltpu.CompilerParams(vmem_limit_bytes=24 << 20),
        cost_estimate=pl.CostEstimate(flops=0, bytes_accessed=0, transcendentals=0),
    )(*operands)


def swapped(x, axis, d):
    return lax.ppermute(x, axis, [(i, i ^ d) for i in range(lax.axis_size(axis))])


def after(x, *earlier):
    return lax.optimization_barrier((x, *earlier))[0]


def after(x, *earlier):
    return lax.optimization_barrier((x, *earlier))[0]


def other_core(x):
    return swapped(x, "seq", 1)


def across_x(x):
    return swapped(x, "probe", 1)


def next_chip(x):
    return swapped(x, "seq", 2)


def beyond_middle(x):
    return swapped(x, "seq", 4)


def gathered_shards(probe_bits, noise_var, kernel_spectrum, symbol, grad_prev):
    rows = kernel_spectrum.shape[1]
    probes = lax.axis_size("probe")
    half, depth, width = rows // 2, lanes // rows, rows // probes
    kernel = kernel_spectrum.T.reshape(rows, depth, lanes).transpose(1, 0, 2)
    symbols = symbol.T.reshape(rows, depth, lanes).transpose(1, 0, 2)
    before = grad_prev.T.reshape(width, depth, lanes).transpose(1, 0, 2)
    square = (lanes, lanes)
    dft, turns = tables(rows)
    first = lanes + 2 * half * depth + lead
    block, sent, dft, turns = pl.pallas_call(
        functools.partial(pack_kernel, half, first),
        out_shape=(
            pltpu.VMEM((first + lanes, lanes), exact),
            pltpu.VMEM((first + lanes // 2, lanes), exact),
            pltpu.VMEM(dft.shape, near),
            pltpu.VMEM(turns.shape, exact),
        ),
        in_specs=[pl.BlockSpec(memory_space=pl.ANY)] * 6,
        out_specs=(pl.BlockSpec(memory_space=pltpu.VMEM),) * 4,
        scratch_shapes=[
            pltpu.VMEM(square, jnp.int32),
            pltpu.VMEM(square, exact),
            pltpu.VMEM(kernel.shape, exact),
            pltpu.VMEM(kernel.shape, exact),
            pltpu.SemaphoreType.DMA((6,)),
        ],
    )(probe_bits.reshape(square), noise_var.reshape(square), kernel, symbols, dft, turns)
    far = beyond_middle(sent)
    neighbour = next_chip(sent)
    passed_on = next_chip(far)
    early = [block, other_core(block), neighbour, far]
    found, left, big_turn = call(
        functools.partial(early_kernel, rows),
        [(len(early), 2, *square), ((4 * lanes, 2 * lanes), near), (rows, lanes, 2 * lanes)],
        [],
        *early,
        dft,
        turns,
    )
    halves = across_x(jnp.concatenate([neighbour[first:], far[first:]], 0))
    blocks = early[:2]
    for x, earlier in ((neighbour, found), (far, found), (passed_on, halves)):
        blocks += [x, other_core(after(x, earlier))]
    field = (rows, *square)
    spectrum, precond, circulant = call(
        functools.partial(inverse_kernel, rows),
        [(rows, 2, *square), field, field],
        [(half, *square), (half, *square), (rows, lead, lanes), (rows, 2, 2, *square)],
        *blocks,
        found,
        left,
        dft,
        turns,
        big_turn,
    )
    passed_half = next_chip(halves[lanes // 2 :])
    last = after(passed_half, precond)
    noises = [halves, other_core(halves), last, other_core(last)]
    share = (depth, width, lanes)
    residual, *parts = call(
        functools.partial(adjoint_kernel, rows, probes),
        [square] + [share] * probes,
        [field, (rows, 2, 2, depth, lanes), (rows, depth, lanes), (rows - 2, *square)],
        *blocks,
        *noises,
        precond,
        circulant,
        spectrum,
        kernel,
        symbols,
        left,
        dft,
        turns,
        big_turn,
    )
    arrived = [swapped(parts[d], "probe", d) for d in range(1, probes)]
    total = lax.optimization_barrier(parts[0] + arrived.pop())
    total = before + sum(arrived, total) / probes
    total = total.transpose(1, 0, 2).reshape(width, depth * lanes).T
    return residual.reshape(probe_bits.shape), total


highest = lax.Precision.HIGHEST
minor_width = 128


def dft_table(height, breadth, modulus, orient):
    left_index = jnp.arange(height, dtype=jnp.int32)[:, None]
    right_index = jnp.arange(breadth, dtype=jnp.int32)[None, :]
    phases = (
        orient * 2.0 * math.pi / modulus * (left_index * right_index % modulus).astype(jnp.float32)
    )
    return (jnp.cos(phases), jnp.sin(phases))


def complex_product(pattern, real_part, imaginary, cosine_table, sine_table):
    real_cos = jnp.einsum(pattern, real_part, cosine_table, precision=highest)
    real_sin = jnp.einsum(pattern, real_part, sine_table, precision=highest)
    if imaginary is None:
        return (real_cos, real_sin)
    imag_cos = jnp.einsum(pattern, imaginary, cosine_table, precision=highest)
    imag_sin = jnp.einsum(pattern, imaginary, sine_table, precision=highest)
    return (real_cos - imag_sin, real_sin + imag_cos)


def rotate(real_part, imaginary, cosine_table, sine_table):
    return (
        real_part * cosine_table - imaginary * sine_table,
        real_part * sine_table + imaginary * cosine_table,
    )


def forward_rows(series):
    major_len = series.shape[-2]
    length = major_len * minor_width
    cosine_table, sine_table = dft_table(major_len, major_len, major_len, -1.0)
    section_real, section_imag = complex_product(
        "...mi,mk->...ik", series, None, cosine_table, sine_table
    )
    turn_cos, turn_sin = dft_table(minor_width, major_len, length, -1.0)
    twisted_real, twisted_imag = rotate(section_real, section_imag, turn_cos, turn_sin)
    cosine_table, sine_table = dft_table(minor_width, minor_width, minor_width, -1.0)
    return complex_product("...ik,ij->...jk", twisted_real, twisted_imag, cosine_table, sine_table)


def inverse_rows(real_part, imaginary):
    major_len = real_part.shape[-1]
    length = major_len * minor_width
    cosine_table, sine_table = dft_table(minor_width, minor_width, minor_width, 1.0)
    section_real, section_imag = complex_product(
        "...jk,ji->...ik", real_part, imaginary, cosine_table, sine_table
    )
    turn_cos, turn_sin = dft_table(minor_width, major_len, length, 1.0)
    twisted_real, twisted_imag = rotate(section_real, section_imag, turn_cos, turn_sin)
    cosine_table, sine_table = dft_table(major_len, major_len, major_len, 1.0)
    final_real, unused = complex_product(
        "...ik,km->...mi", twisted_real, twisted_imag, cosine_table, sine_table
    )
    return final_real


def global_twiddle(local_rows, major_len, samples, orient):
    row_index = lax.axis_index("seq") * local_rows + jnp.arange(local_rows, dtype=jnp.int32)
    column_index = (
        jnp.arange(minor_width, dtype=jnp.int32)[:, None] * major_len
        + jnp.arange(major_len, dtype=jnp.int32)[None, :]
    )
    phases = (
        orient
        * 2.0
        * math.pi
        / samples
        * (row_index[:, None, None] * column_index[None, :, :] % samples).astype(jnp.float32)
    )
    return (jnp.cos(phases), jnp.sin(phases))


def forward_spectrum(series):
    local_rows = series.shape[1]
    major_len = series.shape[2]
    devices = lax.axis_size("seq")
    all_rows = local_rows * devices
    samples = all_rows * major_len * minor_width
    real_part, imaginary = forward_rows(series)
    turn_cos, turn_sin = global_twiddle(local_rows, major_len, samples, -1.0)
    turned_real, turned_imag = rotate(real_part, imaginary, turn_cos, turn_sin)
    arrived = lax.all_to_all(
        jnp.stack([turned_real, turned_imag]), "seq", split_axis=3, concat_axis=2, tiled=True
    )
    block = minor_width // devices * major_len
    arrived = arrived.reshape(arrived.shape[0], arrived.shape[1], all_rows, block)
    cosine_table, sine_table = dft_table(all_rows, all_rows, all_rows, -1.0)
    return complex_product("zrb,ra->zba", arrived[0], arrived[1], cosine_table, sine_table)


def inverse_field(spectrum_real, spectrum_imag):
    all_rows = spectrum_real.shape[2]
    block = spectrum_real.shape[1]
    devices = lax.axis_size("seq")
    major_len = block * devices // minor_width
    cosine_table, sine_table = dft_table(all_rows, all_rows, all_rows, 1.0)
    back_real, back_imag = complex_product(
        "zba,ar->zrb", spectrum_real, spectrum_imag, cosine_table, sine_table
    )
    stacked = jnp.stack([back_real, back_imag])
    stacked = stacked.reshape(
        stacked.shape[0], stacked.shape[1], all_rows, minor_width // devices, major_len
    )
    arrived = lax.all_to_all(stacked, "seq", split_axis=2, concat_axis=3, tiled=True)
    local_rows = arrived.shape[2]
    samples = all_rows * major_len * minor_width
    turn_cos, turn_sin = global_twiddle(local_rows, major_len, samples, 1.0)
    turned_real, turned_imag = rotate(arrived[0], arrived[1], turn_cos, turn_sin)
    return inverse_rows(turned_real, turned_imag) / samples


def shards(probe_bits, noise_var, kernel_spectrum, symbol, grad_prev):
    field_shape = (
        probe_bits.shape[0],
        probe_bits.shape[1],
        probe_bits.shape[2] // minor_width,
        minor_width,
    )
    sign_field = (2 * probe_bits - 1).astype(jnp.float32).reshape(field_shape)
    noise_field = noise_var.reshape(field_shape[1:])
    samples = kernel_spectrum.shape[1] * noise_var.shape[1]
    base_real, base_imag = forward_spectrum(sign_field)
    scaled_real = base_real / symbol
    scaled_imag = base_imag / symbol
    precond = inverse_field(scaled_real, scaled_imag)
    again_real, again_imag = forward_spectrum(precond)
    circulant = inverse_field(kernel_spectrum * again_real, kernel_spectrum * again_imag)
    kernel_image = circulant + noise_field * precond
    numerator, curvature = lax.psum(
        (jnp.sum(sign_field * precond), jnp.sum(precond * kernel_image)), "seq"
    )
    step_size = numerator / curvature
    residual = sign_field - step_size * kernel_image
    cross_term = lax.psum(jnp.sum(residual * kernel_image), "seq")
    weight = -2.0 * cross_term
    resid_real, resid_imag = forward_spectrum(residual)
    applied = (
        inverse_field(kernel_spectrum * resid_real, kernel_spectrum * resid_imag)
        + noise_field * residual
    )
    adjoint = (
        weight / curvature * sign_field
        - 2.0 * weight * step_size / curvature * kernel_image
        - 2.0 * step_size * applied
    )
    adjoint_real, adjoint_imag = forward_spectrum(adjoint)
    local_grad = -(adjoint_real[0] * base_real[0] + adjoint_imag[0] * base_imag[0]) / (
        samples * symbol * symbol
    )
    probes = lax.axis_size("probe")
    summed = lax.psum(local_grad, "probe")
    share_width = summed.shape[1] // probes
    own_share = lax.dynamic_slice_in_dim(
        summed, lax.axis_index("probe") * share_width, share_width, 1
    )
    grad_total = grad_prev + own_share / probes
    return (residual.reshape(probe_bits.shape), grad_total)


def fits(mesh, cols, rows):
    seq, probe = mesh.shape["seq"], mesh.shape["probe"]
    powers = all(n & (n - 1) == 0 for n in (rows, seq, probe))
    return powers and rows == seq == lead and rows % probe == 0 and probe > 1 and cols == lanes * lanes


def solution(mesh):
    placed = (
        P("probe", "seq", None),
        P("seq", None),
        P("seq", None),
        P("seq", None),
        P("seq", "probe"),
    )

    def whole(probe_bits, noise_var, kernel_spectrum, symbol, grad_prev):
        small = fits(mesh, *symbol.shape)
        return jax.shard_map(
            gathered_shards if small else shards,
            mesh=mesh,
            in_specs=placed,
            out_specs=(P("probe", "seq", None), P("seq", "probe")),
            check_vma=False,
        )(probe_bits, noise_var, kernel_spectrum, symbol, grad_prev)

    return whole
```

```python
import functools
import math

import jax
import jax.numpy as jnp
import numpy as np
from jax import lax
from jax.experimental import pallas as pl
from jax.experimental.pallas import tpu as pltpu
from jax.sharding import PartitionSpec as P

lanes = 128
lead = 8
near = jnp.bfloat16
exact = jnp.float32


def split_table(table):
    high = table.astype(near)
    low = (table - high.astype(np.float64)).astype(near)
    return high, low


def angle_parts(phase):
    return np.cos(phase), np.sin(phase)


@functools.cache
def tables(rows):
    index = np.arange(lanes, dtype=np.float64)
    turn = -2.0 * np.pi
    c, s = angle_parts(turn * (np.outer(index, index) % lanes) / lanes)
    c_high, c_low = split_table(c)
    s_high, s_low = split_table(s)
    row_len = lanes * lanes
    wc, ws = angle_parts(turn * np.outer(index, index) / row_len)
    flat = index[:, None] * lanes + index[None, :]
    gc, gs = angle_parts(turn * flat / (rows * row_len))
    turns = np.stack([np.concatenate([wc, ws], 1), np.concatenate([gc, gs], 1)])
    return np.stack([c_high, s_high, c_low, s_low]), turns.astype(np.float32)


def split(x):
    high = x.astype(near)
    return high, (x - high.astype(exact)).astype(near)


def stacked(first, second, axis):
    fh, fl = split(first)
    sh, sl = split(second)
    return jnp.concatenate([fh, sh], axis), jnp.concatenate([fl, sl], axis)


def times(left, right):
    return jnp.dot(left, right, preferred_element_type=exact)


def left_product(table, columns):
    n = table.shape[0] // 2
    high = jnp.concatenate([column[0] for column in columns], 1)
    low = jnp.concatenate([column[1] for column in columns], 1)
    both = times(table[...], high)
    return both[:n] + both[n:] + times(table[:n], low)


def turned(re, im, cos, sin):
    return re * cos - im * sin, re * sin + im * cos


def turned_back(re, im, cos, sin):
    return re * cos + im * sin, im * cos - re * sin


def add(x, y):
    return x[0] + y[0], x[1] + y[1]


def sub(x, y):
    return x[0] - y[0], x[1] - y[1]


def unit_turn(x, k, n, orient):
    k = (k * orient) % n
    if k == 0:
        return x
    if 4 * k == n:
        return -x[1], x[0]
    if 2 * k == n:
        return -x[0], -x[1]
    if 4 * k == 3 * n:
        return x[1], -x[0]
    cos, sin = math.cos(2 * math.pi * k / n), math.sin(2 * math.pi * k / n)
    return x[0] * cos - x[1] * sin, x[0] * sin + x[1] * cos


def small_dft(xs, orient):
    n = len(xs)
    if n == 1:
        return xs
    even, odd = small_dft(xs[0::2], orient), small_dft(xs[1::2], orient)
    odd = [unit_turn(x, k, n, orient) for k, x in enumerate(odd)]
    return [add(e, o) for e, o in zip(even, odd)] + [sub(e, o) for e, o in zip(even, odd)]


def half_dft(xs, orient):
    n = 2 * len(xs)
    even = small_dft(xs, orient)
    odd = small_dft([unit_turn(x, k, n, orient) for k, x in enumerate(xs)], orient)
    return [(odd if r % 2 else even)[r // 2] for r in range(n)]


def pack_kernel(half, first, *refs):
    sources, out, sent, held, landed, done = refs[:6], refs[6], refs[7], refs[8:10], refs[10:14], refs[14]
    targets = (*landed, *held)
    copies = [pltpu.make_async_copy(sources[i], targets[i], done.at[i]) for i in range(6)]
    for copy in copies:
        copy.start()
    bits, noise, kernel, symbol = landed
    copies[0].wait()
    out[:lanes] = (2 * bits[...] - 1).astype(exact).T
    copies[1].wait()
    out[first:] = noise[...].T
    copies[2].wait()
    copies[3].wait()
    depth = kernel.shape[0]
    for a in range(half):
        at = lanes + a * depth
        out[at : at + depth] = kernel[:, a]
        at += half * depth
        out[at : at + depth] = symbol[:, a]
    middle = jnp.concatenate([kernel[0, half : half + 1], symbol[0, half : half + 1]], 0)
    out[first - lead : first] = jnp.concatenate([middle] * (lead // 2), 0)
    sent[:first] = out[:first]
    share = lanes // 2
    side = lax.rem(lax.axis_index("probe"), 2)
    sent[first:] = out[pl.ds(pl.multiple_of(first + side * share, lead), share)]
    copies[4].wait()
    copies[5].wait()


def row_spectra(signs, rows, sign_right, left, w, big_turn):
    lined = [jnp.concatenate([x[:lanes].astype(near)] * 2, 1) for x in signs]
    section = times(jnp.concatenate(lined, 0), sign_right)
    out = []
    for j in range(0, len(signs), 2):
        columns = []
        for k in (j, j + 1):
            at = slice(k * lanes, (k + 1) * lanes)
            columns.append(stacked(*turned(section[at, :lanes], section[at, lanes:], *w), 0))
        done = left_product(left, columns)
        for k in range(2):
            at, r = slice(k * lanes, (k + 1) * lanes), rows[j + k]
            out.append(turned(done[:lanes, at], done[lanes:, at], big_turn[r, :, :lanes], big_turn[r, :, lanes:]))
    return out


def sign_table(dft):
    c_high, s_high, c_low, s_low = (dft[k] for k in range(4))
    return jnp.concatenate([jnp.concatenate([c_high, s_high], 1), jnp.concatenate([c_low, s_low], 1)], 0)


def early_slots(rows):
    return [0, 1, *range(2, rows - 2, 2)]


def early_kernel(rows, *refs):
    early = early_slots(rows)
    blocks = refs[: len(early)]
    dft, turns, found, left, big_turn = refs[len(early) :]
    me = lax.axis_index("seq")
    c_high, s_high, c_low, s_low = (dft[k] for k in range(4))
    left[:lanes] = jnp.concatenate([c_high, -s_high], 1)
    left[lanes : 2 * lanes] = jnp.concatenate([s_high, c_high], 1)
    left[2 * lanes : 3 * lanes] = jnp.concatenate([c_low, -s_low], 1)
    left[3 * lanes :] = jnp.concatenate([s_low, c_low], 1)
    for t in range(0, lanes, lead):
        at = slice(t, t + lead)
        one = turns[1, at, :lanes], turns[1, at, lanes:]
        powers = [(jnp.ones((lead, lanes), exact), jnp.zeros((lead, lanes), exact)), one]
        for r in range(2, rows):
            powers.append(turned(*powers[r // 2], *powers[r - r // 2]))
        for r in range(rows):
            big_turn[r, at, :lanes] = powers[r][0]
            big_turn[r, at, lanes:] = powers[r][1]
    w = turns[0, :, :lanes], turns[0, :, lanes:]
    at = [me ^ j for j in early]
    for k, x in enumerate(row_spectra(blocks, at, sign_table(dft), left, w, big_turn)):
        found[k, 0], found[k, 1] = x


def inverse_kernel(rows, *refs):
    blocks = refs[:rows]
    found, left, dft, turns, big_turn, spectrum, precond, circulant, kernel, symbol, ends, work = refs[rows:]
    half, early = rows // 2, early_slots(rows)
    depth = lanes // rows
    samples = rows * lanes * lanes
    me = lax.axis_index("seq")
    w = turns[0, :, :lanes], turns[0, :, lanes:]
    for k, j in enumerate(early):
        work[me ^ j, 0, 0], work[me ^ j, 0, 1] = found[k, 0], found[k, 1]
    late = [j for j in range(rows) if j not in early]
    at = [me ^ j for j in late]
    for r, x in zip(at, row_spectra([blocks[j] for j in late], at, sign_table(dft), left, w, big_turn)):
        work[r, 0, 0], work[r, 0, 1] = x
    for t in range(0, lanes, lead):
        at = slice(t, t + lead)
        out = small_dft([(work[r, 0, 0, at], work[r, 0, 1, at]) for r in range(rows)], -1)
        for a in range(rows):
            spectrum[a, 0, at], spectrum[a, 1, at] = out[a]
    for j in range(rows):
        place = pl.multiple_of((me ^ j) * depth, depth)
        for a in range(half):
            at = lanes + a * depth
            kernel[a, pl.ds(place, depth)] = blocks[j][at : at + depth]
            at += half * depth
            symbol[a, pl.ds(place, depth)] = blocks[j][at : at + depth]
        ends[me ^ j] = blocks[j][lanes + 2 * half * depth : lanes + 2 * half * depth + lead]
    middle = spectrum[half, 0, 0:1, 0:1] / ends[0, 1:2, 0:1] / samples
    middle_image = middle * ends[0, 0:1, 0:1]
    for t in range(0, lanes, lead):
        at = slice(t, t + lead)
        first, second = [], []
        for a in range(half):
            scale = 2.0 / samples / symbol[a, at]
            if a == 0 and t == 0:
                zero = (lax.broadcasted_iota(jnp.int32, (lead, lanes), 0) == 0) & (
                    lax.broadcasted_iota(jnp.int32, (lead, lanes), 1) == 0
                )
                scale = jnp.where(zero, 0.5 * scale, scale)
            re, im = spectrum[a, 0, at] * scale, spectrum[a, 1, at] * scale
            first.append((re, im))
            second.append((re * kernel[a, at], im * kernel[a, at]))
        for field, entries in enumerate((first, second)):
            out = half_dft(entries, 1)
            for r in range(rows):
                re, im = turned_back(*out[r], big_turn[r, at, :lanes], big_turn[r, at, lanes:])
                work[r, field, 0, at] = re
                work[r, field, 1, at] = im
    c_high, s_high, c_low, s_low = (dft[k] for k in range(4))
    back_right = jnp.concatenate([jnp.concatenate([c_high, s_high], 0), jnp.concatenate([c_low, s_low], 0)], 1)
    highs, lows = [], []
    for r in range(rows):
        columns = [stacked(work[r, field, 1], work[r, field, 0], 0) for field in range(2)]
        done = left_product(left, columns)
        for field in range(2):
            at = slice(field * lanes, (field + 1) * lanes)
            high, low = stacked(*turned_back(done[lanes:, at], done[:lanes, at], *w), 1)
            highs.append(high)
            lows.append(low)
    both = times(jnp.concatenate(highs, 0), back_right)
    done = both[:, :lanes] + both[:, lanes:] + times(jnp.concatenate(lows, 0), back_right[:, :lanes])
    for r in range(rows):
        sign = 1.0 if r % 2 == 0 else -1.0
        precond[r] = done[2 * r * lanes : (2 * r + 1) * lanes] + sign * middle
        circulant[r] = done[(2 * r + 1) * lanes : (2 * r + 2) * lanes] + sign * middle_image


def whole_sum(x):
    return jnp.sum(jnp.sum(x, axis=0, keepdims=True), axis=1, keepdims=True)


def folded(x):
    return sum(x[t : t + lead] for t in range(0, x.shape[0], lead))


def own_spectra(fields, at, left, dft, turns, big_turn):
    rows = big_turn.shape[0]
    depth = lanes // rows
    own = pl.multiple_of(lax.axis_index("seq") * depth, depth)
    c_high, s_high, c_low, s_low = (dft[k] for k in range(4))
    wide_high, wide_low = jnp.concatenate([c_high, s_high], 1), jnp.concatenate([c_low, s_low], 1)
    twice_high = jnp.concatenate([wide_high, wide_high], 0)
    w = turns[0, :, :lanes], turns[0, :, lanes:]
    parts = [left[pl.ds(pl.multiple_of(k * lanes + own, depth), depth)] for k in range(4)]
    block = jnp.concatenate(parts, 0)
    highs, lows = zip(*(split(x) for x in fields))
    highs, lows = jnp.concatenate(highs, 0), jnp.concatenate(lows, 0)
    section = times(jnp.concatenate([highs, lows], 1), twice_high) + times(highs, wide_low)
    out = []
    for j in range(0, len(fields), 2):
        columns = []
        for i in (j, j + 1):
            here = slice(i * lanes, (i + 1) * lanes)
            columns.append(stacked(*turned(section[here, :lanes], section[here, lanes:], *w), 0))
        done = left_product(block, columns)
        for i in range(2):
            here, r = slice(i * lanes, (i + 1) * lanes), at[j + i]
            gc, gs = big_turn[r, pl.ds(own, depth), :lanes], big_turn[r, pl.ds(own, depth), lanes:]
            out.append(turned(done[:depth, here], done[depth:, here], gc, gs))
    return out


def whole_noise(target, held, other):
    share = lanes // 2
    side = lax.rem(lax.axis_index("probe"), 2) * share
    target[pl.ds(pl.multiple_of(side, share), share)] = held[held.shape[0] - share :]
    target[pl.ds(pl.multiple_of(share - side, share), share)] = other[...]


def images(slots, signs, noises, precond, circulant, image, sums):
    me = lax.axis_index("seq")
    fields = []
    numerator, curvature = sums
    for k, j in enumerate(slots):
        p = precond[me ^ j]
        noisy = noises[k][...] * p
        ki = circulant[me ^ j] + noisy
        image[k] = ki
        fields.append(noisy)
        numerator += folded(signs[k][:lanes] * p)
        curvature += folded(p * ki)
    return fields, (numerator, curvature)


def near_kernel(rows, *refs):
    n = rows - 2
    blocks, others = refs[:n], refs[n : n + 2]
    precond, circulant, left, dft, turns, big_turn, image, noise, found, sums = refs[n + 2 :]
    share = lanes // 2
    for j in range(2):
        noise[j] = blocks[j][blocks[j].shape[0] - lanes :]
    for j in range(2, n):
        whole_noise(noise.at[j], blocks[j], others[j % 2].at[(j - 2) // 2 * share : j // 2 * share])
    zero = jnp.zeros((lead, lanes), exact)
    noises = [noise.at[j] for j in range(n)]
    fields, totals = images(range(n), blocks, noises, precond, circulant, image, (zero, zero))
    sums[0], sums[1] = totals
    at = [lax.axis_index("seq") ^ j for j in range(n)]
    for j, x in enumerate(own_spectra(fields, at, left, dft, turns, big_turn)):
        found[j, 0], found[j, 1] = x


def adjoint_kernel(rows, probes, *refs):
    n = rows - 2
    signs = [refs[j].at[:lanes] for j in range(rows)]
    blocks, others = refs[:rows], refs[rows : rows + 2]
    near_image, near_noise, near_found, near_sums = refs[rows + 2 : rows + 6]
    refs = refs[rows + 6 :]
    precond, circulant, spectrum, kernel, symbol, left, dft, turns, big_turn, residual_out = refs[:10]
    outs = refs[10 : 10 + probes]
    image, noise, work, shares = refs[10 + probes :]
    depth = lanes // rows
    samples = rows * lanes * lanes
    me = lax.axis_index("seq")
    own = pl.multiple_of(me * depth, depth)
    at = [me ^ j for j in range(rows)]
    for j in range(n):
        work[at[j], 0, 0], work[at[j], 0, 1] = near_found[j, 0], near_found[j, 1]
    for k in range(2):
        whole_noise(noise.at[k], blocks[n + k], others[k])
    last_noises = [noise.at[k] for k in range(2)]
    sums = (near_sums[0], near_sums[1])
    fields, sums = images(range(n, rows), blocks[n:], last_noises, precond, circulant, image, sums)
    noises = [near_noise.at[j] for j in range(n)] + last_noises
    image = [near_image.at[j] for j in range(n)] + [image.at[k] for k in range(2)]
    numerator, curvature = whole_sum(sums[0]), whole_sum(sums[1])
    for j, x in zip(range(n, rows), own_spectra(fields, at[n:], left, dft, turns, big_turn)):
        work[at[j], 0, 0], work[at[j], 0, 1] = x
    step_size = numerator / curvature
    cross = jnp.zeros((lead, lanes), exact)
    fields = []
    for j in range(rows):
        residual = signs[j][...] - step_size * image[j][...]
        cross += folded(residual * image[j][...])
        fields.append(noises[j][...] * residual)
        if j == 0:
            residual_out[...] = residual.T
    weight = -2.0 * whole_sum(cross)
    for r, x in zip(at, own_spectra(fields, at, left, dft, turns, big_turn)):
        work[r, 1, 0], work[r, 1, 1] = x
    noisy = small_dft([(work[r, 0, 0], work[r, 0, 1]) for r in range(rows)], -1)
    noisy_residual = small_dft([(work[r, 1, 0], work[r, 1, 1]) for r in range(rows)], -1)
    for a in range(rows):
        k, s = kernel[:, a], symbol[:, a]
        total = 0.0
        for part in range(2):
            base = spectrum[a, part, pl.ds(own, depth)]
            ki = k * (base / s) + noisy[a][part]
            applied = k * (base - step_size * ki) + noisy_residual[a][part]
            adjoint = (
                (weight / curvature) * base
                - (2.0 * weight * step_size / curvature) * ki
                - (2.0 * step_size) * applied
            )
            total += adjoint * base
        shares[a] = -total / (samples * s * s)
    width = rows // probes
    column = lax.axis_index("probe")
    for d in range(probes):
        for k in range(width):
            outs[d][:, k] = shares[(column ^ d) * width + k]


def call(kernel, outs, scratch, *operands):
    whole = pl.BlockSpec(memory_space=pltpu.VMEM)
    typed = [out if isinstance(out[0], tuple) else (out, exact) for out in outs]
    shapes = tuple(pltpu.VMEM(shape, dtype) for shape, dtype in typed)
    return pl.pallas_call(
        kernel,
        out_shape=shapes,
        in_specs=[whole] * len(operands),
        out_specs=(whole,) * len(shapes),
        scratch_shapes=[pltpu.VMEM(shape, exact) for shape in scratch],
        compiler_params=pltpu.CompilerParams(vmem_limit_bytes=24 << 20),
        cost_estimate=pl.CostEstimate(flops=0, bytes_accessed=0, transcendentals=0),
    )(*operands)


def swapped(x, axis, d):
    return lax.ppermute(x, axis, [(i, i ^ d) for i in range(lax.axis_size(axis))])


def after(x, *earlier):
    return lax.optimization_barrier((x, *earlier))[0]


def after(x, *earlier):
    return lax.optimization_barrier((x, *earlier))[0]


def other_core(x):
    return swapped(x, "seq", 1)


def across_x(x):
    return swapped(x, "probe", 1)


def next_chip(x):
    return swapped(x, "seq", 2)


def beyond_middle(x):
    return swapped(x, "seq", 4)


def adjoint_calls(
    rows, probes, blocks, noises, precond, circulant, spectrum, kernel, symbols, left, dft, turns, big_turn
):
    square = (lanes, lanes)
    depth, width, n = lanes // rows, rows // probes, rows - 2
    tables_held = (left, dft, turns, big_turn)
    near_parts = call(
        functools.partial(near_kernel, rows),
        [(n, *square), (n, *square), (n, 2, depth, lanes), (2, lead, lanes)],
        [],
        *blocks[:n],
        *noises[:2],
        precond,
        circulant,
        *tables_held,
    )
    return call(
        functools.partial(adjoint_kernel, rows, probes),
        [square] + [(depth, width, lanes)] * probes,
        [(2, *square), (2, *square), (rows, 2, 2, depth, lanes), (rows, depth, lanes)],
        *blocks,
        *noises[2:],
        *near_parts,
        precond,
        circulant,
        spectrum,
        kernel,
        symbols,
        *tables_held,
    )


def gathered_shards(probe_bits, noise_var, kernel_spectrum, symbol, grad_prev):
    rows = kernel_spectrum.shape[1]
    probes = lax.axis_size("probe")
    half, depth, width = rows // 2, lanes // rows, rows // probes
    kernel = kernel_spectrum.T.reshape(rows, depth, lanes).transpose(1, 0, 2)
    symbols = symbol.T.reshape(rows, depth, lanes).transpose(1, 0, 2)
    before = grad_prev.T.reshape(width, depth, lanes).transpose(1, 0, 2)
    square = (lanes, lanes)
    dft, turns = tables(rows)
    first = lanes + 2 * half * depth + lead
    block, sent, dft, turns = pl.pallas_call(
        functools.partial(pack_kernel, half, first),
        out_shape=(
            pltpu.VMEM((first + lanes, lanes), exact),
            pltpu.VMEM((first + lanes // 2, lanes), exact),
            pltpu.VMEM(dft.shape, near),
            pltpu.VMEM(turns.shape, exact),
        ),
        in_specs=[pl.BlockSpec(memory_space=pl.ANY)] * 6,
        out_specs=(pl.BlockSpec(memory_space=pltpu.VMEM),) * 4,
        scratch_shapes=[
            pltpu.VMEM(square, jnp.int32),
            pltpu.VMEM(square, exact),
            pltpu.VMEM(kernel.shape, exact),
            pltpu.VMEM(kernel.shape, exact),
            pltpu.SemaphoreType.DMA((6,)),
        ],
    )(probe_bits.reshape(square), noise_var.reshape(square), kernel, symbols, dft, turns)
    far = beyond_middle(sent)
    neighbour = next_chip(sent)
    passed_on = next_chip(far)
    early = [block, other_core(block), neighbour, far]
    found, left, big_turn = call(
        functools.partial(early_kernel, rows),
        [(len(early), 2, *square), ((4 * lanes, 2 * lanes), near), (rows, lanes, 2 * lanes)],
        [],
        *early,
        dft,
        turns,
    )
    halves = across_x(jnp.concatenate([neighbour[first:], far[first:]], 0))
    blocks = early[:2]
    for x, earlier in ((neighbour, found), (far, found), (passed_on, halves)):
        blocks += [x, other_core(after(x, earlier))]
    field = (rows, *square)
    spectrum, precond, circulant = call(
        functools.partial(inverse_kernel, rows),
        [(rows, 2, *square), field, field],
        [(half, *square), (half, *square), (rows, lead, lanes), (rows, 2, 2, *square)],
        *blocks,
        found,
        left,
        dft,
        turns,
        big_turn,
    )
    passed_half = next_chip(halves[lanes // 2 :])
    last = after(passed_half, precond)
    noises = [halves, other_core(halves), last, other_core(last)]
    residual, *parts = adjoint_calls(
        rows, probes, blocks, noises, precond, circulant, spectrum, kernel, symbols, left, dft, turns, big_turn
    )
    arrived = [swapped(parts[d], "probe", d) for d in range(1, probes)]
    total = lax.optimization_barrier(parts[0] + arrived.pop())
    total = before + sum(arrived, total) / probes
    total = total.transpose(1, 0, 2).reshape(width, depth * lanes).T
    return residual.reshape(probe_bits.shape), total


highest = lax.Precision.HIGHEST
minor_width = 128


def dft_table(height, breadth, modulus, orient):
    left_index = jnp.arange(height, dtype=jnp.int32)[:, None]
    right_index = jnp.arange(breadth, dtype=jnp.int32)[None, :]
    phases = (
        orient * 2.0 * math.pi / modulus * (left_index * right_index % modulus).astype(jnp.float32)
    )
    return (jnp.cos(phases), jnp.sin(phases))


def complex_product(pattern, real_part, imaginary, cosine_table, sine_table):
    real_cos = jnp.einsum(pattern, real_part, cosine_table, precision=highest)
    real_sin = jnp.einsum(pattern, real_part, sine_table, precision=highest)
    if imaginary is None:
        return (real_cos, real_sin)
    imag_cos = jnp.einsum(pattern, imaginary, cosine_table, precision=highest)
    imag_sin = jnp.einsum(pattern, imaginary, sine_table, precision=highest)
    return (real_cos - imag_sin, real_sin + imag_cos)


def rotate(real_part, imaginary, cosine_table, sine_table):
    return (
        real_part * cosine_table - imaginary * sine_table,
        real_part * sine_table + imaginary * cosine_table,
    )


def forward_rows(series):
    major_len = series.shape[-2]
    length = major_len * minor_width
    cosine_table, sine_table = dft_table(major_len, major_len, major_len, -1.0)
    section_real, section_imag = complex_product(
        "...mi,mk->...ik", series, None, cosine_table, sine_table
    )
    turn_cos, turn_sin = dft_table(minor_width, major_len, length, -1.0)
    twisted_real, twisted_imag = rotate(section_real, section_imag, turn_cos, turn_sin)
    cosine_table, sine_table = dft_table(minor_width, minor_width, minor_width, -1.0)
    return complex_product("...ik,ij->...jk", twisted_real, twisted_imag, cosine_table, sine_table)


def inverse_rows(real_part, imaginary):
    major_len = real_part.shape[-1]
    length = major_len * minor_width
    cosine_table, sine_table = dft_table(minor_width, minor_width, minor_width, 1.0)
    section_real, section_imag = complex_product(
        "...jk,ji->...ik", real_part, imaginary, cosine_table, sine_table
    )
    turn_cos, turn_sin = dft_table(minor_width, major_len, length, 1.0)
    twisted_real, twisted_imag = rotate(section_real, section_imag, turn_cos, turn_sin)
    cosine_table, sine_table = dft_table(major_len, major_len, major_len, 1.0)
    final_real, unused = complex_product(
        "...ik,km->...mi", twisted_real, twisted_imag, cosine_table, sine_table
    )
    return final_real


def global_twiddle(local_rows, major_len, samples, orient):
    row_index = lax.axis_index("seq") * local_rows + jnp.arange(local_rows, dtype=jnp.int32)
    column_index = (
        jnp.arange(minor_width, dtype=jnp.int32)[:, None] * major_len
        + jnp.arange(major_len, dtype=jnp.int32)[None, :]
    )
    phases = (
        orient
        * 2.0
        * math.pi
        / samples
        * (row_index[:, None, None] * column_index[None, :, :] % samples).astype(jnp.float32)
    )
    return (jnp.cos(phases), jnp.sin(phases))


def forward_spectrum(series):
    local_rows = series.shape[1]
    major_len = series.shape[2]
    devices = lax.axis_size("seq")
    all_rows = local_rows * devices
    samples = all_rows * major_len * minor_width
    real_part, imaginary = forward_rows(series)
    turn_cos, turn_sin = global_twiddle(local_rows, major_len, samples, -1.0)
    turned_real, turned_imag = rotate(real_part, imaginary, turn_cos, turn_sin)
    arrived = lax.all_to_all(
        jnp.stack([turned_real, turned_imag]), "seq", split_axis=3, concat_axis=2, tiled=True
    )
    block = minor_width // devices * major_len
    arrived = arrived.reshape(arrived.shape[0], arrived.shape[1], all_rows, block)
    cosine_table, sine_table = dft_table(all_rows, all_rows, all_rows, -1.0)
    return complex_product("zrb,ra->zba", arrived[0], arrived[1], cosine_table, sine_table)


def inverse_field(spectrum_real, spectrum_imag):
    all_rows = spectrum_real.shape[2]
    block = spectrum_real.shape[1]
    devices = lax.axis_size("seq")
    major_len = block * devices // minor_width
    cosine_table, sine_table = dft_table(all_rows, all_rows, all_rows, 1.0)
    back_real, back_imag = complex_product(
        "zba,ar->zrb", spectrum_real, spectrum_imag, cosine_table, sine_table
    )
    stacked = jnp.stack([back_real, back_imag])
    stacked = stacked.reshape(
        stacked.shape[0], stacked.shape[1], all_rows, minor_width // devices, major_len
    )
    arrived = lax.all_to_all(stacked, "seq", split_axis=2, concat_axis=3, tiled=True)
    local_rows = arrived.shape[2]
    samples = all_rows * major_len * minor_width
    turn_cos, turn_sin = global_twiddle(local_rows, major_len, samples, 1.0)
    turned_real, turned_imag = rotate(arrived[0], arrived[1], turn_cos, turn_sin)
    return inverse_rows(turned_real, turned_imag) / samples


def shards(probe_bits, noise_var, kernel_spectrum, symbol, grad_prev):
    field_shape = (
        probe_bits.shape[0],
        probe_bits.shape[1],
        probe_bits.shape[2] // minor_width,
        minor_width,
    )
    sign_field = (2 * probe_bits - 1).astype(jnp.float32).reshape(field_shape)
    noise_field = noise_var.reshape(field_shape[1:])
    samples = kernel_spectrum.shape[1] * noise_var.shape[1]
    base_real, base_imag = forward_spectrum(sign_field)
    scaled_real = base_real / symbol
    scaled_imag = base_imag / symbol
    precond = inverse_field(scaled_real, scaled_imag)
    again_real, again_imag = forward_spectrum(precond)
    circulant = inverse_field(kernel_spectrum * again_real, kernel_spectrum * again_imag)
    kernel_image = circulant + noise_field * precond
    numerator, curvature = lax.psum(
        (jnp.sum(sign_field * precond), jnp.sum(precond * kernel_image)), "seq"
    )
    step_size = numerator / curvature
    residual = sign_field - step_size * kernel_image
    cross_term = lax.psum(jnp.sum(residual * kernel_image), "seq")
    weight = -2.0 * cross_term
    resid_real, resid_imag = forward_spectrum(residual)
    applied = (
        inverse_field(kernel_spectrum * resid_real, kernel_spectrum * resid_imag)
        + noise_field * residual
    )
    adjoint = (
        weight / curvature * sign_field
        - 2.0 * weight * step_size / curvature * kernel_image
        - 2.0 * step_size * applied
    )
    adjoint_real, adjoint_imag = forward_spectrum(adjoint)
    local_grad = -(adjoint_real[0] * base_real[0] + adjoint_imag[0] * base_imag[0]) / (
        samples * symbol * symbol
    )
    probes = lax.axis_size("probe")
    summed = lax.psum(local_grad, "probe")
    share_width = summed.shape[1] // probes
    own_share = lax.dynamic_slice_in_dim(
        summed, lax.axis_index("probe") * share_width, share_width, 1
    )
    grad_total = grad_prev + own_share / probes
    return (residual.reshape(probe_bits.shape), grad_total)


def fits(mesh, cols, rows):
    seq, probe = mesh.shape["seq"], mesh.shape["probe"]
    powers = all(n & (n - 1) == 0 for n in (rows, seq, probe))
    return powers and rows == seq == lead and rows % probe == 0 and probe > 1 and cols == lanes * lanes


def solution(mesh):
    placed = (
        P("probe", "seq", None),
        P("seq", None),
        P("seq", None),
        P("seq", None),
        P("seq", "probe"),
    )

    def whole(probe_bits, noise_var, kernel_spectrum, symbol, grad_prev):
        small = fits(mesh, *symbol.shape)
        return jax.shard_map(
            gathered_shards if small else shards,
            mesh=mesh,
            in_specs=placed,
            out_specs=(P("probe", "seq", None), P("seq", "probe")),
            check_vma=False,
        )(probe_bits, noise_var, kernel_spectrum, symbol, grad_prev)

    return whole
```

```python
import functools
import math

import jax
import jax.numpy as jnp
import numpy as np
from jax import lax
from jax.experimental import pallas as pl
from jax.experimental.pallas import tpu as pltpu
from jax.sharding import PartitionSpec as P

lanes = 128
lead = 8
near = jnp.bfloat16
exact = jnp.float32


def split_table(table):
    high = table.astype(near)
    low = (table - high.astype(np.float64)).astype(near)
    return high, low


def angle_parts(phase):
    return np.cos(phase), np.sin(phase)


@functools.cache
def tables(rows):
    index = np.arange(lanes, dtype=np.float64)
    turn = -2.0 * np.pi
    c, s = angle_parts(turn * (np.outer(index, index) % lanes) / lanes)
    c_high, c_low = split_table(c)
    s_high, s_low = split_table(s)
    row_len = lanes * lanes
    wc, ws = angle_parts(turn * np.outer(index, index) / row_len)
    flat = index[:, None] * lanes + index[None, :]
    gc, gs = angle_parts(turn * flat / (rows * row_len))
    turns = np.stack([np.concatenate([wc, ws], 1), np.concatenate([gc, gs], 1)])
    return np.stack([c_high, s_high, c_low, s_low]), turns.astype(np.float32)


def split(x):
    high = x.astype(near)
    return high, (x - high.astype(exact)).astype(near)


def stacked(first, second, axis):
    fh, fl = split(first)
    sh, sl = split(second)
    return jnp.concatenate([fh, sh], axis), jnp.concatenate([fl, sl], axis)


def times(left, right):
    return jnp.dot(left, right, preferred_element_type=exact)


def left_product(table, columns):
    n = table.shape[0] // 2
    high = jnp.concatenate([column[0] for column in columns], 1)
    low = jnp.concatenate([column[1] for column in columns], 1)
    both = times(table[...], high)
    return both[:n] + both[n:] + times(table[:n], low)


def turned(re, im, cos, sin):
    return re * cos - im * sin, re * sin + im * cos


def turned_back(re, im, cos, sin):
    return re * cos + im * sin, im * cos - re * sin


def add(x, y):
    return x[0] + y[0], x[1] + y[1]


def sub(x, y):
    return x[0] - y[0], x[1] - y[1]


def unit_turn(x, k, n, orient):
    k = (k * orient) % n
    if k == 0:
        return x
    if 4 * k == n:
        return -x[1], x[0]
    if 2 * k == n:
        return -x[0], -x[1]
    if 4 * k == 3 * n:
        return x[1], -x[0]
    cos, sin = math.cos(2 * math.pi * k / n), math.sin(2 * math.pi * k / n)
    return x[0] * cos - x[1] * sin, x[0] * sin + x[1] * cos


def small_dft(xs, orient):
    n = len(xs)
    if n == 1:
        return xs
    even, odd = small_dft(xs[0::2], orient), small_dft(xs[1::2], orient)
    odd = [unit_turn(x, k, n, orient) for k, x in enumerate(odd)]
    return [add(e, o) for e, o in zip(even, odd)] + [sub(e, o) for e, o in zip(even, odd)]


def half_dft(xs, orient):
    n = 2 * len(xs)
    even = small_dft(xs, orient)
    odd = small_dft([unit_turn(x, k, n, orient) for k, x in enumerate(xs)], orient)
    return [(odd if r % 2 else even)[r // 2] for r in range(n)]


def pack_kernel(half, first, *refs):
    sources, out, sent, held, landed, done = refs[:6], refs[6], refs[7], refs[8:10], refs[10:14], refs[14]
    targets = (*landed, *held)
    copies = [pltpu.make_async_copy(sources[i], targets[i], done.at[i]) for i in range(6)]
    for copy in copies:
        copy.start()
    bits, noise, kernel, symbol = landed
    copies[0].wait()
    out[:lanes] = (2 * bits[...] - 1).astype(exact).T
    copies[1].wait()
    out[first:] = noise[...].T
    copies[2].wait()
    copies[3].wait()
    depth = kernel.shape[0]
    for a in range(half):
        at = lanes + a * depth
        out[at : at + depth] = kernel[:, a]
        at += half * depth
        out[at : at + depth] = symbol[:, a]
    middle = jnp.concatenate([kernel[0, half : half + 1], symbol[0, half : half + 1]], 0)
    out[first - lead : first] = jnp.concatenate([middle] * (lead // 2), 0)
    sent[:first] = out[:first]
    share = lanes // 2
    side = lax.rem(lax.axis_index("probe"), 2)
    sent[first:] = out[pl.ds(pl.multiple_of(first + side * share, lead), share)]
    copies[4].wait()
    copies[5].wait()


def row_spectra(signs, rows, sign_right, left, w, big_turn):
    lined = [jnp.concatenate([x[:lanes].astype(near)] * 2, 1) for x in signs]
    section = times(jnp.concatenate(lined, 0), sign_right)
    out = []
    for j in range(0, len(signs), 2):
        columns = []
        for k in (j, j + 1):
            at = slice(k * lanes, (k + 1) * lanes)
            columns.append(stacked(*turned(section[at, :lanes], section[at, lanes:], *w), 0))
        done = left_product(left, columns)
        for k in range(2):
            at, r = slice(k * lanes, (k + 1) * lanes), rows[j + k]
            out.append(turned(done[:lanes, at], done[lanes:, at], big_turn[r, :, :lanes], big_turn[r, :, lanes:]))
    return out


def sign_table(dft):
    c_high, s_high, c_low, s_low = (dft[k] for k in range(4))
    return jnp.concatenate([jnp.concatenate([c_high, s_high], 1), jnp.concatenate([c_low, s_low], 1)], 0)


def early_slots(rows):
    return [0, 1, *range(2, rows - 2, 2)]


def early_kernel(rows, *refs):
    early = early_slots(rows)
    blocks = refs[: len(early)]
    dft, turns, found, left, big_turn = refs[len(early) :]
    me = lax.axis_index("seq")
    c_high, s_high, c_low, s_low = (dft[k] for k in range(4))
    left[:lanes] = jnp.concatenate([c_high, -s_high], 1)
    left[lanes : 2 * lanes] = jnp.concatenate([s_high, c_high], 1)
    left[2 * lanes : 3 * lanes] = jnp.concatenate([c_low, -s_low], 1)
    left[3 * lanes :] = jnp.concatenate([s_low, c_low], 1)
    for t in range(0, lanes, lead):
        at = slice(t, t + lead)
        one = turns[1, at, :lanes], turns[1, at, lanes:]
        powers = [(jnp.ones((lead, lanes), exact), jnp.zeros((lead, lanes), exact)), one]
        for r in range(2, rows):
            powers.append(turned(*powers[r // 2], *powers[r - r // 2]))
        for r in range(rows):
            big_turn[r, at, :lanes] = powers[r][0]
            big_turn[r, at, lanes:] = powers[r][1]
    w = turns[0, :, :lanes], turns[0, :, lanes:]
    at = [me ^ j for j in early]
    for k, x in enumerate(row_spectra(blocks, at, sign_table(dft), left, w, big_turn)):
        found[k, 0], found[k, 1] = x


def inverse_kernel(rows, *refs):
    blocks = refs[:rows]
    found, left, dft, turns, big_turn, spectrum, precond, circulant, kernel, symbol, ends, work = refs[rows:]
    half, early = rows // 2, early_slots(rows)
    depth = lanes // rows
    samples = rows * lanes * lanes
    me = lax.axis_index("seq")
    w = turns[0, :, :lanes], turns[0, :, lanes:]
    for k, j in enumerate(early):
        work[me ^ j, 0, 0], work[me ^ j, 0, 1] = found[k, 0], found[k, 1]
    late = [j for j in range(rows) if j not in early]
    at = [me ^ j for j in late]
    for r, x in zip(at, row_spectra([blocks[j] for j in late], at, sign_table(dft), left, w, big_turn)):
        work[r, 0, 0], work[r, 0, 1] = x
    own = pl.ds(pl.multiple_of(me * depth, depth), depth)
    for a, x in enumerate(small_dft([(work[r, 0, 0, own], work[r, 0, 1, own]) for r in range(rows)], -1)):
        spectrum[a, 0], spectrum[a, 1] = x
    for j in range(rows):
        place = pl.multiple_of((me ^ j) * depth, depth)
        for a in range(half):
            at = lanes + a * depth
            kernel[a, pl.ds(place, depth)] = blocks[j][at : at + depth]
            at += half * depth
            symbol[a, pl.ds(place, depth)] = blocks[j][at : at + depth]
        ends[me ^ j] = blocks[j][lanes + 2 * half * depth : lanes + 2 * half * depth + lead]
    middle = sum((-1.0) ** r * work[r, 0, 0, 0:1, 0:1] for r in range(rows))
    middle = middle / ends[0, 1:2, 0:1] / samples
    middle_image = middle * ends[0, 0:1, 0:1]
    for t in range(0, lanes, lead):
        at = slice(t, t + lead)
        lower = small_dft([(work[r, 0, 0, at], work[r, 0, 1, at]) for r in range(rows)], -1)[:half]
        first, second = [], []
        for a in range(half):
            scale = 2.0 / samples / symbol[a, at]
            if a == 0 and t == 0:
                zero = (lax.broadcasted_iota(jnp.int32, (lead, lanes), 0) == 0) & (
                    lax.broadcasted_iota(jnp.int32, (lead, lanes), 1) == 0
                )
                scale = jnp.where(zero, 0.5 * scale, scale)
            re, im = lower[a][0] * scale, lower[a][1] * scale
            first.append((re, im))
            second.append((re * kernel[a, at], im * kernel[a, at]))
        for field, entries in enumerate((first, second)):
            out = half_dft(entries, 1)
            for r in range(rows):
                re, im = turned_back(*out[r], big_turn[r, at, :lanes], big_turn[r, at, lanes:])
                work[r, field, 0, at] = re
                work[r, field, 1, at] = im
    c_high, s_high, c_low, s_low = (dft[k] for k in range(4))
    back_right = jnp.concatenate([jnp.concatenate([c_high, s_high], 0), jnp.concatenate([c_low, s_low], 0)], 1)
    highs, lows = [], []
    for r in range(rows):
        columns = [stacked(work[r, field, 1], work[r, field, 0], 0) for field in range(2)]
        done = left_product(left, columns)
        for field in range(2):
            at = slice(field * lanes, (field + 1) * lanes)
            high, low = stacked(*turned_back(done[lanes:, at], done[:lanes, at], *w), 1)
            highs.append(high)
            lows.append(low)
    both = times(jnp.concatenate(highs, 0), back_right)
    done = both[:, :lanes] + both[:, lanes:] + times(jnp.concatenate(lows, 0), back_right[:, :lanes])
    for r in range(rows):
        sign = 1.0 if r % 2 == 0 else -1.0
        precond[r] = done[2 * r * lanes : (2 * r + 1) * lanes] + sign * middle
        circulant[r] = done[(2 * r + 1) * lanes : (2 * r + 2) * lanes] + sign * middle_image


def whole_sum(x):
    return jnp.sum(jnp.sum(x, axis=0, keepdims=True), axis=1, keepdims=True)


def folded(x):
    return sum(x[t : t + lead] for t in range(0, x.shape[0], lead))


def own_spectra(fields, at, left, dft, turns, big_turn):
    rows = big_turn.shape[0]
    depth = lanes // rows
    own = pl.multiple_of(lax.axis_index("seq") * depth, depth)
    c_high, s_high, c_low, s_low = (dft[k] for k in range(4))
    wide_high, wide_low = jnp.concatenate([c_high, s_high], 1), jnp.concatenate([c_low, s_low], 1)
    twice_high = jnp.concatenate([wide_high, wide_high], 0)
    w = turns[0, :, :lanes], turns[0, :, lanes:]
    parts = [left[pl.ds(pl.multiple_of(k * lanes + own, depth), depth)] for k in range(4)]
    block = jnp.concatenate(parts, 0)
    highs, lows = zip(*(split(x) for x in fields))
    highs, lows = jnp.concatenate(highs, 0), jnp.concatenate(lows, 0)
    section = times(jnp.concatenate([highs, lows], 1), twice_high) + times(highs, wide_low)
    out = []
    for j in range(0, len(fields), 2):
        columns = []
        for i in (j, j + 1):
            here = slice(i * lanes, (i + 1) * lanes)
            columns.append(stacked(*turned(section[here, :lanes], section[here, lanes:], *w), 0))
        done = left_product(block, columns)
        for i in range(2):
            here, r = slice(i * lanes, (i + 1) * lanes), at[j + i]
            gc, gs = big_turn[r, pl.ds(own, depth), :lanes], big_turn[r, pl.ds(own, depth), lanes:]
            out.append(turned(done[:depth, here], done[depth:, here], gc, gs))
    return out


def whole_noise(target, held, other):
    share = lanes // 2
    side = lax.rem(lax.axis_index("probe"), 2) * share
    target[pl.ds(pl.multiple_of(side, share), share)] = held[held.shape[0] - share :]
    target[pl.ds(pl.multiple_of(share - side, share), share)] = other[...]


def images(slots, signs, noises, precond, circulant, image, sums):
    me = lax.axis_index("seq")
    fields = []
    numerator, curvature = sums
    for k, j in enumerate(slots):
        p = precond[me ^ j]
        noisy = noises[k][...] * p
        ki = circulant[me ^ j] + noisy
        image[k] = ki
        fields.append(noisy)
        numerator += folded(signs[k][:lanes] * p)
        curvature += folded(p * ki)
    return fields, (numerator, curvature)


def near_kernel(rows, *refs):
    n = rows - 2
    blocks, others = refs[:n], refs[n : n + 2]
    precond, circulant, left, dft, turns, big_turn, image, noise, found, sums = refs[n + 2 :]
    share = lanes // 2
    for j in range(2):
        noise[j] = blocks[j][blocks[j].shape[0] - lanes :]
    for j in range(2, n):
        whole_noise(noise.at[j], blocks[j], others[j % 2].at[(j - 2) // 2 * share : j // 2 * share])
    zero = jnp.zeros((lead, lanes), exact)
    noises = [noise.at[j] for j in range(n)]
    fields, totals = images(range(n), blocks, noises, precond, circulant, image, (zero, zero))
    sums[0], sums[1] = totals
    at = [lax.axis_index("seq") ^ j for j in range(n)]
    for j, x in enumerate(own_spectra(fields, at, left, dft, turns, big_turn)):
        found[j, 0], found[j, 1] = x


def adjoint_kernel(rows, probes, *refs):
    n = rows - 2
    signs = [refs[j].at[:lanes] for j in range(rows)]
    blocks, others = refs[:rows], refs[rows : rows + 2]
    near_image, near_noise, near_found, near_sums = refs[rows + 2 : rows + 6]
    refs = refs[rows + 6 :]
    precond, circulant, spectrum, kernel, symbol, left, dft, turns, big_turn, residual_out = refs[:10]
    outs = refs[10 : 10 + probes]
    image, noise, work, shares = refs[10 + probes :]
    depth = lanes // rows
    samples = rows * lanes * lanes
    me = lax.axis_index("seq")
    own = pl.multiple_of(me * depth, depth)
    at = [me ^ j for j in range(rows)]
    for j in range(n):
        work[at[j], 0, 0], work[at[j], 0, 1] = near_found[j, 0], near_found[j, 1]
    for k in range(2):
        whole_noise(noise.at[k], others[k].at[: lanes // 2], others[k].at[lanes // 2 :])
    last_noises = [noise.at[k] for k in range(2)]
    sums = (near_sums[0], near_sums[1])
    fields, sums = images(range(n, rows), blocks[n:], last_noises, precond, circulant, image, sums)
    noises = [near_noise.at[j] for j in range(n)] + last_noises
    image = [near_image.at[j] for j in range(n)] + [image.at[k] for k in range(2)]
    numerator, curvature = whole_sum(sums[0]), whole_sum(sums[1])
    for j, x in zip(range(n, rows), own_spectra(fields, at[n:], left, dft, turns, big_turn)):
        work[at[j], 0, 0], work[at[j], 0, 1] = x
    step_size = numerator / curvature
    cross = jnp.zeros((lead, lanes), exact)
    fields = []
    for j in range(rows):
        residual = signs[j][...] - step_size * image[j][...]
        cross += folded(residual * image[j][...])
        fields.append(noises[j][...] * residual)
        if j == 0:
            residual_out[...] = residual.T
    weight = -2.0 * whole_sum(cross)
    for r, x in zip(at, own_spectra(fields, at, left, dft, turns, big_turn)):
        work[r, 1, 0], work[r, 1, 1] = x
    noisy = small_dft([(work[r, 0, 0], work[r, 0, 1]) for r in range(rows)], -1)
    noisy_residual = small_dft([(work[r, 1, 0], work[r, 1, 1]) for r in range(rows)], -1)
    for a in range(rows):
        k, s = kernel[:, a], symbol[:, a]
        total = 0.0
        for part in range(2):
            base = spectrum[a, part]
            ki = k * (base / s) + noisy[a][part]
            applied = k * (base - step_size * ki) + noisy_residual[a][part]
            adjoint = (
                (weight / curvature) * base
                - (2.0 * weight * step_size / curvature) * ki
                - (2.0 * step_size) * applied
            )
            total += adjoint * base
        shares[a] = -total / (samples * s * s)
    width = rows // probes
    column = lax.axis_index("probe")
    for d in range(probes):
        for k in range(width):
            outs[d][:, k] = shares[(column ^ d) * width + k]


def call(kernel, outs, scratch, *operands):
    whole = pl.BlockSpec(memory_space=pltpu.VMEM)
    typed = [out if isinstance(out[0], tuple) else (out, exact) for out in outs]
    shapes = tuple(pltpu.VMEM(shape, dtype) for shape, dtype in typed)
    return pl.pallas_call(
        kernel,
        out_shape=shapes,
        in_specs=[whole] * len(operands),
        out_specs=(whole,) * len(shapes),
        scratch_shapes=[pltpu.VMEM(shape, exact) for shape in scratch],
        compiler_params=pltpu.CompilerParams(vmem_limit_bytes=24 << 20),
        cost_estimate=pl.CostEstimate(flops=0, bytes_accessed=0, transcendentals=0),
    )(*operands)


def swapped(x, axis, d):
    return lax.ppermute(x, axis, [(i, i ^ d) for i in range(lax.axis_size(axis))])


def after(x, *earlier):
    return lax.optimization_barrier((x, *earlier))[0]


def after(x, *earlier):
    return lax.optimization_barrier((x, *earlier))[0]


def other_core(x):
    return swapped(x, "seq", 1)


def across_x(x):
    return swapped(x, "probe", 1)


def next_chip(x):
    return swapped(x, "seq", 2)


def beyond_middle(x):
    return swapped(x, "seq", 4)


def adjoint_calls(
    rows, probes, blocks, noises, precond, circulant, spectrum, kernel, symbols, left, dft, turns, big_turn
):
    square = (lanes, lanes)
    depth, width, n = lanes // rows, rows // probes, rows - 2
    tables_held = (left, dft, turns, big_turn)
    near_parts = call(
        functools.partial(near_kernel, rows),
        [(n, *square), (n, *square), (n, 2, depth, lanes), (2, lead, lanes)],
        [],
        *blocks[:n],
        *noises[:2],
        precond,
        circulant,
        *tables_held,
    )
    return call(
        functools.partial(adjoint_kernel, rows, probes),
        [square] + [(depth, width, lanes)] * probes,
        [(2, *square), (2, *square), (rows, 2, 2, depth, lanes), (rows, depth, lanes)],
        *blocks,
        *noises[2:],
        *near_parts,
        precond,
        circulant,
        spectrum,
        kernel,
        symbols,
        *tables_held,
    )


def gathered_shards(probe_bits, noise_var, kernel_spectrum, symbol, grad_prev):
    rows = kernel_spectrum.shape[1]
    probes = lax.axis_size("probe")
    half, depth, width = rows // 2, lanes // rows, rows // probes
    kernel = kernel_spectrum.T.reshape(rows, depth, lanes).transpose(1, 0, 2)
    symbols = symbol.T.reshape(rows, depth, lanes).transpose(1, 0, 2)
    before = grad_prev.T.reshape(width, depth, lanes).transpose(1, 0, 2)
    square = (lanes, lanes)
    dft, turns = tables(rows)
    first = lanes + 2 * half * depth + lead
    block, sent, dft, turns = pl.pallas_call(
        functools.partial(pack_kernel, half, first),
        out_shape=(
            pltpu.VMEM((first + lanes, lanes), exact),
            pltpu.VMEM((first + lanes // 2, lanes), exact),
            pltpu.VMEM(dft.shape, near),
            pltpu.VMEM(turns.shape, exact),
        ),
        in_specs=[pl.BlockSpec(memory_space=pl.ANY)] * 6,
        out_specs=(pl.BlockSpec(memory_space=pltpu.VMEM),) * 4,
        scratch_shapes=[
            pltpu.VMEM(square, jnp.int32),
            pltpu.VMEM(square, exact),
            pltpu.VMEM(kernel.shape, exact),
            pltpu.VMEM(kernel.shape, exact),
            pltpu.SemaphoreType.DMA((6,)),
        ],
    )(probe_bits.reshape(square), noise_var.reshape(square), kernel, symbols, dft, turns)
    far = beyond_middle(sent)
    neighbour = next_chip(sent)
    passed_on = next_chip(far[:first])
    early = [block, other_core(block), neighbour, far]
    found, left, big_turn = call(
        functools.partial(early_kernel, rows),
        [(len(early), 2, *square), ((4 * lanes, 2 * lanes), near), (rows, lanes, 2 * lanes)],
        [],
        *early,
        dft,
        turns,
    )
    halves = across_x(jnp.concatenate([neighbour[first:], far[first:]], 0))
    blocks = early[:2]
    for x, earlier in ((neighbour, found), (far, found), (passed_on, halves)):
        blocks += [x, other_core(after(x, earlier))]
    field = (rows, *square)
    spectrum, precond, circulant = call(
        functools.partial(inverse_kernel, rows),
        [(rows, 2, depth, lanes), field, field],
        [(half, *square), (half, *square), (rows, lead, lanes), (rows, 2, 2, *square)],
        *blocks,
        found,
        left,
        dft,
        turns,
        big_turn,
    )
    passed_noise = next_chip(jnp.concatenate([far[first:], halves[lanes // 2 :]], 0))
    last = after(passed_noise, precond)
    noises = [halves, other_core(halves), last, other_core(last)]
    residual, *parts = adjoint_calls(
        rows, probes, blocks, noises, precond, circulant, spectrum, kernel, symbols, left, dft, turns, big_turn
    )
    arrived = [swapped(parts[d], "probe", d) for d in range(1, probes)]
    total = lax.optimization_barrier(parts[0] + arrived.pop())
    total = before + sum(arrived, total) / probes
    total = total.transpose(1, 0, 2).reshape(width, depth * lanes).T
    return residual.reshape(probe_bits.shape), total


highest = lax.Precision.HIGHEST
minor_width = 128


def dft_table(height, breadth, modulus, orient):
    left_index = jnp.arange(height, dtype=jnp.int32)[:, None]
    right_index = jnp.arange(breadth, dtype=jnp.int32)[None, :]
    phases = (
        orient * 2.0 * math.pi / modulus * (left_index * right_index % modulus).astype(jnp.float32)
    )
    return (jnp.cos(phases), jnp.sin(phases))


def complex_product(pattern, real_part, imaginary, cosine_table, sine_table):
    real_cos = jnp.einsum(pattern, real_part, cosine_table, precision=highest)
    real_sin = jnp.einsum(pattern, real_part, sine_table, precision=highest)
    if imaginary is None:
        return (real_cos, real_sin)
    imag_cos = jnp.einsum(pattern, imaginary, cosine_table, precision=highest)
    imag_sin = jnp.einsum(pattern, imaginary, sine_table, precision=highest)
    return (real_cos - imag_sin, real_sin + imag_cos)


def rotate(real_part, imaginary, cosine_table, sine_table):
    return (
        real_part * cosine_table - imaginary * sine_table,
        real_part * sine_table + imaginary * cosine_table,
    )


def forward_rows(series):
    major_len = series.shape[-2]
    length = major_len * minor_width
    cosine_table, sine_table = dft_table(major_len, major_len, major_len, -1.0)
    section_real, section_imag = complex_product(
        "...mi,mk->...ik", series, None, cosine_table, sine_table
    )
    turn_cos, turn_sin = dft_table(minor_width, major_len, length, -1.0)
    twisted_real, twisted_imag = rotate(section_real, section_imag, turn_cos, turn_sin)
    cosine_table, sine_table = dft_table(minor_width, minor_width, minor_width, -1.0)
    return complex_product("...ik,ij->...jk", twisted_real, twisted_imag, cosine_table, sine_table)


def inverse_rows(real_part, imaginary):
    major_len = real_part.shape[-1]
    length = major_len * minor_width
    cosine_table, sine_table = dft_table(minor_width, minor_width, minor_width, 1.0)
    section_real, section_imag = complex_product(
        "...jk,ji->...ik", real_part, imaginary, cosine_table, sine_table
    )
    turn_cos, turn_sin = dft_table(minor_width, major_len, length, 1.0)
    twisted_real, twisted_imag = rotate(section_real, section_imag, turn_cos, turn_sin)
    cosine_table, sine_table = dft_table(major_len, major_len, major_len, 1.0)
    final_real, unused = complex_product(
        "...ik,km->...mi", twisted_real, twisted_imag, cosine_table, sine_table
    )
    return final_real


def global_twiddle(local_rows, major_len, samples, orient):
    row_index = lax.axis_index("seq") * local_rows + jnp.arange(local_rows, dtype=jnp.int32)
    column_index = (
        jnp.arange(minor_width, dtype=jnp.int32)[:, None] * major_len
        + jnp.arange(major_len, dtype=jnp.int32)[None, :]
    )
    phases = (
        orient
        * 2.0
        * math.pi
        / samples
        * (row_index[:, None, None] * column_index[None, :, :] % samples).astype(jnp.float32)
    )
    return (jnp.cos(phases), jnp.sin(phases))


def forward_spectrum(series):
    local_rows = series.shape[1]
    major_len = series.shape[2]
    devices = lax.axis_size("seq")
    all_rows = local_rows * devices
    samples = all_rows * major_len * minor_width
    real_part, imaginary = forward_rows(series)
    turn_cos, turn_sin = global_twiddle(local_rows, major_len, samples, -1.0)
    turned_real, turned_imag = rotate(real_part, imaginary, turn_cos, turn_sin)
    arrived = lax.all_to_all(
        jnp.stack([turned_real, turned_imag]), "seq", split_axis=3, concat_axis=2, tiled=True
    )
    block = minor_width // devices * major_len
    arrived = arrived.reshape(arrived.shape[0], arrived.shape[1], all_rows, block)
    cosine_table, sine_table = dft_table(all_rows, all_rows, all_rows, -1.0)
    return complex_product("zrb,ra->zba", arrived[0], arrived[1], cosine_table, sine_table)


def inverse_field(spectrum_real, spectrum_imag):
    all_rows = spectrum_real.shape[2]
    block = spectrum_real.shape[1]
    devices = lax.axis_size("seq")
    major_len = block * devices // minor_width
    cosine_table, sine_table = dft_table(all_rows, all_rows, all_rows, 1.0)
    back_real, back_imag = complex_product(
        "zba,ar->zrb", spectrum_real, spectrum_imag, cosine_table, sine_table
    )
    stacked = jnp.stack([back_real, back_imag])
    stacked = stacked.reshape(
        stacked.shape[0], stacked.shape[1], all_rows, minor_width // devices, major_len
    )
    arrived = lax.all_to_all(stacked, "seq", split_axis=2, concat_axis=3, tiled=True)
    local_rows = arrived.shape[2]
    samples = all_rows * major_len * minor_width
    turn_cos, turn_sin = global_twiddle(local_rows, major_len, samples, 1.0)
    turned_real, turned_imag = rotate(arrived[0], arrived[1], turn_cos, turn_sin)
    return inverse_rows(turned_real, turned_imag) / samples


def shards(probe_bits, noise_var, kernel_spectrum, symbol, grad_prev):
    field_shape = (
        probe_bits.shape[0],
        probe_bits.shape[1],
        probe_bits.shape[2] // minor_width,
        minor_width,
    )
    sign_field = (2 * probe_bits - 1).astype(jnp.float32).reshape(field_shape)
    noise_field = noise_var.reshape(field_shape[1:])
    samples = kernel_spectrum.shape[1] * noise_var.shape[1]
    base_real, base_imag = forward_spectrum(sign_field)
    scaled_real = base_real / symbol
    scaled_imag = base_imag / symbol
    precond = inverse_field(scaled_real, scaled_imag)
    again_real, again_imag = forward_spectrum(precond)
    circulant = inverse_field(kernel_spectrum * again_real, kernel_spectrum * again_imag)
    kernel_image = circulant + noise_field * precond
    numerator, curvature = lax.psum(
        (jnp.sum(sign_field * precond), jnp.sum(precond * kernel_image)), "seq"
    )
    step_size = numerator / curvature
    residual = sign_field - step_size * kernel_image
    cross_term = lax.psum(jnp.sum(residual * kernel_image), "seq")
    weight = -2.0 * cross_term
    resid_real, resid_imag = forward_spectrum(residual)
    applied = (
        inverse_field(kernel_spectrum * resid_real, kernel_spectrum * resid_imag)
        + noise_field * residual
    )
    adjoint = (
        weight / curvature * sign_field
        - 2.0 * weight * step_size / curvature * kernel_image
        - 2.0 * step_size * applied
    )
    adjoint_real, adjoint_imag = forward_spectrum(adjoint)
    local_grad = -(adjoint_real[0] * base_real[0] + adjoint_imag[0] * base_imag[0]) / (
        samples * symbol * symbol
    )
    probes = lax.axis_size("probe")
    summed = lax.psum(local_grad, "probe")
    share_width = summed.shape[1] // probes
    own_share = lax.dynamic_slice_in_dim(
        summed, lax.axis_index("probe") * share_width, share_width, 1
    )
    grad_total = grad_prev + own_share / probes
    return (residual.reshape(probe_bits.shape), grad_total)


def fits(mesh, cols, rows):
    seq, probe = mesh.shape["seq"], mesh.shape["probe"]
    powers = all(n & (n - 1) == 0 for n in (rows, seq, probe))
    return powers and rows == seq == lead and rows % probe == 0 and probe > 1 and cols == lanes * lanes


def solution(mesh):
    placed = (
        P("probe", "seq", None),
        P("seq", None),
        P("seq", None),
        P("seq", None),
        P("seq", "probe"),
    )

    def whole(probe_bits, noise_var, kernel_spectrum, symbol, grad_prev):
        small = fits(mesh, *symbol.shape)
        return jax.shard_map(
            gathered_shards if small else shards,
            mesh=mesh,
            in_specs=placed,
            out_specs=(P("probe", "seq", None), P("seq", "probe")),
            check_vma=False,
        )(probe_bits, noise_var, kernel_spectrum, symbol, grad_prev)

    return whole
```

```python
import functools
import math

import jax
import jax.numpy as jnp
import numpy as np
from jax import lax
from jax.experimental import pallas as pl
from jax.experimental.pallas import tpu as pltpu
from jax.sharding import PartitionSpec as P

lanes = 128
lead = 8
near = jnp.bfloat16
exact = jnp.float32


def split_table(table):
    high = table.astype(near)
    low = (table - high.astype(np.float64)).astype(near)
    return high, low


def angle_parts(phase):
    return np.cos(phase), np.sin(phase)


@functools.cache
def tables(rows):
    index = np.arange(lanes, dtype=np.float64)
    turn = -2.0 * np.pi
    c, s = angle_parts(turn * (np.outer(index, index) % lanes) / lanes)
    c_high, c_low = split_table(c)
    s_high, s_low = split_table(s)
    row_len = lanes * lanes
    wc, ws = angle_parts(turn * np.outer(index, index) / row_len)
    flat = index[:, None] * lanes + index[None, :]
    gc, gs = angle_parts(turn * flat / (rows * row_len))
    turns = np.stack([np.concatenate([wc, ws], 1), np.concatenate([gc, gs], 1)])
    return np.stack([c_high, s_high, c_low, s_low]), turns.astype(np.float32)


def split(x):
    high = x.astype(near)
    return high, (x - high.astype(exact)).astype(near)


def stacked(first, second, axis):
    fh, fl = split(first)
    sh, sl = split(second)
    return jnp.concatenate([fh, sh], axis), jnp.concatenate([fl, sl], axis)


def times(left, right):
    return jnp.dot(left, right, preferred_element_type=exact)


def left_product(table, columns):
    n = table.shape[0] // 2
    high = jnp.concatenate([column[0] for column in columns], 1)
    low = jnp.concatenate([column[1] for column in columns], 1)
    both = times(table[...], high)
    return both[:n] + both[n:] + times(table[:n], low)


def turned(re, im, cos, sin):
    return re * cos - im * sin, re * sin + im * cos


def turned_back(re, im, cos, sin):
    return re * cos + im * sin, im * cos - re * sin


def add(x, y):
    return x[0] + y[0], x[1] + y[1]


def sub(x, y):
    return x[0] - y[0], x[1] - y[1]


def unit_turn(x, k, n, orient):
    k = (k * orient) % n
    if k == 0:
        return x
    if 4 * k == n:
        return -x[1], x[0]
    if 2 * k == n:
        return -x[0], -x[1]
    if 4 * k == 3 * n:
        return x[1], -x[0]
    cos, sin = math.cos(2 * math.pi * k / n), math.sin(2 * math.pi * k / n)
    return x[0] * cos - x[1] * sin, x[0] * sin + x[1] * cos


def small_dft(xs, orient):
    n = len(xs)
    if n == 1:
        return xs
    even, odd = small_dft(xs[0::2], orient), small_dft(xs[1::2], orient)
    odd = [unit_turn(x, k, n, orient) for k, x in enumerate(odd)]
    return [add(e, o) for e, o in zip(even, odd)] + [sub(e, o) for e, o in zip(even, odd)]


def half_dft(xs, orient):
    n = 2 * len(xs)
    even = small_dft(xs, orient)
    odd = small_dft([unit_turn(x, k, n, orient) for k, x in enumerate(xs)], orient)
    return [(odd if r % 2 else even)[r // 2] for r in range(n)]


def pack_kernel(half, first, *refs):
    sources, out, sent, held, landed, done = refs[:6], refs[6], refs[7], refs[8:10], refs[10:14], refs[14]
    targets = (*landed, *held)
    copies = [pltpu.make_async_copy(sources[i], targets[i], done.at[i]) for i in range(6)]
    for copy in copies:
        copy.start()
    bits, noise, kernel, symbol = landed
    copies[0].wait()
    out[:lanes] = (2 * bits[...] - 1).astype(exact).T
    copies[1].wait()
    out[first:] = noise[...].T
    copies[2].wait()
    copies[3].wait()
    depth = kernel.shape[0]
    for a in range(half):
        at = lanes + a * depth
        out[at : at + depth] = kernel[:, a]
        at += half * depth
        out[at : at + depth] = symbol[:, a]
    middle = jnp.concatenate([kernel[0, half : half + 1], symbol[0, half : half + 1]], 0)
    out[first - lead : first] = jnp.concatenate([middle] * (lead // 2), 0)
    sent[:first] = out[:first]
    share = lanes // 2
    side = lax.rem(lax.axis_index("probe"), 2)
    sent[first:] = out[pl.ds(pl.multiple_of(first + side * share, lead), share)]
    copies[4].wait()
    copies[5].wait()


def row_spectra(signs, rows, sign_right, left, w, big_turn):
    lined = [jnp.concatenate([x[:lanes].astype(near)] * 2, 1) for x in signs]
    section = times(jnp.concatenate(lined, 0), sign_right)
    out = []
    for j in range(0, len(signs), 2):
        columns = []
        for k in (j, j + 1):
            at = slice(k * lanes, (k + 1) * lanes)
            columns.append(stacked(*turned(section[at, :lanes], section[at, lanes:], *w), 0))
        done = left_product(left, columns)
        for k in range(2):
            at, r = slice(k * lanes, (k + 1) * lanes), rows[j + k]
            out.append(turned(done[:lanes, at], done[lanes:, at], big_turn[r, :, :lanes], big_turn[r, :, lanes:]))
    return out


def sign_table(dft):
    c_high, s_high, c_low, s_low = (dft[k] for k in range(4))
    return jnp.concatenate([jnp.concatenate([c_high, s_high], 1), jnp.concatenate([c_low, s_low], 1)], 0)


def early_slots(rows):
    return [0, 1, *range(2, rows - 2, 2)]


def early_kernel(rows, *refs):
    early = early_slots(rows)
    blocks = refs[: len(early)]
    dft, turns, found, left, big_turn = refs[len(early) :]
    me = lax.axis_index("seq")
    c_high, s_high, c_low, s_low = (dft[k] for k in range(4))
    left[:lanes] = jnp.concatenate([c_high, -s_high], 1)
    left[lanes : 2 * lanes] = jnp.concatenate([s_high, c_high], 1)
    left[2 * lanes : 3 * lanes] = jnp.concatenate([c_low, -s_low], 1)
    left[3 * lanes :] = jnp.concatenate([s_low, c_low], 1)
    for t in range(0, lanes, lead):
        at = slice(t, t + lead)
        one = turns[1, at, :lanes], turns[1, at, lanes:]
        powers = [(jnp.ones((lead, lanes), exact), jnp.zeros((lead, lanes), exact)), one]
        for r in range(2, rows):
            powers.append(turned(*powers[r // 2], *powers[r - r // 2]))
        for r in range(rows):
            big_turn[r, at, :lanes] = powers[r][0]
            big_turn[r, at, lanes:] = powers[r][1]
    w = turns[0, :, :lanes], turns[0, :, lanes:]
    at = [me ^ j for j in early]
    for k, x in enumerate(row_spectra(blocks, at, sign_table(dft), left, w, big_turn)):
        found[k, 0], found[k, 1] = x


def inverse_kernel(rows, *refs):
    blocks = refs[:rows]
    found, left, dft, turns, big_turn, spectrum, precond, circulant, kernel, symbol, ends, work = refs[rows:]
    half, early = rows // 2, early_slots(rows)
    depth = lanes // rows
    samples = rows * lanes * lanes
    me = lax.axis_index("seq")
    w = turns[0, :, :lanes], turns[0, :, lanes:]
    for k, j in enumerate(early):
        work[me ^ j, 0, 0], work[me ^ j, 0, 1] = found[k, 0], found[k, 1]
    late = [j for j in range(rows) if j not in early]
    at = [me ^ j for j in late]
    for r, x in zip(at, row_spectra([blocks[j] for j in late], at, sign_table(dft), left, w, big_turn)):
        work[r, 0, 0], work[r, 0, 1] = x
    own = pl.ds(pl.multiple_of(me * depth, depth), depth)
    for a, x in enumerate(small_dft([(work[r, 0, 0, own], work[r, 0, 1, own]) for r in range(rows)], -1)):
        spectrum[a, 0], spectrum[a, 1] = x
    for j in range(rows):
        place = pl.multiple_of((me ^ j) * depth, depth)
        for a in range(half):
            at = lanes + a * depth
            kernel[a, pl.ds(place, depth)] = blocks[j][at : at + depth]
            at += half * depth
            symbol[a, pl.ds(place, depth)] = blocks[j][at : at + depth]
        ends[me ^ j] = blocks[j][lanes + 2 * half * depth : lanes + 2 * half * depth + lead]
    middle = sum((-1.0) ** r * work[r, 0, 0, 0:1, 0:1] for r in range(rows))
    middle = middle / ends[0, 1:2, 0:1] / samples
    middle_image = middle * ends[0, 0:1, 0:1]
    for t in range(0, lanes, lead):
        at = slice(t, t + lead)
        lower = small_dft([(work[r, 0, 0, at], work[r, 0, 1, at]) for r in range(rows)], -1)[:half]
        first, second = [], []
        for a in range(half):
            scale = 2.0 / samples / symbol[a, at]
            if a == 0 and t == 0:
                zero = (lax.broadcasted_iota(jnp.int32, (lead, lanes), 0) == 0) & (
                    lax.broadcasted_iota(jnp.int32, (lead, lanes), 1) == 0
                )
                scale = jnp.where(zero, 0.5 * scale, scale)
            re, im = lower[a][0] * scale, lower[a][1] * scale
            first.append((re, im))
            second.append((re * kernel[a, at], im * kernel[a, at]))
        for field, entries in enumerate((first, second)):
            out = half_dft(entries, 1)
            for r in range(rows):
                re, im = turned_back(*out[r], big_turn[r, at, :lanes], big_turn[r, at, lanes:])
                work[r, field, 0, at] = re
                work[r, field, 1, at] = im
    c_high, s_high, c_low, s_low = (dft[k] for k in range(4))
    back_right = jnp.concatenate([jnp.concatenate([c_high, s_high], 0), jnp.concatenate([c_low, s_low], 0)], 1)
    highs, lows = [], []
    for r in range(rows):
        columns = [stacked(work[r, field, 1], work[r, field, 0], 0) for field in range(2)]
        done = left_product(left, columns)
        for field in range(2):
            at = slice(field * lanes, (field + 1) * lanes)
            high, low = stacked(*turned_back(done[lanes:, at], done[:lanes, at], *w), 1)
            highs.append(high)
            lows.append(low)
    both = times(jnp.concatenate(highs, 0), back_right)
    done = both[:, :lanes] + both[:, lanes:] + times(jnp.concatenate(lows, 0), back_right[:, :lanes])
    for r in range(rows):
        sign = 1.0 if r % 2 == 0 else -1.0
        precond[r] = done[2 * r * lanes : (2 * r + 1) * lanes] + sign * middle
        circulant[r] = done[(2 * r + 1) * lanes : (2 * r + 2) * lanes] + sign * middle_image


def whole_sum(x):
    return jnp.sum(jnp.sum(x, axis=0, keepdims=True), axis=1, keepdims=True)


def folded(x):
    return sum(x[t : t + lead] for t in range(0, x.shape[0], lead))


def own_spectra(fields, at, left, dft, turns, big_turn):
    rows = big_turn.shape[0]
    depth = lanes // rows
    own = pl.multiple_of(lax.axis_index("seq") * depth, depth)
    c_high, s_high, c_low, s_low = (dft[k] for k in range(4))
    wide_high, wide_low = jnp.concatenate([c_high, s_high], 1), jnp.concatenate([c_low, s_low], 1)
    twice_high = jnp.concatenate([wide_high, wide_high], 0)
    w = turns[0, :, :lanes], turns[0, :, lanes:]
    parts = [left[pl.ds(pl.multiple_of(k * lanes + own, depth), depth)] for k in range(4)]
    block = jnp.concatenate(parts, 0)
    highs, lows = zip(*(split(x) for x in fields))
    highs, lows = jnp.concatenate(highs, 0), jnp.concatenate(lows, 0)
    section = times(jnp.concatenate([highs, lows], 1), twice_high) + times(highs, wide_low)
    out = []
    for j in range(0, len(fields), 2):
        columns = []
        for i in (j, j + 1):
            here = slice(i * lanes, (i + 1) * lanes)
            columns.append(stacked(*turned(section[here, :lanes], section[here, lanes:], *w), 0))
        done = left_product(block, columns)
        for i in range(2):
            here, r = slice(i * lanes, (i + 1) * lanes), at[j + i]
            gc, gs = big_turn[r, pl.ds(own, depth), :lanes], big_turn[r, pl.ds(own, depth), lanes:]
            out.append(turned(done[:depth, here], done[depth:, here], gc, gs))
    return out


def whole_noise(target, held, other):
    share = lanes // 2
    side = lax.rem(lax.axis_index("probe"), 2) * share
    target[pl.ds(pl.multiple_of(side, share), share)] = held[held.shape[0] - share :]
    target[pl.ds(pl.multiple_of(share - side, share), share)] = other[...]


def images(slots, signs, noises, precond, circulant, image, sums):
    me = lax.axis_index("seq")
    fields = []
    numerator, curvature = sums
    for k, j in enumerate(slots):
        p = precond[me ^ j]
        noisy = noises[k][...] * p
        ki = circulant[me ^ j] + noisy
        image[k] = ki
        fields.append(noisy)
        numerator += folded(signs[k][:lanes] * p)
        curvature += folded(p * ki)
    return fields, (numerator, curvature)


def near_kernel(rows, *refs):
    n = rows - 2
    blocks, others = refs[:n], refs[n : n + 2]
    precond, circulant, left, dft, turns, big_turn, image, noise, found, sums = refs[n + 2 :]
    share = lanes // 2
    for j in range(2):
        noise[j] = blocks[j][blocks[j].shape[0] - lanes :]
    for j in range(2, n):
        whole_noise(noise.at[j], blocks[j], others[j % 2].at[(j - 2) // 2 * share : j // 2 * share])
    zero = jnp.zeros((lead, lanes), exact)
    noises = [noise.at[j] for j in range(n)]
    fields, totals = images(range(n), blocks, noises, precond, circulant, image, (zero, zero))
    sums[0], sums[1] = totals
    at = [lax.axis_index("seq") ^ j for j in range(n)]
    fields += [noises[j][...] * blocks[j][:lanes] for j in range(2)] + [noises[j][...] * image[j] for j in range(2)]
    for j, x in enumerate(own_spectra(fields, at + at[:2] * 2, left, dft, turns, big_turn)):
        found[j, 0], found[j, 1] = x


def adjoint_kernel(rows, probes, *refs):
    n = rows - 2
    signs = [refs[j].at[:lanes] for j in range(rows)]
    blocks, others = refs[:rows], refs[rows : rows + 2]
    near_image, near_noise, near_found, near_sums = refs[rows + 2 : rows + 6]
    refs = refs[rows + 6 :]
    precond, circulant, spectrum, kernel, symbol, left, dft, turns, big_turn, residual_out = refs[:10]
    outs = refs[10 : 10 + probes]
    image, noise, work, shares = refs[10 + probes :]
    depth = lanes // rows
    samples = rows * lanes * lanes
    me = lax.axis_index("seq")
    own = pl.multiple_of(me * depth, depth)
    at = [me ^ j for j in range(rows)]
    for j in range(n):
        work[at[j], 0, 0], work[at[j], 0, 1] = near_found[j, 0], near_found[j, 1]
    for k in range(2):
        whole_noise(noise.at[k], others[k].at[: lanes // 2], others[k].at[lanes // 2 :])
    last_noises = [noise.at[k] for k in range(2)]
    sums = (near_sums[0], near_sums[1])
    fields, sums = images(range(n, rows), blocks[n:], last_noises, precond, circulant, image, sums)
    noises = [near_noise.at[j] for j in range(n)] + last_noises
    image = [near_image.at[j] for j in range(n)] + [image.at[k] for k in range(2)]
    numerator, curvature = whole_sum(sums[0]), whole_sum(sums[1])
    for j, x in zip(range(n, rows), own_spectra(fields, at[n:], left, dft, turns, big_turn)):
        work[at[j], 0, 0], work[at[j], 0, 1] = x
    step_size = numerator / curvature
    cross = jnp.zeros((lead, lanes), exact)
    fields = []
    for j in range(rows):
        residual = signs[j][...] - step_size * image[j][...]
        cross += folded(residual * image[j][...])
        if j >= 2:
            fields.append(noises[j][...] * residual)
        if j == 0:
            residual_out[...] = residual.T
    weight = -2.0 * whole_sum(cross)
    for j in range(2):
        for part in range(2):
            work[at[j], 1, part] = near_found[n + j, part] - step_size * near_found[n + 2 + j, part]
    for r, x in zip(at[2:], own_spectra(fields, at[2:], left, dft, turns, big_turn)):
        work[r, 1, 0], work[r, 1, 1] = x
    noisy = small_dft([(work[r, 0, 0], work[r, 0, 1]) for r in range(rows)], -1)
    noisy_residual = small_dft([(work[r, 1, 0], work[r, 1, 1]) for r in range(rows)], -1)
    for a in range(rows):
        k, s = kernel[:, a], symbol[:, a]
        total = 0.0
        for part in range(2):
            base = spectrum[a, part]
            ki = k * (base / s) + noisy[a][part]
            applied = k * (base - step_size * ki) + noisy_residual[a][part]
            adjoint = (
                (weight / curvature) * base
                - (2.0 * weight * step_size / curvature) * ki
                - (2.0 * step_size) * applied
            )
            total += adjoint * base
        shares[a] = -total / (samples * s * s)
    width = rows // probes
    column = lax.axis_index("probe")
    for d in range(probes):
        for k in range(width):
            outs[d][:, k] = shares[(column ^ d) * width + k]


def call(kernel, outs, scratch, *operands):
    whole = pl.BlockSpec(memory_space=pltpu.VMEM)
    typed = [out if isinstance(out[0], tuple) else (out, exact) for out in outs]
    shapes = tuple(pltpu.VMEM(shape, dtype) for shape, dtype in typed)
    return pl.pallas_call(
        kernel,
        out_shape=shapes,
        in_specs=[whole] * len(operands),
        out_specs=(whole,) * len(shapes),
        scratch_shapes=[pltpu.VMEM(shape, exact) for shape in scratch],
        compiler_params=pltpu.CompilerParams(vmem_limit_bytes=24 << 20),
        cost_estimate=pl.CostEstimate(flops=0, bytes_accessed=0, transcendentals=0),
    )(*operands)


def swapped(x, axis, d):
    return lax.ppermute(x, axis, [(i, i ^ d) for i in range(lax.axis_size(axis))])


def after(x, *earlier):
    return lax.optimization_barrier((x, *earlier))[0]


def after(x, *earlier):
    return lax.optimization_barrier((x, *earlier))[0]


def other_core(x):
    return swapped(x, "seq", 1)


def across_x(x):
    return swapped(x, "probe", 1)


def next_chip(x):
    return swapped(x, "seq", 2)


def beyond_middle(x):
    return swapped(x, "seq", 4)


def adjoint_calls(
    rows, probes, blocks, noises, precond, circulant, spectrum, kernel, symbols, left, dft, turns, big_turn
):
    square = (lanes, lanes)
    depth, width, n = lanes // rows, rows // probes, rows - 2
    tables_held = (left, dft, turns, big_turn)
    near_parts = call(
        functools.partial(near_kernel, rows),
        [(n, *square), (n, *square), (n + 4, 2, depth, lanes), (2, lead, lanes)],
        [],
        *blocks[:n],
        *noises[:2],
        precond,
        circulant,
        *tables_held,
    )
    return call(
        functools.partial(adjoint_kernel, rows, probes),
        [square] + [(depth, width, lanes)] * probes,
        [(2, *square), (2, *square), (rows, 2, 2, depth, lanes), (rows, depth, lanes)],
        *blocks,
        *noises[2:],
        *near_parts,
        precond,
        circulant,
        spectrum,
        kernel,
        symbols,
        *tables_held,
    )


def gathered_shards(probe_bits, noise_var, kernel_spectrum, symbol, grad_prev):
    rows = kernel_spectrum.shape[1]
    probes = lax.axis_size("probe")
    half, depth, width = rows // 2, lanes // rows, rows // probes
    kernel = kernel_spectrum.T.reshape(rows, depth, lanes).transpose(1, 0, 2)
    symbols = symbol.T.reshape(rows, depth, lanes).transpose(1, 0, 2)
    before = grad_prev.T.reshape(width, depth, lanes).transpose(1, 0, 2)
    square = (lanes, lanes)
    dft, turns = tables(rows)
    first = lanes + 2 * half * depth + lead
    block, sent, dft, turns = pl.pallas_call(
        functools.partial(pack_kernel, half, first),
        out_shape=(
            pltpu.VMEM((first + lanes, lanes), exact),
            pltpu.VMEM((first + lanes // 2, lanes), exact),
            pltpu.VMEM(dft.shape, near),
            pltpu.VMEM(turns.shape, exact),
        ),
        in_specs=[pl.BlockSpec(memory_space=pl.ANY)] * 6,
        out_specs=(pl.BlockSpec(memory_space=pltpu.VMEM),) * 4,
        scratch_shapes=[
            pltpu.VMEM(square, jnp.int32),
            pltpu.VMEM(square, exact),
            pltpu.VMEM(kernel.shape, exact),
            pltpu.VMEM(kernel.shape, exact),
            pltpu.SemaphoreType.DMA((6,)),
        ],
    )(probe_bits.reshape(square), noise_var.reshape(square), kernel, symbols, dft, turns)
    far = beyond_middle(sent)
    neighbour = next_chip(sent)
    passed_on = next_chip(far[:first])
    early = [block, other_core(block), neighbour, far]
    found, left, big_turn = call(
        functools.partial(early_kernel, rows),
        [(len(early), 2, *square), ((4 * lanes, 2 * lanes), near), (rows, lanes, 2 * lanes)],
        [],
        *early,
        dft,
        turns,
    )
    halves = across_x(jnp.concatenate([neighbour[first:], far[first:]], 0))
    blocks = early[:2]
    for x, earlier in ((neighbour, found), (far, found), (passed_on, halves)):
        blocks += [x, other_core(after(x, earlier))]
    field = (rows, *square)
    spectrum, precond, circulant = call(
        functools.partial(inverse_kernel, rows),
        [(rows, 2, depth, lanes), field, field],
        [(half, *square), (half, *square), (rows, lead, lanes), (rows, 2, 2, *square)],
        *blocks,
        found,
        left,
        dft,
        turns,
        big_turn,
    )
    passed_noise = next_chip(jnp.concatenate([far[first:], halves[lanes // 2 :]], 0))
    last = after(passed_noise, precond)
    noises = [halves, other_core(halves), last, other_core(last)]
    residual, *parts = adjoint_calls(
        rows, probes, blocks, noises, precond, circulant, spectrum, kernel, symbols, left, dft, turns, big_turn
    )
    near_y, opposite, near_x = (swapped(parts[d], "probe", d) for d in (2, 3, 1))
    total = lax.optimization_barrier(parts[0] + near_y)
    total = lax.optimization_barrier(total + opposite)
    total = before + (total + near_x) / probes
    total = total.transpose(1, 0, 2).reshape(width, depth * lanes).T
    return residual.reshape(probe_bits.shape), total


highest = lax.Precision.HIGHEST
minor_width = 128


def dft_table(height, breadth, modulus, orient):
    left_index = jnp.arange(height, dtype=jnp.int32)[:, None]
    right_index = jnp.arange(breadth, dtype=jnp.int32)[None, :]
    phases = (
        orient * 2.0 * math.pi / modulus * (left_index * right_index % modulus).astype(jnp.float32)
    )
    return (jnp.cos(phases), jnp.sin(phases))


def complex_product(pattern, real_part, imaginary, cosine_table, sine_table):
    real_cos = jnp.einsum(pattern, real_part, cosine_table, precision=highest)
    real_sin = jnp.einsum(pattern, real_part, sine_table, precision=highest)
    if imaginary is None:
        return (real_cos, real_sin)
    imag_cos = jnp.einsum(pattern, imaginary, cosine_table, precision=highest)
    imag_sin = jnp.einsum(pattern, imaginary, sine_table, precision=highest)
    return (real_cos - imag_sin, real_sin + imag_cos)


def rotate(real_part, imaginary, cosine_table, sine_table):
    return (
        real_part * cosine_table - imaginary * sine_table,
        real_part * sine_table + imaginary * cosine_table,
    )


def forward_rows(series):
    major_len = series.shape[-2]
    length = major_len * minor_width
    cosine_table, sine_table = dft_table(major_len, major_len, major_len, -1.0)
    section_real, section_imag = complex_product(
        "...mi,mk->...ik", series, None, cosine_table, sine_table
    )
    turn_cos, turn_sin = dft_table(minor_width, major_len, length, -1.0)
    twisted_real, twisted_imag = rotate(section_real, section_imag, turn_cos, turn_sin)
    cosine_table, sine_table = dft_table(minor_width, minor_width, minor_width, -1.0)
    return complex_product("...ik,ij->...jk", twisted_real, twisted_imag, cosine_table, sine_table)


def inverse_rows(real_part, imaginary):
    major_len = real_part.shape[-1]
    length = major_len * minor_width
    cosine_table, sine_table = dft_table(minor_width, minor_width, minor_width, 1.0)
    section_real, section_imag = complex_product(
        "...jk,ji->...ik", real_part, imaginary, cosine_table, sine_table
    )
    turn_cos, turn_sin = dft_table(minor_width, major_len, length, 1.0)
    twisted_real, twisted_imag = rotate(section_real, section_imag, turn_cos, turn_sin)
    cosine_table, sine_table = dft_table(major_len, major_len, major_len, 1.0)
    final_real, unused = complex_product(
        "...ik,km->...mi", twisted_real, twisted_imag, cosine_table, sine_table
    )
    return final_real


def global_twiddle(local_rows, major_len, samples, orient):
    row_index = lax.axis_index("seq") * local_rows + jnp.arange(local_rows, dtype=jnp.int32)
    column_index = (
        jnp.arange(minor_width, dtype=jnp.int32)[:, None] * major_len
        + jnp.arange(major_len, dtype=jnp.int32)[None, :]
    )
    phases = (
        orient
        * 2.0
        * math.pi
        / samples
        * (row_index[:, None, None] * column_index[None, :, :] % samples).astype(jnp.float32)
    )
    return (jnp.cos(phases), jnp.sin(phases))


def forward_spectrum(series):
    local_rows = series.shape[1]
    major_len = series.shape[2]
    devices = lax.axis_size("seq")
    all_rows = local_rows * devices
    samples = all_rows * major_len * minor_width
    real_part, imaginary = forward_rows(series)
    turn_cos, turn_sin = global_twiddle(local_rows, major_len, samples, -1.0)
    turned_real, turned_imag = rotate(real_part, imaginary, turn_cos, turn_sin)
    arrived = lax.all_to_all(
        jnp.stack([turned_real, turned_imag]), "seq", split_axis=3, concat_axis=2, tiled=True
    )
    block = minor_width // devices * major_len
    arrived = arrived.reshape(arrived.shape[0], arrived.shape[1], all_rows, block)
    cosine_table, sine_table = dft_table(all_rows, all_rows, all_rows, -1.0)
    return complex_product("zrb,ra->zba", arrived[0], arrived[1], cosine_table, sine_table)


def inverse_field(spectrum_real, spectrum_imag):
    all_rows = spectrum_real.shape[2]
    block = spectrum_real.shape[1]
    devices = lax.axis_size("seq")
    major_len = block * devices // minor_width
    cosine_table, sine_table = dft_table(all_rows, all_rows, all_rows, 1.0)
    back_real, back_imag = complex_product(
        "zba,ar->zrb", spectrum_real, spectrum_imag, cosine_table, sine_table
    )
    stacked = jnp.stack([back_real, back_imag])
    stacked = stacked.reshape(
        stacked.shape[0], stacked.shape[1], all_rows, minor_width // devices, major_len
    )
    arrived = lax.all_to_all(stacked, "seq", split_axis=2, concat_axis=3, tiled=True)
    local_rows = arrived.shape[2]
    samples = all_rows * major_len * minor_width
    turn_cos, turn_sin = global_twiddle(local_rows, major_len, samples, 1.0)
    turned_real, turned_imag = rotate(arrived[0], arrived[1], turn_cos, turn_sin)
    return inverse_rows(turned_real, turned_imag) / samples


def shards(probe_bits, noise_var, kernel_spectrum, symbol, grad_prev):
    field_shape = (
        probe_bits.shape[0],
        probe_bits.shape[1],
        probe_bits.shape[2] // minor_width,
        minor_width,
    )
    sign_field = (2 * probe_bits - 1).astype(jnp.float32).reshape(field_shape)
    noise_field = noise_var.reshape(field_shape[1:])
    samples = kernel_spectrum.shape[1] * noise_var.shape[1]
    base_real, base_imag = forward_spectrum(sign_field)
    scaled_real = base_real / symbol
    scaled_imag = base_imag / symbol
    precond = inverse_field(scaled_real, scaled_imag)
    again_real, again_imag = forward_spectrum(precond)
    circulant = inverse_field(kernel_spectrum * again_real, kernel_spectrum * again_imag)
    kernel_image = circulant + noise_field * precond
    numerator, curvature = lax.psum(
        (jnp.sum(sign_field * precond), jnp.sum(precond * kernel_image)), "seq"
    )
    step_size = numerator / curvature
    residual = sign_field - step_size * kernel_image
    cross_term = lax.psum(jnp.sum(residual * kernel_image), "seq")
    weight = -2.0 * cross_term
    resid_real, resid_imag = forward_spectrum(residual)
    applied = (
        inverse_field(kernel_spectrum * resid_real, kernel_spectrum * resid_imag)
        + noise_field * residual
    )
    adjoint = (
        weight / curvature * sign_field
        - 2.0 * weight * step_size / curvature * kernel_image
        - 2.0 * step_size * applied
    )
    adjoint_real, adjoint_imag = forward_spectrum(adjoint)
    local_grad = -(adjoint_real[0] * base_real[0] + adjoint_imag[0] * base_imag[0]) / (
        samples * symbol * symbol
    )
    probes = lax.axis_size("probe")
    summed = lax.psum(local_grad, "probe")
    share_width = summed.shape[1] // probes
    own_share = lax.dynamic_slice_in_dim(
        summed, lax.axis_index("probe") * share_width, share_width, 1
    )
    grad_total = grad_prev + own_share / probes
    return (residual.reshape(probe_bits.shape), grad_total)


def fits(mesh, cols, rows):
    seq, probe = mesh.shape["seq"], mesh.shape["probe"]
    powers = all(n & (n - 1) == 0 for n in (rows, seq, probe))
    return powers and rows == seq == lead and rows % probe == 0 and probe > 1 and cols == lanes * lanes


def solution(mesh):
    placed = (
        P("probe", "seq", None),
        P("seq", None),
        P("seq", None),
        P("seq", None),
        P("seq", "probe"),
    )

    def whole(probe_bits, noise_var, kernel_spectrum, symbol, grad_prev):
        small = fits(mesh, *symbol.shape)
        return jax.shard_map(
            gathered_shards if small else shards,
            mesh=mesh,
            in_specs=placed,
            out_specs=(P("probe", "seq", None), P("seq", "probe")),
            check_vma=False,
        )(probe_bits, noise_var, kernel_spectrum, symbol, grad_prev)

    return whole
```

```python
import functools
import math

import jax
import jax.numpy as jnp
import numpy as np
from jax import lax
from jax.experimental import pallas as pl
from jax.experimental.pallas import tpu as pltpu
from jax.sharding import PartitionSpec as P

lanes = 128
lead = 8
near = jnp.bfloat16
exact = jnp.float32


def split_table(table):
    high = table.astype(near)
    low = (table - high.astype(np.float64)).astype(near)
    return high, low


def angle_parts(phase):
    return np.cos(phase), np.sin(phase)


@functools.cache
def tables(rows):
    index = np.arange(lanes, dtype=np.float64)
    turn = -2.0 * np.pi
    c, s = angle_parts(turn * (np.outer(index, index) % lanes) / lanes)
    c_high, c_low = split_table(c)
    s_high, s_low = split_table(s)
    row_len = lanes * lanes
    wc, ws = angle_parts(turn * np.outer(index, index) / row_len)
    flat = index[:, None] * lanes + index[None, :]
    gc, gs = angle_parts(turn * flat / (rows * row_len))
    turns = np.stack([np.concatenate([wc, ws], 1), np.concatenate([gc, gs], 1)])
    return np.stack([c_high, s_high, c_low, s_low]), turns.astype(np.float32)


def split(x):
    high = x.astype(near)
    return high, (x - high.astype(exact)).astype(near)


def stacked(first, second, axis):
    fh, fl = split(first)
    sh, sl = split(second)
    return jnp.concatenate([fh, sh], axis), jnp.concatenate([fl, sl], axis)


def times(left, right):
    return jnp.dot(left, right, preferred_element_type=exact)


def left_product(table, columns):
    n = table.shape[0] // 2
    high = jnp.concatenate([column[0] for column in columns], 1)
    low = jnp.concatenate([column[1] for column in columns], 1)
    both = times(table[...], high)
    return both[:n] + both[n:] + times(table[:n], low)


def turned(re, im, cos, sin):
    return re * cos - im * sin, re * sin + im * cos


def turned_back(re, im, cos, sin):
    return re * cos + im * sin, im * cos - re * sin


def add(x, y):
    return x[0] + y[0], x[1] + y[1]


def sub(x, y):
    return x[0] - y[0], x[1] - y[1]


def unit_turn(x, k, n, orient):
    k = (k * orient) % n
    if k == 0:
        return x
    if 4 * k == n:
        return -x[1], x[0]
    if 2 * k == n:
        return -x[0], -x[1]
    if 4 * k == 3 * n:
        return x[1], -x[0]
    cos, sin = math.cos(2 * math.pi * k / n), math.sin(2 * math.pi * k / n)
    return x[0] * cos - x[1] * sin, x[0] * sin + x[1] * cos


def small_dft(xs, orient):
    n = len(xs)
    if n == 1:
        return xs
    even, odd = small_dft(xs[0::2], orient), small_dft(xs[1::2], orient)
    odd = [unit_turn(x, k, n, orient) for k, x in enumerate(odd)]
    return [add(e, o) for e, o in zip(even, odd)] + [sub(e, o) for e, o in zip(even, odd)]


def half_dft(xs, orient):
    n = 2 * len(xs)
    even = small_dft(xs, orient)
    odd = small_dft([unit_turn(x, k, n, orient) for k, x in enumerate(xs)], orient)
    return [(odd if r % 2 else even)[r // 2] for r in range(n)]


def pack_kernel(half, first, *refs):
    sources, out, sent, held, landed, done = refs[:6], refs[6], refs[7], refs[8:10], refs[10:14], refs[14]
    targets = (*landed, *held)
    copies = [pltpu.make_async_copy(sources[i], targets[i], done.at[i]) for i in range(6)]
    for copy in copies:
        copy.start()
    bits, noise, kernel, symbol = landed
    copies[0].wait()
    out[:lanes] = (2 * bits[...] - 1).astype(exact).T
    copies[1].wait()
    out[first:] = noise[...].T
    copies[2].wait()
    copies[3].wait()
    depth = kernel.shape[0]
    for a in range(half):
        at = lanes + a * depth
        out[at : at + depth] = kernel[:, a]
        at += half * depth
        out[at : at + depth] = symbol[:, a]
    middle = jnp.concatenate([kernel[0, half : half + 1], symbol[0, half : half + 1]], 0)
    out[first - lead : first] = jnp.concatenate([middle] * (lead // 2), 0)
    sent[:first] = out[:first]
    share = lanes // 2
    side = lax.div(lax.axis_index("probe"), lax.axis_size("probe") // 2)
    sent[first:] = out[pl.ds(pl.multiple_of(first + side * share, lead), share)]
    copies[4].wait()
    copies[5].wait()


def row_spectra(signs, rows, sign_right, left, w, big_turn):
    lined = [jnp.concatenate([x[:lanes].astype(near)] * 2, 1) for x in signs]
    section = times(jnp.concatenate(lined, 0), sign_right)
    out = []
    for j in range(0, len(signs), 2):
        columns = []
        for k in (j, j + 1):
            at = slice(k * lanes, (k + 1) * lanes)
            columns.append(stacked(*turned(section[at, :lanes], section[at, lanes:], *w), 0))
        done = left_product(left, columns)
        for k in range(2):
            at, r = slice(k * lanes, (k + 1) * lanes), rows[j + k]
            out.append(turned(done[:lanes, at], done[lanes:, at], big_turn[r, :, :lanes], big_turn[r, :, lanes:]))
    return out


def sign_table(dft):
    c_high, s_high, c_low, s_low = (dft[k] for k in range(4))
    return jnp.concatenate([jnp.concatenate([c_high, s_high], 1), jnp.concatenate([c_low, s_low], 1)], 0)


def early_slots(rows):
    return [0, 1, *range(2, rows - 2, 2)]


def early_kernel(rows, *refs):
    early = early_slots(rows)
    blocks = refs[: len(early)]
    dft, turns, found, left, big_turn = refs[len(early) :]
    me = lax.axis_index("seq")
    c_high, s_high, c_low, s_low = (dft[k] for k in range(4))
    left[:lanes] = jnp.concatenate([c_high, -s_high], 1)
    left[lanes : 2 * lanes] = jnp.concatenate([s_high, c_high], 1)
    left[2 * lanes : 3 * lanes] = jnp.concatenate([c_low, -s_low], 1)
    left[3 * lanes :] = jnp.concatenate([s_low, c_low], 1)
    for t in range(0, lanes, lead):
        at = slice(t, t + lead)
        one = turns[1, at, :lanes], turns[1, at, lanes:]
        powers = [(jnp.ones((lead, lanes), exact), jnp.zeros((lead, lanes), exact)), one]
        for r in range(2, rows):
            powers.append(turned(*powers[r // 2], *powers[r - r // 2]))
        for r in range(rows):
            big_turn[r, at, :lanes] = powers[r][0]
            big_turn[r, at, lanes:] = powers[r][1]
    w = turns[0, :, :lanes], turns[0, :, lanes:]
    at = [me ^ j for j in early]
    for k, x in enumerate(row_spectra(blocks, at, sign_table(dft), left, w, big_turn)):
        found[k, 0], found[k, 1] = x


def inverse_kernel(rows, *refs):
    blocks = refs[:rows]
    found, left, dft, turns, big_turn, spectrum, precond, circulant, kernel, symbol, ends, work = refs[rows:]
    half, early = rows // 2, early_slots(rows)
    depth = lanes // rows
    samples = rows * lanes * lanes
    me = lax.axis_index("seq")
    w = turns[0, :, :lanes], turns[0, :, lanes:]
    for k, j in enumerate(early):
        work[me ^ j, 0, 0], work[me ^ j, 0, 1] = found[k, 0], found[k, 1]
    late = [j for j in range(rows) if j not in early]
    at = [me ^ j for j in late]
    for r, x in zip(at, row_spectra([blocks[j] for j in late], at, sign_table(dft), left, w, big_turn)):
        work[r, 0, 0], work[r, 0, 1] = x
    own = pl.ds(pl.multiple_of(me * depth, depth), depth)
    for a, x in enumerate(small_dft([(work[r, 0, 0, own], work[r, 0, 1, own]) for r in range(rows)], -1)):
        spectrum[a, 0], spectrum[a, 1] = x
    for j in range(rows):
        place = pl.multiple_of((me ^ j) * depth, depth)
        for a in range(half):
            at = lanes + a * depth
            kernel[a, pl.ds(place, depth)] = blocks[j][at : at + depth]
            at += half * depth
            symbol[a, pl.ds(place, depth)] = blocks[j][at : at + depth]
        ends[me ^ j] = blocks[j][lanes + 2 * half * depth : lanes + 2 * half * depth + lead]
    middle = sum((-1.0) ** r * work[r, 0, 0, 0:1, 0:1] for r in range(rows))
    middle = middle / ends[0, 1:2, 0:1] / samples
    middle_image = middle * ends[0, 0:1, 0:1]
    for t in range(0, lanes, lead):
        at = slice(t, t + lead)
        lower = small_dft([(work[r, 0, 0, at], work[r, 0, 1, at]) for r in range(rows)], -1)[:half]
        first, second = [], []
        for a in range(half):
            scale = 2.0 / samples / symbol[a, at]
            if a == 0 and t == 0:
                zero = (lax.broadcasted_iota(jnp.int32, (lead, lanes), 0) == 0) & (
                    lax.broadcasted_iota(jnp.int32, (lead, lanes), 1) == 0
                )
                scale = jnp.where(zero, 0.5 * scale, scale)
            re, im = lower[a][0] * scale, lower[a][1] * scale
            first.append((re, im))
            second.append((re * kernel[a, at], im * kernel[a, at]))
        for field, entries in enumerate((first, second)):
            out = half_dft(entries, 1)
            for r in range(rows):
                re, im = turned_back(*out[r], big_turn[r, at, :lanes], big_turn[r, at, lanes:])
                work[r, field, 0, at] = re
                work[r, field, 1, at] = im
    c_high, s_high, c_low, s_low = (dft[k] for k in range(4))
    back_right = jnp.concatenate([jnp.concatenate([c_high, s_high], 0), jnp.concatenate([c_low, s_low], 0)], 1)
    highs, lows = [], []
    for r in range(rows):
        columns = [stacked(work[r, field, 1], work[r, field, 0], 0) for field in range(2)]
        done = left_product(left, columns)
        for field in range(2):
            at = slice(field * lanes, (field + 1) * lanes)
            high, low = stacked(*turned_back(done[lanes:, at], done[:lanes, at], *w), 1)
            highs.append(high)
            lows.append(low)
    both = times(jnp.concatenate(highs, 0), back_right)
    done = both[:, :lanes] + both[:, lanes:] + times(jnp.concatenate(lows, 0), back_right[:, :lanes])
    for r in range(rows):
        sign = 1.0 if r % 2 == 0 else -1.0
        precond[r] = done[2 * r * lanes : (2 * r + 1) * lanes] + sign * middle
        circulant[r] = done[(2 * r + 1) * lanes : (2 * r + 2) * lanes] + sign * middle_image


def whole_sum(x):
    return jnp.sum(jnp.sum(x, axis=0, keepdims=True), axis=1, keepdims=True)


def folded(x):
    return sum(x[t : t + lead] for t in range(0, x.shape[0], lead))


def own_spectra(fields, at, left, dft, turns, big_turn):
    rows = big_turn.shape[0]
    depth = lanes // rows
    own = pl.multiple_of(lax.axis_index("seq") * depth, depth)
    c_high, s_high, c_low, s_low = (dft[k] for k in range(4))
    wide_high, wide_low = jnp.concatenate([c_high, s_high], 1), jnp.concatenate([c_low, s_low], 1)
    twice_high = jnp.concatenate([wide_high, wide_high], 0)
    w = turns[0, :, :lanes], turns[0, :, lanes:]
    parts = [left[pl.ds(pl.multiple_of(k * lanes + own, depth), depth)] for k in range(4)]
    block = jnp.concatenate(parts, 0)
    highs, lows = zip(*(split(x) for x in fields))
    highs, lows = jnp.concatenate(highs, 0), jnp.concatenate(lows, 0)
    section = times(jnp.concatenate([highs, lows], 1), twice_high) + times(highs, wide_low)
    out = []
    for j in range(0, len(fields), 2):
        columns = []
        for i in (j, j + 1):
            here = slice(i * lanes, (i + 1) * lanes)
            columns.append(stacked(*turned(section[here, :lanes], section[here, lanes:], *w), 0))
        done = left_product(block, columns)
        for i in range(2):
            here, r = slice(i * lanes, (i + 1) * lanes), at[j + i]
            gc, gs = big_turn[r, pl.ds(own, depth), :lanes], big_turn[r, pl.ds(own, depth), lanes:]
            out.append(turned(done[:depth, here], done[depth:, here], gc, gs))
    return out


def whole_noise(target, held, other):
    share = lanes // 2
    side = lax.div(lax.axis_index("probe"), lax.axis_size("probe") // 2) * share
    target[pl.ds(pl.multiple_of(side, share), share)] = held[held.shape[0] - share :]
    target[pl.ds(pl.multiple_of(share - side, share), share)] = other[...]


def images(slots, signs, noises, precond, circulant, image, sums):
    me = lax.axis_index("seq")
    fields = []
    numerator, curvature = sums
    for k, j in enumerate(slots):
        p = precond[me ^ j]
        noisy = noises[k][...] * p
        ki = circulant[me ^ j] + noisy
        image[k] = ki
        fields.append(noisy)
        numerator += folded(signs[k][:lanes] * p)
        curvature += folded(p * ki)
    return fields, (numerator, curvature)


def near_kernel(rows, *refs):
    n = rows - 2
    blocks, others = refs[:n], refs[n : n + 2]
    precond, circulant, left, dft, turns, big_turn, image, noise, found, sums = refs[n + 2 :]
    share = lanes // 2
    for j in range(2):
        noise[j] = blocks[j][blocks[j].shape[0] - lanes :]
    for j in range(2, n):
        whole_noise(noise.at[j], blocks[j], others[j % 2].at[(j - 2) // 2 * share : j // 2 * share])
    zero = jnp.zeros((lead, lanes), exact)
    noises = [noise.at[j] for j in range(n)]
    fields, totals = images(range(n), blocks, noises, precond, circulant, image, (zero, zero))
    sums[0], sums[1] = totals
    at = [lax.axis_index("seq") ^ j for j in range(n)]
    fields += [noises[j][...] * blocks[j][:lanes] for j in range(2)] + [noises[j][...] * image[j] for j in range(2)]
    for j, x in enumerate(own_spectra(fields, at + at[:2] * 2, left, dft, turns, big_turn)):
        found[j, 0], found[j, 1] = x


def adjoint_kernel(rows, probes, *refs):
    n = rows - 2
    signs = [refs[j].at[:lanes] for j in range(rows)]
    blocks, others = refs[:rows], refs[rows : rows + 2]
    near_image, near_noise, near_found, near_sums = refs[rows + 2 : rows + 6]
    refs = refs[rows + 6 :]
    precond, circulant, spectrum, kernel, symbol, left, dft, turns, big_turn, residual_out = refs[:10]
    outs = refs[10 : 10 + probes]
    image, noise, work, shares = refs[10 + probes :]
    depth = lanes // rows
    samples = rows * lanes * lanes
    me = lax.axis_index("seq")
    own = pl.multiple_of(me * depth, depth)
    at = [me ^ j for j in range(rows)]
    for j in range(n):
        work[at[j], 0, 0], work[at[j], 0, 1] = near_found[j, 0], near_found[j, 1]
    for k in range(2):
        whole_noise(noise.at[k], others[k].at[: lanes // 2], others[k].at[lanes // 2 :])
    last_noises = [noise.at[k] for k in range(2)]
    sums = (near_sums[0], near_sums[1])
    fields, sums = images(range(n, rows), blocks[n:], last_noises, precond, circulant, image, sums)
    noises = [near_noise.at[j] for j in range(n)] + last_noises
    image = [near_image.at[j] for j in range(n)] + [image.at[k] for k in range(2)]
    numerator, curvature = whole_sum(sums[0]), whole_sum(sums[1])
    for j, x in zip(range(n, rows), own_spectra(fields, at[n:], left, dft, turns, big_turn)):
        work[at[j], 0, 0], work[at[j], 0, 1] = x
    step_size = numerator / curvature
    cross = jnp.zeros((lead, lanes), exact)
    fields = []
    for j in range(rows):
        residual = signs[j][...] - step_size * image[j][...]
        cross += folded(residual * image[j][...])
        if j >= 2:
            fields.append(noises[j][...] * residual)
        if j == 0:
            residual_out[...] = residual.T
    weight = -2.0 * whole_sum(cross)
    for j in range(2):
        for part in range(2):
            work[at[j], 1, part] = near_found[n + j, part] - step_size * near_found[n + 2 + j, part]
    for r, x in zip(at[2:], own_spectra(fields, at[2:], left, dft, turns, big_turn)):
        work[r, 1, 0], work[r, 1, 1] = x
    noisy = small_dft([(work[r, 0, 0], work[r, 0, 1]) for r in range(rows)], -1)
    noisy_residual = small_dft([(work[r, 1, 0], work[r, 1, 1]) for r in range(rows)], -1)
    for a in range(rows):
        k, s = kernel[:, a], symbol[:, a]
        total = 0.0
        for part in range(2):
            base = spectrum[a, part]
            ki = k * (base / s) + noisy[a][part]
            applied = k * (base - step_size * ki) + noisy_residual[a][part]
            adjoint = (
                (weight / curvature) * base
                - (2.0 * weight * step_size / curvature) * ki
                - (2.0 * step_size) * applied
            )
            total += adjoint * base
        shares[a] = -total / (samples * s * s)
    width = rows // probes
    column = lax.axis_index("probe")
    for d in range(probes):
        for k in range(width):
            outs[d][:, k] = shares[(column ^ d) * width + k]


def call(kernel, outs, scratch, *operands):
    whole = pl.BlockSpec(memory_space=pltpu.VMEM)
    typed = [out if isinstance(out[0], tuple) else (out, exact) for out in outs]
    shapes = tuple(pltpu.VMEM(shape, dtype) for shape, dtype in typed)
    return pl.pallas_call(
        kernel,
        out_shape=shapes,
        in_specs=[whole] * len(operands),
        out_specs=(whole,) * len(shapes),
        scratch_shapes=[pltpu.VMEM(shape, exact) for shape in scratch],
        compiler_params=pltpu.CompilerParams(vmem_limit_bytes=24 << 20),
        cost_estimate=pl.CostEstimate(flops=0, bytes_accessed=0, transcendentals=0),
    )(*operands)


def swapped(x, axis, d):
    return lax.ppermute(x, axis, [(i, i ^ d) for i in range(lax.axis_size(axis))])


def after(x, *earlier):
    return lax.optimization_barrier((x, *earlier))[0]


def after(x, *earlier):
    return lax.optimization_barrier((x, *earlier))[0]


def other_core(x):
    return swapped(x, "seq", 1)


def across_y(x):
    return swapped(x, "probe", lax.axis_size("probe") // 2)


def next_chip(x):
    return swapped(x, "seq", 2)


def beyond_middle(x):
    return swapped(x, "seq", 4)


def adjoint_calls(
    rows, probes, blocks, noises, precond, circulant, spectrum, kernel, symbols, left, dft, turns, big_turn
):
    square = (lanes, lanes)
    depth, width, n = lanes // rows, rows // probes, rows - 2
    tables_held = (left, dft, turns, big_turn)
    near_parts = call(
        functools.partial(near_kernel, rows),
        [(n, *square), (n, *square), (n + 4, 2, depth, lanes), (2, lead, lanes)],
        [],
        *blocks[:n],
        *noises[:2],
        precond,
        circulant,
        *tables_held,
    )
    return call(
        functools.partial(adjoint_kernel, rows, probes),
        [square] + [(depth, width, lanes)] * probes,
        [(2, *square), (2, *square), (rows, 2, 2, depth, lanes), (rows, depth, lanes)],
        *blocks,
        *noises[2:],
        *near_parts,
        precond,
        circulant,
        spectrum,
        kernel,
        symbols,
        *tables_held,
    )


def gathered_shards(probe_bits, noise_var, kernel_spectrum, symbol, grad_prev):
    rows = kernel_spectrum.shape[1]
    probes = lax.axis_size("probe")
    half, depth, width = rows // 2, lanes // rows, rows // probes
    kernel = kernel_spectrum.T.reshape(rows, depth, lanes).transpose(1, 0, 2)
    symbols = symbol.T.reshape(rows, depth, lanes).transpose(1, 0, 2)
    before = grad_prev.T.reshape(width, depth, lanes).transpose(1, 0, 2)
    square = (lanes, lanes)
    dft, turns = tables(rows)
    first = lanes + 2 * half * depth + lead
    block, sent, dft, turns = pl.pallas_call(
        functools.partial(pack_kernel, half, first),
        out_shape=(
            pltpu.VMEM((first + lanes, lanes), exact),
            pltpu.VMEM((first + lanes // 2, lanes), exact),
            pltpu.VMEM(dft.shape, near),
            pltpu.VMEM(turns.shape, exact),
        ),
        in_specs=[pl.BlockSpec(memory_space=pl.ANY)] * 6,
        out_specs=(pl.BlockSpec(memory_space=pltpu.VMEM),) * 4,
        scratch_shapes=[
            pltpu.VMEM(square, jnp.int32),
            pltpu.VMEM(square, exact),
            pltpu.VMEM(kernel.shape, exact),
            pltpu.VMEM(kernel.shape, exact),
            pltpu.SemaphoreType.DMA((6,)),
        ],
    )(probe_bits.reshape(square), noise_var.reshape(square), kernel, symbols, dft, turns)
    far = beyond_middle(sent)
    neighbour = next_chip(sent)
    passed_on = next_chip(far[:first])
    early = [block, other_core(block), neighbour, far]
    found, left, big_turn = call(
        functools.partial(early_kernel, rows),
        [(len(early), 2, *square), ((4 * lanes, 2 * lanes), near), (rows, lanes, 2 * lanes)],
        [],
        *early,
        dft,
        turns,
    )
    halves = across_y(jnp.concatenate([neighbour[first:], far[first:]], 0))
    blocks = early[:2]
    for x, earlier in ((neighbour, found), (far, found), (passed_on, halves)):
        blocks += [x, other_core(after(x, earlier))]
    field = (rows, *square)
    spectrum, precond, circulant = call(
        functools.partial(inverse_kernel, rows),
        [(rows, 2, depth, lanes), field, field],
        [(half, *square), (half, *square), (rows, lead, lanes), (rows, 2, 2, *square)],
        *blocks,
        found,
        left,
        dft,
        turns,
        big_turn,
    )
    passed_noise = next_chip(jnp.concatenate([far[first:], halves[lanes // 2 :]], 0))
    last = after(passed_noise, precond)
    noises = [halves, other_core(halves), last, other_core(last)]
    residual, *parts = adjoint_calls(
        rows, probes, blocks, noises, precond, circulant, spectrum, kernel, symbols, left, dft, turns, big_turn
    )
    near_y, opposite, near_x = (swapped(parts[d], "probe", d) for d in (2, 3, 1))
    total = lax.optimization_barrier(parts[0] + near_y)
    total = lax.optimization_barrier(total + opposite)
    total = before + (total + near_x) / probes
    total = total.transpose(1, 0, 2).reshape(width, depth * lanes).T
    return residual.reshape(probe_bits.shape), total


highest = lax.Precision.HIGHEST
minor_width = 128


def dft_table(height, breadth, modulus, orient):
    left_index = jnp.arange(height, dtype=jnp.int32)[:, None]
    right_index = jnp.arange(breadth, dtype=jnp.int32)[None, :]
    phases = (
        orient * 2.0 * math.pi / modulus * (left_index * right_index % modulus).astype(jnp.float32)
    )
    return (jnp.cos(phases), jnp.sin(phases))


def complex_product(pattern, real_part, imaginary, cosine_table, sine_table):
    real_cos = jnp.einsum(pattern, real_part, cosine_table, precision=highest)
    real_sin = jnp.einsum(pattern, real_part, sine_table, precision=highest)
    if imaginary is None:
        return (real_cos, real_sin)
    imag_cos = jnp.einsum(pattern, imaginary, cosine_table, precision=highest)
    imag_sin = jnp.einsum(pattern, imaginary, sine_table, precision=highest)
    return (real_cos - imag_sin, real_sin + imag_cos)


def rotate(real_part, imaginary, cosine_table, sine_table):
    return (
        real_part * cosine_table - imaginary * sine_table,
        real_part * sine_table + imaginary * cosine_table,
    )


def forward_rows(series):
    major_len = series.shape[-2]
    length = major_len * minor_width
    cosine_table, sine_table = dft_table(major_len, major_len, major_len, -1.0)
    section_real, section_imag = complex_product(
        "...mi,mk->...ik", series, None, cosine_table, sine_table
    )
    turn_cos, turn_sin = dft_table(minor_width, major_len, length, -1.0)
    twisted_real, twisted_imag = rotate(section_real, section_imag, turn_cos, turn_sin)
    cosine_table, sine_table = dft_table(minor_width, minor_width, minor_width, -1.0)
    return complex_product("...ik,ij->...jk", twisted_real, twisted_imag, cosine_table, sine_table)


def inverse_rows(real_part, imaginary):
    major_len = real_part.shape[-1]
    length = major_len * minor_width
    cosine_table, sine_table = dft_table(minor_width, minor_width, minor_width, 1.0)
    section_real, section_imag = complex_product(
        "...jk,ji->...ik", real_part, imaginary, cosine_table, sine_table
    )
    turn_cos, turn_sin = dft_table(minor_width, major_len, length, 1.0)
    twisted_real, twisted_imag = rotate(section_real, section_imag, turn_cos, turn_sin)
    cosine_table, sine_table = dft_table(major_len, major_len, major_len, 1.0)
    final_real, unused = complex_product(
        "...ik,km->...mi", twisted_real, twisted_imag, cosine_table, sine_table
    )
    return final_real


def global_twiddle(local_rows, major_len, samples, orient):
    row_index = lax.axis_index("seq") * local_rows + jnp.arange(local_rows, dtype=jnp.int32)
    column_index = (
        jnp.arange(minor_width, dtype=jnp.int32)[:, None] * major_len
        + jnp.arange(major_len, dtype=jnp.int32)[None, :]
    )
    phases = (
        orient
        * 2.0
        * math.pi
        / samples
        * (row_index[:, None, None] * column_index[None, :, :] % samples).astype(jnp.float32)
    )
    return (jnp.cos(phases), jnp.sin(phases))


def forward_spectrum(series):
    local_rows = series.shape[1]
    major_len = series.shape[2]
    devices = lax.axis_size("seq")
    all_rows = local_rows * devices
    samples = all_rows * major_len * minor_width
    real_part, imaginary = forward_rows(series)
    turn_cos, turn_sin = global_twiddle(local_rows, major_len, samples, -1.0)
    turned_real, turned_imag = rotate(real_part, imaginary, turn_cos, turn_sin)
    arrived = lax.all_to_all(
        jnp.stack([turned_real, turned_imag]), "seq", split_axis=3, concat_axis=2, tiled=True
    )
    block = minor_width // devices * major_len
    arrived = arrived.reshape(arrived.shape[0], arrived.shape[1], all_rows, block)
    cosine_table, sine_table = dft_table(all_rows, all_rows, all_rows, -1.0)
    return complex_product("zrb,ra->zba", arrived[0], arrived[1], cosine_table, sine_table)


def inverse_field(spectrum_real, spectrum_imag):
    all_rows = spectrum_real.shape[2]
    block = spectrum_real.shape[1]
    devices = lax.axis_size("seq")
    major_len = block * devices // minor_width
    cosine_table, sine_table = dft_table(all_rows, all_rows, all_rows, 1.0)
    back_real, back_imag = complex_product(
        "zba,ar->zrb", spectrum_real, spectrum_imag, cosine_table, sine_table
    )
    stacked = jnp.stack([back_real, back_imag])
    stacked = stacked.reshape(
        stacked.shape[0], stacked.shape[1], all_rows, minor_width // devices, major_len
    )
    arrived = lax.all_to_all(stacked, "seq", split_axis=2, concat_axis=3, tiled=True)
    local_rows = arrived.shape[2]
    samples = all_rows * major_len * minor_width
    turn_cos, turn_sin = global_twiddle(local_rows, major_len, samples, 1.0)
    turned_real, turned_imag = rotate(arrived[0], arrived[1], turn_cos, turn_sin)
    return inverse_rows(turned_real, turned_imag) / samples


def shards(probe_bits, noise_var, kernel_spectrum, symbol, grad_prev):
    field_shape = (
        probe_bits.shape[0],
        probe_bits.shape[1],
        probe_bits.shape[2] // minor_width,
        minor_width,
    )
    sign_field = (2 * probe_bits - 1).astype(jnp.float32).reshape(field_shape)
    noise_field = noise_var.reshape(field_shape[1:])
    samples = kernel_spectrum.shape[1] * noise_var.shape[1]
    base_real, base_imag = forward_spectrum(sign_field)
    scaled_real = base_real / symbol
    scaled_imag = base_imag / symbol
    precond = inverse_field(scaled_real, scaled_imag)
    again_real, again_imag = forward_spectrum(precond)
    circulant = inverse_field(kernel_spectrum * again_real, kernel_spectrum * again_imag)
    kernel_image = circulant + noise_field * precond
    numerator, curvature = lax.psum(
        (jnp.sum(sign_field * precond), jnp.sum(precond * kernel_image)), "seq"
    )
    step_size = numerator / curvature
    residual = sign_field - step_size * kernel_image
    cross_term = lax.psum(jnp.sum(residual * kernel_image), "seq")
    weight = -2.0 * cross_term
    resid_real, resid_imag = forward_spectrum(residual)
    applied = (
        inverse_field(kernel_spectrum * resid_real, kernel_spectrum * resid_imag)
        + noise_field * residual
    )
    adjoint = (
        weight / curvature * sign_field
        - 2.0 * weight * step_size / curvature * kernel_image
        - 2.0 * step_size * applied
    )
    adjoint_real, adjoint_imag = forward_spectrum(adjoint)
    local_grad = -(adjoint_real[0] * base_real[0] + adjoint_imag[0] * base_imag[0]) / (
        samples * symbol * symbol
    )
    probes = lax.axis_size("probe")
    summed = lax.psum(local_grad, "probe")
    share_width = summed.shape[1] // probes
    own_share = lax.dynamic_slice_in_dim(
        summed, lax.axis_index("probe") * share_width, share_width, 1
    )
    grad_total = grad_prev + own_share / probes
    return (residual.reshape(probe_bits.shape), grad_total)


def fits(mesh, cols, rows):
    seq, probe = mesh.shape["seq"], mesh.shape["probe"]
    powers = all(n & (n - 1) == 0 for n in (rows, seq, probe))
    return powers and rows == seq == lead and rows % probe == 0 and probe > 1 and cols == lanes * lanes


def solution(mesh):
    placed = (
        P("probe", "seq", None),
        P("seq", None),
        P("seq", None),
        P("seq", None),
        P("seq", "probe"),
    )

    def whole(probe_bits, noise_var, kernel_spectrum, symbol, grad_prev):
        small = fits(mesh, *symbol.shape)
        return jax.shard_map(
            gathered_shards if small else shards,
            mesh=mesh,
            in_specs=placed,
            out_specs=(P("probe", "seq", None), P("seq", "probe")),
            check_vma=False,
        )(probe_bits, noise_var, kernel_spectrum, symbol, grad_prev)

    return whole
```

```python
import functools
import math

import jax
import jax.numpy as jnp
import numpy as np
from jax import lax
from jax.experimental import pallas as pl
from jax.experimental.pallas import tpu as pltpu
from jax.sharding import PartitionSpec as P

lanes = 128
lead = 8
near = jnp.bfloat16
exact = jnp.float32


def split_table(table):
    high = table.astype(near)
    low = (table - high.astype(np.float64)).astype(near)
    return high, low


def angle_parts(phase):
    return np.cos(phase), np.sin(phase)


@functools.cache
def tables(rows):
    index = np.arange(lanes, dtype=np.float64)
    turn = -2.0 * np.pi
    c, s = angle_parts(turn * (np.outer(index, index) % lanes) / lanes)
    c_high, c_low = split_table(c)
    s_high, s_low = split_table(s)
    row_len = lanes * lanes
    wc, ws = angle_parts(turn * np.outer(index, index) / row_len)
    flat = index[:, None] * lanes + index[None, :]
    gc, gs = angle_parts(turn * flat / (rows * row_len))
    turns = np.stack([np.concatenate([wc, ws], 1), np.concatenate([gc, gs], 1)])
    return np.stack([c_high, s_high, c_low, s_low]), turns.astype(np.float32)


def split(x):
    high = x.astype(near)
    return high, (x - high.astype(exact)).astype(near)


def stacked(first, second, axis):
    fh, fl = split(first)
    sh, sl = split(second)
    return jnp.concatenate([fh, sh], axis), jnp.concatenate([fl, sl], axis)


def times(left, right):
    return jnp.dot(left, right, preferred_element_type=exact)


def left_product(table, columns):
    n = table.shape[0] // 2
    high = jnp.concatenate([column[0] for column in columns], 1)
    low = jnp.concatenate([column[1] for column in columns], 1)
    both = times(table[...], high)
    return both[:n] + both[n:] + times(table[:n], low)


def turned(re, im, cos, sin):
    return re * cos - im * sin, re * sin + im * cos


def turned_back(re, im, cos, sin):
    return re * cos + im * sin, im * cos - re * sin


def add(x, y):
    return x[0] + y[0], x[1] + y[1]


def sub(x, y):
    return x[0] - y[0], x[1] - y[1]


def unit_turn(x, k, n, orient):
    k = (k * orient) % n
    if k == 0:
        return x
    if 4 * k == n:
        return -x[1], x[0]
    if 2 * k == n:
        return -x[0], -x[1]
    if 4 * k == 3 * n:
        return x[1], -x[0]
    cos, sin = math.cos(2 * math.pi * k / n), math.sin(2 * math.pi * k / n)
    return x[0] * cos - x[1] * sin, x[0] * sin + x[1] * cos


def small_dft(xs, orient):
    n = len(xs)
    if n == 1:
        return xs
    even, odd = small_dft(xs[0::2], orient), small_dft(xs[1::2], orient)
    odd = [unit_turn(x, k, n, orient) for k, x in enumerate(odd)]
    return [add(e, o) for e, o in zip(even, odd)] + [sub(e, o) for e, o in zip(even, odd)]


def half_dft(xs, orient):
    n = 2 * len(xs)
    even = small_dft(xs, orient)
    odd = small_dft([unit_turn(x, k, n, orient) for k, x in enumerate(xs)], orient)
    return [(odd if r % 2 else even)[r // 2] for r in range(n)]


def pack_kernel(half, first, *refs):
    sources, out, sent, held, landed, done = refs[:6], refs[6], refs[7], refs[8:10], refs[10:14], refs[14]
    targets = (*landed, *held)
    copies = [pltpu.make_async_copy(sources[i], targets[i], done.at[i]) for i in range(6)]
    for copy in copies:
        copy.start()
    bits, noise, kernel, symbol = landed
    copies[0].wait()
    out[:lanes] = (2 * bits[...] - 1).astype(exact).T
    copies[1].wait()
    out[first:] = noise[...].T
    copies[2].wait()
    copies[3].wait()
    depth = kernel.shape[0]
    for a in range(half):
        at = lanes + a * depth
        out[at : at + depth] = kernel[:, a]
        at += half * depth
        out[at : at + depth] = symbol[:, a]
    middle = jnp.concatenate([kernel[0, half : half + 1], symbol[0, half : half + 1]], 0)
    out[first - lead : first] = jnp.concatenate([middle] * (lead // 2), 0)
    sent[:first] = out[:first]
    share = lanes // 2
    side = lax.div(lax.axis_index("probe"), lax.axis_size("probe") // 2)
    sent[first:] = out[pl.ds(pl.multiple_of(first + side * share, lead), share)]
    copies[4].wait()
    copies[5].wait()


def row_spectra(signs, rows, sign_right, left, w, big_turn):
    lined = [jnp.concatenate([x[:lanes].astype(near)] * 2, 1) for x in signs]
    section = times(jnp.concatenate(lined, 0), sign_right)
    out = []
    for j in range(0, len(signs), 2):
        columns = []
        for k in (j, j + 1):
            at = slice(k * lanes, (k + 1) * lanes)
            columns.append(stacked(*turned(section[at, :lanes], section[at, lanes:], *w), 0))
        done = left_product(left, columns)
        for k in range(2):
            at, r = slice(k * lanes, (k + 1) * lanes), rows[j + k]
            out.append(turned(done[:lanes, at], done[lanes:, at], big_turn[r, :, :lanes], big_turn[r, :, lanes:]))
    return out


def sign_table(dft):
    c_high, s_high, c_low, s_low = (dft[k] for k in range(4))
    return jnp.concatenate([jnp.concatenate([c_high, s_high], 1), jnp.concatenate([c_low, s_low], 1)], 0)


def early_slots(rows):
    return [0, 1, *range(2, rows - 2, 2)]


def early_kernel(rows, *refs):
    early = early_slots(rows)
    blocks = refs[: len(early)]
    dft, turns, found, left, big_turn = refs[len(early) :]
    me = lax.axis_index("seq")
    c_high, s_high, c_low, s_low = (dft[k] for k in range(4))
    left[:lanes] = jnp.concatenate([c_high, -s_high], 1)
    left[lanes : 2 * lanes] = jnp.concatenate([s_high, c_high], 1)
    left[2 * lanes : 3 * lanes] = jnp.concatenate([c_low, -s_low], 1)
    left[3 * lanes :] = jnp.concatenate([s_low, c_low], 1)
    for t in range(0, lanes, lead):
        at = slice(t, t + lead)
        one = turns[1, at, :lanes], turns[1, at, lanes:]
        powers = [(jnp.ones((lead, lanes), exact), jnp.zeros((lead, lanes), exact)), one]
        for r in range(2, rows):
            powers.append(turned(*powers[r // 2], *powers[r - r // 2]))
        for r in range(rows):
            big_turn[r, at, :lanes] = powers[r][0]
            big_turn[r, at, lanes:] = powers[r][1]
    w = turns[0, :, :lanes], turns[0, :, lanes:]
    at = [me ^ j for j in early]
    for k, x in enumerate(row_spectra(blocks, at, sign_table(dft), left, w, big_turn)):
        found[k, 0], found[k, 1] = x


def inverse_kernel(rows, *refs):
    blocks = refs[:rows]
    found, left, dft, turns, big_turn, spectrum, precond, circulant, kernel, symbol, ends, work = refs[rows:]
    half, early = rows // 2, early_slots(rows)
    depth = lanes // rows
    samples = rows * lanes * lanes
    me = lax.axis_index("seq")
    w = turns[0, :, :lanes], turns[0, :, lanes:]
    for k, j in enumerate(early):
        work[me ^ j, 0, 0], work[me ^ j, 0, 1] = found[k, 0], found[k, 1]
    late = [j for j in range(rows) if j not in early]
    at = [me ^ j for j in late]
    for r, x in zip(at, row_spectra([blocks[j] for j in late], at, sign_table(dft), left, w, big_turn)):
        work[r, 0, 0], work[r, 0, 1] = x
    own = pl.ds(pl.multiple_of(me * depth, depth), depth)
    for a, x in enumerate(small_dft([(work[r, 0, 0, own], work[r, 0, 1, own]) for r in range(rows)], -1)):
        spectrum[a, 0], spectrum[a, 1] = x
    for j in range(rows):
        place = pl.multiple_of((me ^ j) * depth, depth)
        for a in range(half):
            at = lanes + a * depth
            kernel[a, pl.ds(place, depth)] = blocks[j][at : at + depth]
            at += half * depth
            symbol[a, pl.ds(place, depth)] = blocks[j][at : at + depth]
        ends[me ^ j] = blocks[j][lanes + 2 * half * depth : lanes + 2 * half * depth + lead]
    middle = sum((-1.0) ** r * work[r, 0, 0, 0:1, 0:1] for r in range(rows))
    middle = middle / ends[0, 1:2, 0:1] / samples
    middle_image = middle * ends[0, 0:1, 0:1]
    for t in range(0, lanes, lead):
        at = slice(t, t + lead)
        lower = small_dft([(work[r, 0, 0, at], work[r, 0, 1, at]) for r in range(rows)], -1)[:half]
        first, second = [], []
        for a in range(half):
            scale = 2.0 / samples / symbol[a, at]
            if a == 0 and t == 0:
                zero = (lax.broadcasted_iota(jnp.int32, (lead, lanes), 0) == 0) & (
                    lax.broadcasted_iota(jnp.int32, (lead, lanes), 1) == 0
                )
                scale = jnp.where(zero, 0.5 * scale, scale)
            re, im = lower[a][0] * scale, lower[a][1] * scale
            first.append((re, im))
            second.append((re * kernel[a, at], im * kernel[a, at]))
        for field, entries in enumerate((first, second)):
            out = half_dft(entries, 1)
            for r in range(rows):
                re, im = turned_back(*out[r], big_turn[r, at, :lanes], big_turn[r, at, lanes:])
                work[r, field, 0, at] = re
                work[r, field, 1, at] = im
    c_high, s_high, c_low, s_low = (dft[k] for k in range(4))
    back_right = jnp.concatenate([jnp.concatenate([c_high, s_high], 0), jnp.concatenate([c_low, s_low], 0)], 1)
    highs, lows = [], []
    for r in range(rows):
        columns = [stacked(work[r, field, 1], work[r, field, 0], 0) for field in range(2)]
        done = left_product(left, columns)
        for field in range(2):
            at = slice(field * lanes, (field + 1) * lanes)
            high, low = stacked(*turned_back(done[lanes:, at], done[:lanes, at], *w), 1)
            highs.append(high)
            lows.append(low)
    both = times(jnp.concatenate(highs, 0), back_right)
    done = both[:, :lanes] + both[:, lanes:] + times(jnp.concatenate(lows, 0), back_right[:, :lanes])
    for r in range(rows):
        sign = 1.0 if r % 2 == 0 else -1.0
        precond[r] = done[2 * r * lanes : (2 * r + 1) * lanes] + sign * middle
        circulant[r] = done[(2 * r + 1) * lanes : (2 * r + 2) * lanes] + sign * middle_image


def whole_sum(x):
    return jnp.sum(jnp.sum(x, axis=0, keepdims=True), axis=1, keepdims=True)


def folded(x):
    return sum(x[t : t + lead] for t in range(0, x.shape[0], lead))


def own_spectra(fields, at, left, dft, turns, big_turn):
    rows = big_turn.shape[0]
    depth = lanes // rows
    own = pl.multiple_of(lax.axis_index("seq") * depth, depth)
    c_high, s_high, c_low, s_low = (dft[k] for k in range(4))
    wide_high, wide_low = jnp.concatenate([c_high, s_high], 1), jnp.concatenate([c_low, s_low], 1)
    twice_high = jnp.concatenate([wide_high, wide_high], 0)
    w = turns[0, :, :lanes], turns[0, :, lanes:]
    parts = [left[pl.ds(pl.multiple_of(k * lanes + own, depth), depth)] for k in range(4)]
    block = jnp.concatenate(parts, 0)
    highs, lows = zip(*(split(x) for x in fields))
    highs, lows = jnp.concatenate(highs, 0), jnp.concatenate(lows, 0)
    section = times(jnp.concatenate([highs, lows], 1), twice_high) + times(highs, wide_low)
    out = []
    for j in range(0, len(fields), 2):
        columns = []
        for i in (j, j + 1):
            here = slice(i * lanes, (i + 1) * lanes)
            columns.append(stacked(*turned(section[here, :lanes], section[here, lanes:], *w), 0))
        done = left_product(block, columns)
        for i in range(2):
            here, r = slice(i * lanes, (i + 1) * lanes), at[j + i]
            gc, gs = big_turn[r, pl.ds(own, depth), :lanes], big_turn[r, pl.ds(own, depth), lanes:]
            out.append(turned(done[:depth, here], done[depth:, here], gc, gs))
    return out


def whole_noise(target, held, other):
    share = lanes // 2
    side = lax.div(lax.axis_index("probe"), lax.axis_size("probe") // 2) * share
    target[pl.ds(pl.multiple_of(side, share), share)] = held[held.shape[0] - share :]
    target[pl.ds(pl.multiple_of(share - side, share), share)] = other[...]


def images(slots, signs, noises, precond, circulant, image, sums):
    me = lax.axis_index("seq")
    fields = []
    numerator, curvature = sums
    for k, j in enumerate(slots):
        p = precond[me ^ j]
        noisy = noises[k][...] * p
        ki = circulant[me ^ j] + noisy
        image[k] = ki
        fields.append(noisy)
        numerator += folded(signs[k][:lanes] * p)
        curvature += folded(p * ki)
    return fields, (numerator, curvature)


def near_kernel(rows, *refs):
    n = rows - 2
    blocks, others = refs[:n], refs[n : n + 2]
    precond, circulant, left, dft, turns, big_turn, image, noise, found, sums = refs[n + 2 :]
    share = lanes // 2
    for j in range(2):
        noise[j] = blocks[j][blocks[j].shape[0] - lanes :]
    for j in range(2, n):
        whole_noise(noise.at[j], blocks[j], others[j % 2].at[(j - 2) // 2 * share : j // 2 * share])
    zero = jnp.zeros((lead, lanes), exact)
    noises = [noise.at[j] for j in range(n)]
    fields, totals = images(range(n), blocks, noises, precond, circulant, image, (zero, zero))
    sums[0], sums[1] = totals
    at = [lax.axis_index("seq") ^ j for j in range(n)]
    fields += [noises[j][...] * blocks[j][:lanes] for j in range(2)] + [noises[j][...] * image[j] for j in range(2)]
    for j, x in enumerate(own_spectra(fields, at + at[:2] * 2, left, dft, turns, big_turn)):
        found[j, 0], found[j, 1] = x


def adjoint_kernel(rows, probes, *refs):
    n = rows - 2
    signs = [refs[j].at[:lanes] for j in range(rows)]
    blocks, others = refs[:rows], refs[rows : rows + 2]
    near_image, near_noise, near_found, near_sums = refs[rows + 2 : rows + 6]
    refs = refs[rows + 6 :]
    precond, circulant, spectrum, kernel, symbol, left, dft, turns, big_turn, residual_out = refs[:10]
    outs = refs[10 : 10 + probes]
    image, noise, work, shares = refs[10 + probes :]
    depth = lanes // rows
    samples = rows * lanes * lanes
    me = lax.axis_index("seq")
    own = pl.multiple_of(me * depth, depth)
    at = [me ^ j for j in range(rows)]
    for j in range(n):
        work[at[j], 0, 0], work[at[j], 0, 1] = near_found[j, 0], near_found[j, 1]
    for k in range(2):
        whole_noise(noise.at[k], others[k].at[: lanes // 2], others[k].at[lanes // 2 :])
    last_noises = [noise.at[k] for k in range(2)]
    sums = (near_sums[0], near_sums[1])
    fields, sums = images(range(n, rows), blocks[n:], last_noises, precond, circulant, image, sums)
    noises = [near_noise.at[j] for j in range(n)] + last_noises
    image = [near_image.at[j] for j in range(n)] + [image.at[k] for k in range(2)]
    numerator, curvature = whole_sum(sums[0]), whole_sum(sums[1])
    for j, x in zip(range(n, rows), own_spectra(fields, at[n:], left, dft, turns, big_turn)):
        work[at[j], 0, 0], work[at[j], 0, 1] = x
    step_size = numerator / curvature
    cross = jnp.zeros((lead, lanes), exact)
    fields = []
    for j in range(rows):
        residual = signs[j][...] - step_size * image[j][...]
        cross += folded(residual * image[j][...])
        if j >= 2:
            fields.append(noises[j][...] * residual)
        if j == 0:
            residual_out[...] = residual.T
    weight = -2.0 * whole_sum(cross)
    for j in range(2):
        for part in range(2):
            work[at[j], 1, part] = near_found[n + j, part] - step_size * near_found[n + 2 + j, part]
    for r, x in zip(at[2:], own_spectra(fields, at[2:], left, dft, turns, big_turn)):
        work[r, 1, 0], work[r, 1, 1] = x
    noisy = small_dft([(work[r, 0, 0], work[r, 0, 1]) for r in range(rows)], -1)
    noisy_residual = small_dft([(work[r, 1, 0], work[r, 1, 1]) for r in range(rows)], -1)
    for a in range(rows):
        k, s = kernel[:, a], symbol[:, a]
        total = 0.0
        for part in range(2):
            base = spectrum[a, part]
            ki = k * (base / s) + noisy[a][part]
            applied = k * (base - step_size * ki) + noisy_residual[a][part]
            adjoint = (
                (weight / curvature) * base
                - (2.0 * weight * step_size / curvature) * ki
                - (2.0 * step_size) * applied
            )
            total += adjoint * base
        shares[a] = -total / (samples * s * s)
    width = rows // probes
    column = lax.axis_index("probe")
    for d in range(probes):
        for k in range(width):
            outs[d][:, k] = shares[(column ^ d) * width + k]


def call(kernel, outs, scratch, *operands):
    whole = pl.BlockSpec(memory_space=pltpu.VMEM)
    typed = [out if isinstance(out[0], tuple) else (out, exact) for out in outs]
    shapes = tuple(pltpu.VMEM(shape, dtype) for shape, dtype in typed)
    return pl.pallas_call(
        kernel,
        out_shape=shapes,
        in_specs=[whole] * len(operands),
        out_specs=(whole,) * len(shapes),
        scratch_shapes=[pltpu.VMEM(shape, exact) for shape in scratch],
        compiler_params=pltpu.CompilerParams(vmem_limit_bytes=24 << 20),
        cost_estimate=pl.CostEstimate(flops=0, bytes_accessed=0, transcendentals=0),
    )(*operands)


def swapped(x, axis, d):
    return lax.ppermute(x, axis, [(i, i ^ d) for i in range(lax.axis_size(axis))])


def after(x, *earlier):
    return lax.optimization_barrier((x, *earlier))[0]


def after(x, *earlier):
    return lax.optimization_barrier((x, *earlier))[0]


def other_core(x):
    return swapped(x, "seq", 1)


def across_y(x):
    return swapped(x, "probe", lax.axis_size("probe") // 2)


def next_chip(x):
    return swapped(x, "seq", 2)


def beyond_middle(x):
    return swapped(x, "seq", 4)


def adjoint_calls(
    rows, probes, blocks, noises, precond, circulant, spectrum, kernel, symbols, left, dft, turns, big_turn
):
    square = (lanes, lanes)
    depth, width, n = lanes // rows, rows // probes, rows - 2
    tables_held = (left, dft, turns, big_turn)
    near_parts = call(
        functools.partial(near_kernel, rows),
        [(n, *square), (n, *square), (n + 4, 2, depth, lanes), (2, lead, lanes)],
        [],
        *blocks[:n],
        *noises[:2],
        precond,
        circulant,
        *tables_held,
    )
    return call(
        functools.partial(adjoint_kernel, rows, probes),
        [square] + [(depth, width, lanes)] * probes,
        [(2, *square), (2, *square), (rows, 2, 2, depth, lanes), (rows, depth, lanes)],
        *blocks,
        *noises[2:],
        *near_parts,
        precond,
        circulant,
        spectrum,
        kernel,
        symbols,
        *tables_held,
    )


def gathered_shards(probe_bits, noise_var, kernel_spectrum, symbol, grad_prev):
    rows = kernel_spectrum.shape[1]
    probes = lax.axis_size("probe")
    half, depth, width = rows // 2, lanes // rows, rows // probes
    kernel = kernel_spectrum.T.reshape(rows, depth, lanes).transpose(1, 0, 2)
    symbols = symbol.T.reshape(rows, depth, lanes).transpose(1, 0, 2)
    before = grad_prev.T.reshape(width, depth, lanes).transpose(1, 0, 2)
    square = (lanes, lanes)
    dft, turns = tables(rows)
    first = lanes + 2 * half * depth + lead
    block, sent, dft, turns = pl.pallas_call(
        functools.partial(pack_kernel, half, first),
        out_shape=(
            pltpu.VMEM((first + lanes, lanes), exact),
            pltpu.VMEM((first + lanes // 2, lanes), exact),
            pltpu.VMEM(dft.shape, near),
            pltpu.VMEM(turns.shape, exact),
        ),
        in_specs=[pl.BlockSpec(memory_space=pl.ANY)] * 6,
        out_specs=(pl.BlockSpec(memory_space=pltpu.VMEM),) * 4,
        scratch_shapes=[
            pltpu.VMEM(square, jnp.int32),
            pltpu.VMEM(square, exact),
            pltpu.VMEM(kernel.shape, exact),
            pltpu.VMEM(kernel.shape, exact),
            pltpu.SemaphoreType.DMA((6,)),
        ],
    )(probe_bits.reshape(square), noise_var.reshape(square), kernel, symbols, dft, turns)
    far = beyond_middle(sent)
    neighbour = next_chip(sent)
    passed_on = next_chip(far[:first])
    early = [block, other_core(block), neighbour, far]
    found, left, big_turn = call(
        functools.partial(early_kernel, rows),
        [(len(early), 2, *square), ((4 * lanes, 2 * lanes), near), (rows, lanes, 2 * lanes)],
        [],
        *early,
        dft,
        turns,
    )
    halves = across_y(jnp.concatenate([neighbour[first:], far[first:]], 0))
    blocks = early[:2]
    for x, earlier in ((neighbour, found), (far, found), (passed_on, halves)):
        blocks += [x, other_core(after(x, earlier))]
    field = (rows, *square)
    spectrum, precond, circulant = call(
        functools.partial(inverse_kernel, rows),
        [(rows, 2, depth, lanes), field, field],
        [(half, *square), (half, *square), (rows, lead, lanes), (rows, 2, 2, *square)],
        *blocks,
        found,
        left,
        dft,
        turns,
        big_turn,
    )
    passed_noise = next_chip(jnp.concatenate([far[first:], halves[lanes // 2 :]], 0))
    last = after(passed_noise, precond)
    noises = [halves, other_core(halves), last, other_core(last)]
    residual, *parts = adjoint_calls(
        rows, probes, blocks, noises, precond, circulant, spectrum, kernel, symbols, left, dft, turns, big_turn
    )
    near_x, opposite, near_y = (swapped(parts[d], "probe", d) for d in (1, 3, 2))
    total = lax.optimization_barrier(parts[0] + near_x)
    total = lax.optimization_barrier(total + opposite)
    total = before + (total + near_y) / probes
    total = total.transpose(1, 0, 2).reshape(width, depth * lanes).T
    return residual.reshape(probe_bits.shape), total


highest = lax.Precision.HIGHEST
minor_width = 128


def dft_table(height, breadth, modulus, orient):
    left_index = jnp.arange(height, dtype=jnp.int32)[:, None]
    right_index = jnp.arange(breadth, dtype=jnp.int32)[None, :]
    phases = (
        orient * 2.0 * math.pi / modulus * (left_index * right_index % modulus).astype(jnp.float32)
    )
    return (jnp.cos(phases), jnp.sin(phases))


def complex_product(pattern, real_part, imaginary, cosine_table, sine_table):
    real_cos = jnp.einsum(pattern, real_part, cosine_table, precision=highest)
    real_sin = jnp.einsum(pattern, real_part, sine_table, precision=highest)
    if imaginary is None:
        return (real_cos, real_sin)
    imag_cos = jnp.einsum(pattern, imaginary, cosine_table, precision=highest)
    imag_sin = jnp.einsum(pattern, imaginary, sine_table, precision=highest)
    return (real_cos - imag_sin, real_sin + imag_cos)


def rotate(real_part, imaginary, cosine_table, sine_table):
    return (
        real_part * cosine_table - imaginary * sine_table,
        real_part * sine_table + imaginary * cosine_table,
    )


def forward_rows(series):
    major_len = series.shape[-2]
    length = major_len * minor_width
    cosine_table, sine_table = dft_table(major_len, major_len, major_len, -1.0)
    section_real, section_imag = complex_product(
        "...mi,mk->...ik", series, None, cosine_table, sine_table
    )
    turn_cos, turn_sin = dft_table(minor_width, major_len, length, -1.0)
    twisted_real, twisted_imag = rotate(section_real, section_imag, turn_cos, turn_sin)
    cosine_table, sine_table = dft_table(minor_width, minor_width, minor_width, -1.0)
    return complex_product("...ik,ij->...jk", twisted_real, twisted_imag, cosine_table, sine_table)


def inverse_rows(real_part, imaginary):
    major_len = real_part.shape[-1]
    length = major_len * minor_width
    cosine_table, sine_table = dft_table(minor_width, minor_width, minor_width, 1.0)
    section_real, section_imag = complex_product(
        "...jk,ji->...ik", real_part, imaginary, cosine_table, sine_table
    )
    turn_cos, turn_sin = dft_table(minor_width, major_len, length, 1.0)
    twisted_real, twisted_imag = rotate(section_real, section_imag, turn_cos, turn_sin)
    cosine_table, sine_table = dft_table(major_len, major_len, major_len, 1.0)
    final_real, unused = complex_product(
        "...ik,km->...mi", twisted_real, twisted_imag, cosine_table, sine_table
    )
    return final_real


def global_twiddle(local_rows, major_len, samples, orient):
    row_index = lax.axis_index("seq") * local_rows + jnp.arange(local_rows, dtype=jnp.int32)
    column_index = (
        jnp.arange(minor_width, dtype=jnp.int32)[:, None] * major_len
        + jnp.arange(major_len, dtype=jnp.int32)[None, :]
    )
    phases = (
        orient
        * 2.0
        * math.pi
        / samples
        * (row_index[:, None, None] * column_index[None, :, :] % samples).astype(jnp.float32)
    )
    return (jnp.cos(phases), jnp.sin(phases))


def forward_spectrum(series):
    local_rows = series.shape[1]
    major_len = series.shape[2]
    devices = lax.axis_size("seq")
    all_rows = local_rows * devices
    samples = all_rows * major_len * minor_width
    real_part, imaginary = forward_rows(series)
    turn_cos, turn_sin = global_twiddle(local_rows, major_len, samples, -1.0)
    turned_real, turned_imag = rotate(real_part, imaginary, turn_cos, turn_sin)
    arrived = lax.all_to_all(
        jnp.stack([turned_real, turned_imag]), "seq", split_axis=3, concat_axis=2, tiled=True
    )
    block = minor_width // devices * major_len
    arrived = arrived.reshape(arrived.shape[0], arrived.shape[1], all_rows, block)
    cosine_table, sine_table = dft_table(all_rows, all_rows, all_rows, -1.0)
    return complex_product("zrb,ra->zba", arrived[0], arrived[1], cosine_table, sine_table)


def inverse_field(spectrum_real, spectrum_imag):
    all_rows = spectrum_real.shape[2]
    block = spectrum_real.shape[1]
    devices = lax.axis_size("seq")
    major_len = block * devices // minor_width
    cosine_table, sine_table = dft_table(all_rows, all_rows, all_rows, 1.0)
    back_real, back_imag = complex_product(
        "zba,ar->zrb", spectrum_real, spectrum_imag, cosine_table, sine_table
    )
    stacked = jnp.stack([back_real, back_imag])
    stacked = stacked.reshape(
        stacked.shape[0], stacked.shape[1], all_rows, minor_width // devices, major_len
    )
    arrived = lax.all_to_all(stacked, "seq", split_axis=2, concat_axis=3, tiled=True)
    local_rows = arrived.shape[2]
    samples = all_rows * major_len * minor_width
    turn_cos, turn_sin = global_twiddle(local_rows, major_len, samples, 1.0)
    turned_real, turned_imag = rotate(arrived[0], arrived[1], turn_cos, turn_sin)
    return inverse_rows(turned_real, turned_imag) / samples


def shards(probe_bits, noise_var, kernel_spectrum, symbol, grad_prev):
    field_shape = (
        probe_bits.shape[0],
        probe_bits.shape[1],
        probe_bits.shape[2] // minor_width,
        minor_width,
    )
    sign_field = (2 * probe_bits - 1).astype(jnp.float32).reshape(field_shape)
    noise_field = noise_var.reshape(field_shape[1:])
    samples = kernel_spectrum.shape[1] * noise_var.shape[1]
    base_real, base_imag = forward_spectrum(sign_field)
    scaled_real = base_real / symbol
    scaled_imag = base_imag / symbol
    precond = inverse_field(scaled_real, scaled_imag)
    again_real, again_imag = forward_spectrum(precond)
    circulant = inverse_field(kernel_spectrum * again_real, kernel_spectrum * again_imag)
    kernel_image = circulant + noise_field * precond
    numerator, curvature = lax.psum(
        (jnp.sum(sign_field * precond), jnp.sum(precond * kernel_image)), "seq"
    )
    step_size = numerator / curvature
    residual = sign_field - step_size * kernel_image
    cross_term = lax.psum(jnp.sum(residual * kernel_image), "seq")
    weight = -2.0 * cross_term
    resid_real, resid_imag = forward_spectrum(residual)
    applied = (
        inverse_field(kernel_spectrum * resid_real, kernel_spectrum * resid_imag)
        + noise_field * residual
    )
    adjoint = (
        weight / curvature * sign_field
        - 2.0 * weight * step_size / curvature * kernel_image
        - 2.0 * step_size * applied
    )
    adjoint_real, adjoint_imag = forward_spectrum(adjoint)
    local_grad = -(adjoint_real[0] * base_real[0] + adjoint_imag[0] * base_imag[0]) / (
        samples * symbol * symbol
    )
    probes = lax.axis_size("probe")
    summed = lax.psum(local_grad, "probe")
    share_width = summed.shape[1] // probes
    own_share = lax.dynamic_slice_in_dim(
        summed, lax.axis_index("probe") * share_width, share_width, 1
    )
    grad_total = grad_prev + own_share / probes
    return (residual.reshape(probe_bits.shape), grad_total)


def fits(mesh, cols, rows):
    seq, probe = mesh.shape["seq"], mesh.shape["probe"]
    powers = all(n & (n - 1) == 0 for n in (rows, seq, probe))
    return powers and rows == seq == lead and rows % probe == 0 and probe > 1 and cols == lanes * lanes


def solution(mesh):
    placed = (
        P("probe", "seq", None),
        P("seq", None),
        P("seq", None),
        P("seq", None),
        P("seq", "probe"),
    )

    def whole(probe_bits, noise_var, kernel_spectrum, symbol, grad_prev):
        small = fits(mesh, *symbol.shape)
        return jax.shard_map(
            gathered_shards if small else shards,
            mesh=mesh,
            in_specs=placed,
            out_specs=(P("probe", "seq", None), P("seq", "probe")),
            check_vma=False,
        )(probe_bits, noise_var, kernel_spectrum, symbol, grad_prev)

    return whole
```
